256 devices in a mesh: con: 8 (over y, x_hi), var: 32 (over x_lo, z, core).
Axes of the slice: x: 4 (x_hi: 2, x_lo: 2; x = x_hi * 2 + x_lo), y: 4, z: 8, core: 2. Of those that a mesh axis runs over, the one named last changes fastest.
Arguments:
- tiles: float32 [8, 32, 72, 128, 128], P('con', 'var'), may hold values from -0.25 to 0.25
- row_tile: int32 [8, 32, 72], P('con', 'var'), may hold values from 0 to 511, as said below
- col_tile: int32 [8, 32, 72], P('con', 'var'), may hold values from 0 to 31
- diag_cost: float32 [131072], P('var'), may hold values from 0.1 to 2
- linear_cost: float32 [8, 131072], P(None, 'var'), may hold values from -6 to 6
- bound_center: float32 [8, 524288], P(None, ('con', 'var')), may hold values from -6 to 6
- bound_width: float32 [8, 524288], P(None, ('con', 'var')), may hold values from 0.05 to 1
- rho_level: int32 [524288], P(('con', 'var')), may hold values from 0 to 3
- sigma_level: int32 [8], replicated, may hold values from 0 to 3
- state_x: float32 [8, 131072], P(None, 'var'), may hold values from -6 to 6
- state_w: float32 [8, 524288], P(None, ('con', 'var')), may hold values from -6 to 6
- prev_x: float32 [8, 131072], P(None, 'var'), may hold values from -6 to 6
- prev_w: float32 [8, 524288], P(None, ('con', 'var')), may hold values from -6 to 6
- prev_gx: float32 [8, 131072], P(None, 'var'), may hold values from -6 to 6
- prev_gw: float32 [8, 524288], P(None, ('con', 'var')), may hold values from -6 to 6
- hist_sx: float32 [8, 8, 131072], P(None, None, 'var'), may hold values from -6 to 6
- hist_sw: float32 [8, 8, 524288], P(None, None, ('con', 'var')), may hold values from -6 to 6
- hist_gx: float32 [8, 8, 131072], P(None, None, 'var'), may hold values from -6 to 6
- hist_gw: float32 [8, 8, 524288], P(None, None, ('con', 'var')), may hold values from -6 to 6
- slot_order: int32 [8], replicated, may hold values from 0 to 7, each once
Outputs:
- next_x: float32 [8, 131072], P(None, 'var')
- next_w: float32 [8, 524288], P(None, ('con', 'var'))
The draws below stay inside these ranges and needn't reach their ends.
Inputs may be any that keep to these rules, and one draw needn't show every extreme that they name: `row_tile`: split each constraint block's block rows into 32 runs of 524288 / (128 * 8 * 32) consecutive block rows. Among the 72 blocks (c, v, t) of one pair (c, v), at most ceil(72 / 32) lie in the block rows of one run, and some run holds exactly that many. `slot_order`: a permutation of the 8 slots.
All inputs are finite; a program needn't handle non-finite values.
Results may differ from the reference program's by a relative error of at most 0.0003.
Values sent between devices are 32-bit elements; how exact they have to be, the bound alone decides.
No kernel may reach another device: no remote copies, remote signals or barrier semaphores. Data moves between devices by JAX's collectives and lax.ppermute only.
A program may use at most 64 MiB of HBM per device.

```python
import math
import jax
import jax.numpy as jnp
from jax import lax

NC = 524288
NV = 131072
TILE = 128
QPS = 8
TILES_DEV = 72
MEM = 8
CG_ITERS = 1
STEPS = 2
N_CON = 8
N_VAR = 32


def draw_row_tile(key, part):
    key = jax.random.fold_in(key, 11)
    shift_key, local_key = jax.random.split(key)
    run_length = NC // (TILE * N_CON * N_VAR)
    shift = jax.random.randint(shift_key, (N_CON, N_VAR, 1), 0, N_VAR, dtype=jnp.int32)
    owner = (jnp.arange(TILES_DEV, dtype=jnp.int32)[None, None, :] + shift) % N_VAR
    local = jax.random.randint(local_key, (N_CON, N_VAR, TILES_DEV), 0, run_length, dtype=jnp.int32)
    return (owner * run_length + local).astype(jnp.int32)


def with_ends(drawn, stream_key, least, high):
    spot = [jax.random.randint(jax.random.fold_in(stream_key, axis), (), 0, length) for axis, length in enumerate(drawn.shape)]
    main_axis = drawn.shape.index(max(drawn.shape))
    next_to = spot[:main_axis] + [(spot[main_axis] + 1) % drawn.shape[main_axis]] + spot[main_axis + 1:]
    return drawn.at[tuple(spot)].set(least).at[tuple(next_to)].set(high)


def levels(key, extent, cuts, smallest, largest):
    gain, own = 1.0, jax.random.fold_in(key, 6)
    for axis_at, blocks in cuts:
        steps = jnp.exp(jax.random.uniform(jax.random.fold_in(own, axis_at), (blocks,), jnp.float32, smallest / len(cuts), largest / len(cuts)))
        gain = gain * jnp.repeat(steps, extent[axis_at] // blocks).reshape([-1 if axis == axis_at else 1 for axis in range(len(extent))])
    return gain


def centred(own_key, shape, width, limit, cuts=(), held_as=jnp.bfloat16):
    values = jax.random.normal(own_key, shape, jnp.float32) * width
    if len(cuts) > 0:
        values = levels(own_key, shape, cuts, -0.22, 0.18) * values
    return jnp.clip(values, min=-limit, max=limit).astype(held_as)


def setup_inputs(seed: int = 0) -> dict:
    keys = jax.random.split(jax.random.key(seed), 21)
    return {
        "tiles": centred(keys[0], (N_CON, N_VAR, TILES_DEV, TILE, TILE), (TILE * max(1, TILES_DEV * N_VAR * TILE * N_CON // NC)) ** -0.5, 0.25, ((0, 8), (1, 32)), jnp.float32),
        "row_tile": draw_row_tile(jax.random.fold_in(keys[20], 71), 0),
        "col_tile": with_ends(jax.random.randint(keys[2], (N_CON, N_VAR, TILES_DEV), 0, NV // (TILE * N_VAR)), jax.random.fold_in(keys[2], 1), 0, (NV // (TILE * N_VAR)) - 1).astype(jnp.int32),
        "diag_cost": jnp.clip(jnp.exp(math.log(2.0) - 2.9957323 * jax.random.uniform(keys[3], (NV,), jnp.float32) ** levels(keys[3], (NV,), ((0, 32),), -0.2, 0.2)), 0.1, 2.0),
        "linear_cost": centred(keys[4], (QPS, NV), 1.0, 6.0, ((1, 32),), jnp.float32),
        "bound_center": centred(keys[5], (QPS, NC), 1.0, 6.0, ((1, 256),), jnp.float32),
        "bound_width": jnp.clip(jnp.exp(math.log(1.0) - 2.9957323 * jax.random.uniform(keys[6], (QPS, NC), jnp.float32) ** levels(keys[6], (QPS, NC), ((1, 256),), -0.2, 0.2)), 0.05, 1.0),
        "rho_level": with_ends(jax.random.randint(keys[7], (NC,), 0, 4), jax.random.fold_in(keys[7], 1), 0, 3).astype(jnp.int32),
        "sigma_level": with_ends(jax.random.randint(keys[8], (QPS,), 0, 4), jax.random.fold_in(keys[8], 1), 0, 3).astype(jnp.int32),
        "state_x": centred(keys[9], (QPS, NV), 1.0, 6.0, ((1, 32),), jnp.float32),
        "state_w": centred(keys[10], (QPS, NC), 1.0, 6.0, ((1, 256),), jnp.float32),
        "prev_x": centred(keys[11], (QPS, NV), 1.0, 6.0, ((1, 32),), jnp.float32),
        "prev_w": centred(keys[12], (QPS, NC), 1.0, 6.0, ((1, 256),), jnp.float32),
        "prev_gx": centred(keys[13], (QPS, NV), 0.5, 6.0, ((1, 32),), jnp.float32),
        "prev_gw": centred(keys[14], (QPS, NC), 0.5, 6.0, ((1, 256),), jnp.float32),
        "hist_sx": centred(keys[15], (MEM, QPS, NV), 0.5, 6.0, ((2, 32),), jnp.float32),
        "hist_sw": centred(keys[16], (MEM, QPS, NC), 0.5, 6.0, ((2, 256),), jnp.float32),
        "hist_gx": centred(keys[17], (MEM, QPS, NV), 0.5, 6.0, ((2, 32),), jnp.float32),
        "hist_gw": centred(keys[18], (MEM, QPS, NC), 0.5, 6.0, ((2, 256),), jnp.float32),
        "slot_order": jax.random.permutation(keys[19], MEM).astype(jnp.int32),
    }


highest = lax.Precision.HIGHEST
relax = 1.6
ridge = 0.01

def tile_positions(row_tile, col_tile):
    row_count = NC // (TILE * N_CON)
    col_count = NV // (TILE * N_VAR)
    con_ids = jnp.arange(N_CON, dtype=jnp.int32)[:, None, None]
    var_ids = jnp.arange(N_VAR, dtype=jnp.int32)[None, :, None]
    rows_all = (con_ids * row_count + row_tile).reshape(-1).astype(jnp.int32)
    cols_all = (var_ids * col_count + col_tile).reshape(-1).astype(jnp.int32)
    return (rows_all, cols_all)

def apply_matrix(blocks, rows_all, cols_all, vector):
    pieces = vector.reshape(QPS, NV // TILE, TILE)[:, cols_all]
    contrib = jnp.einsum('ktj,tij->kti', pieces, blocks, precision=highest)
    result = jnp.zeros((QPS, NC // TILE, TILE), jnp.float32).at[:, rows_all].add(contrib)
    return result.reshape(QPS, NC)

def apply_transpose(blocks, rows_all, cols_all, vector):
    pieces = vector.reshape(QPS, NC // TILE, TILE)[:, rows_all]
    contrib = jnp.einsum('kti,tij->ktj', pieces, blocks, precision=highest)
    result = jnp.zeros((QPS, NV // TILE, TILE), jnp.float32).at[:, cols_all].add(contrib)
    return result.reshape(QPS, NV)

def solve_small(system, rhs):
    lower = jnp.linalg.cholesky(system)
    first = jax.scipy.linalg.solve_triangular(lower, rhs[:, :, None], lower=True)
    return jax.scipy.linalg.solve_triangular(lower, first, trans=1, lower=True)[:, :, 0]

def reference(tiles, row_tile, col_tile, diag_cost, linear_cost, bound_center, bound_width, rho_level, sigma_level, state_x, state_w, prev_x, prev_w, prev_gx, prev_gw, hist_sx, hist_sw, hist_gx, hist_gw, slot_order):
    blocks = tiles.reshape(-1, TILE, TILE)
    rows_all, cols_all = tile_positions(row_tile, col_tile)
    rho = 0.4 * (1.0 + rho_level.astype(jnp.float32))
    sigma = 0.2 * (1.0 + sigma_level.astype(jnp.float32))[:, None]
    lower_bound = bound_center - bound_width
    upper_bound = bound_center + bound_width

    def evaluate(primal, shifted):
        slack = jnp.clip(shifted, lower_bound, upper_bound)
        dual = rho * (shifted - slack)
        image_start = apply_matrix(blocks, rows_all, cols_all, primal)
        resid = -linear_cost - diag_cost * primal + apply_transpose(blocks, rows_all, cols_all, rho * (slack - image_start) - dual)
        direction = resid
        res_norm = jnp.sum(resid * resid, axis=1)
        trial = primal
        for inner in range(CG_ITERS):
            image = apply_matrix(blocks, rows_all, cols_all, direction)
            curved = (diag_cost + sigma) * direction + apply_transpose(blocks, rows_all, cols_all, rho * image)
            step_len = res_norm / jnp.sum(direction * curved, axis=1)
            trial = trial + step_len[:, None] * direction
            if inner + 1 < CG_ITERS:
                resid = resid - step_len[:, None] * curved
                norm_next = jnp.sum(resid * resid, axis=1)
                direction = resid + (norm_next / res_norm)[:, None] * direction
                res_norm = norm_next
        trial_image = apply_matrix(blocks, rows_all, cols_all, trial)
        primal_next = relax * trial + (1.0 - relax) * primal
        shifted_next = relax * trial_image + (1.0 - relax) * slack + (shifted - slack)
        return (primal_next, shifted_next)
    identity = jnp.eye(MEM, dtype=jnp.float32)
    state_a, state_b = (state_x, state_w)
    for step_index in range(STEPS):
        mapped_a, mapped_b = evaluate(state_a, state_b)
        resid_a = mapped_a - state_a
        resid_b = mapped_b - state_b
        chosen = (jnp.arange(MEM, dtype=jnp.int32) == slot_order[step_index])[:, None, None]
        hist_sx = jnp.where(chosen, (state_a - prev_x)[None], hist_sx)
        hist_sw = jnp.where(chosen, (state_b - prev_w)[None], hist_sw)
        hist_gx = jnp.where(chosen, (resid_a - prev_gx)[None], hist_gx)
        hist_gw = jnp.where(chosen, (resid_b - prev_gw)[None], hist_gw)
        gram = jnp.einsum('mkn,pkn->kmp', hist_gx, hist_gx, precision=highest) + jnp.einsum('mkn,pkn->kmp', hist_gw, hist_gw, precision=highest)
        rhs = jnp.einsum('mkn,kn->km', hist_gx, resid_a, precision=highest) + jnp.einsum('mkn,kn->km', hist_gw, resid_b, precision=highest)
        frob = jnp.sum(hist_sx * hist_sx, axis=(0, 2)) + jnp.sum(hist_sw * hist_sw, axis=(0, 2)) + jnp.sum(hist_gx * hist_gx, axis=(0, 2)) + jnp.sum(hist_gw * hist_gw, axis=(0, 2))
        coef = solve_small(gram + (ridge * frob)[:, None, None] * identity, rhs)
        prev_x, prev_w, prev_gx, prev_gw = (state_a, state_b, resid_a, resid_b)
        state_a = state_a + resid_a - jnp.einsum('km,mkn->kn', coef, hist_sx + hist_gx, precision=highest)
        state_b = state_b + resid_b - jnp.einsum('km,mkn->kn', coef, hist_sw + hist_gw, precision=highest)
    return (state_a, state_b)
```

```python
import jax
import jax.numpy as jnp
from jax import lax
from jax.sharding import PartitionSpec as P

STEPS = 2


highest = lax.Precision.HIGHEST
relax = 1.6
ridge = 0.01


def solve_small(system, rhs):
    lower = jnp.linalg.cholesky(system)
    first = jax.scipy.linalg.solve_triangular(lower, rhs[:, :, None], lower=True)
    return jax.scipy.linalg.solve_triangular(lower, first, trans=1, lower=True)[:, :, 0]


def dots(left, right):
    return jnp.einsum("mkn,pkn->kmp", left, right, precision=highest)


def per_device(
    tiles,
    row_tile,
    col_tile,
    diag_cost,
    linear_cost,
    bound_center,
    bound_width,
    rho_level,
    sigma_level,
    state_x,
    state_w,
    prev_x,
    prev_w,
    prev_gx,
    prev_gw,
    hist_sx,
    hist_sw,
    hist_gx,
    hist_gw,
    slot_order,
):
    problems, var_cols = state_x.shape
    tile_size = tiles.shape[-1]
    memory = hist_sx.shape[0]
    var_count, con_count = lax.axis_size("var"), lax.axis_size("con")
    col_count = var_cols // tile_size
    run_length = state_w.shape[1] // tile_size
    blocks = tiles.reshape(-1, tile_size, tile_size)
    count = blocks.shape[0]
    per_run = -(-count // var_count)
    slots = var_count * per_run
    rows_here = row_tile.reshape(-1)
    cols_here = col_tile.reshape(-1)

    owner = rows_here // run_length
    ids = jnp.arange(count, dtype=jnp.int32)
    rank = jnp.sum((owner[:, None] == owner[None, :]) & (ids[None, :] < ids[:, None]), axis=1)
    slot = owner * per_run + rank.astype(jnp.int32)
    filled = jnp.arange(slots, dtype=jnp.int32)[:, None] == slot[None, :]
    local_row = jnp.sum(jnp.where(filled, (rows_here % run_length)[None, :], 0), axis=1)
    place = filled.astype(jnp.float32)

    col_onehot = (jnp.arange(col_count, dtype=jnp.int32)[:, None] == cols_here[None, :]).astype(
        jnp.float32
    )
    rho = 0.4 * (1.0 + rho_level.astype(jnp.float32))
    sigma = 0.2 * (1.0 + sigma_level.astype(jnp.float32))[:, None]
    lower_bound = bound_center - bound_width
    upper_bound = bound_center + bound_width
    con_id = lax.axis_index("con")
    share = var_cols // con_count

    def mine(x):
        return lax.dynamic_slice_in_dim(x, con_id * share, share, axis=-1)

    def exchange(x):
        return lax.all_to_all(x, "var", 0, 0, tiled=True)

    def products(vector):
        pieces = jnp.take(vector.reshape(problems, col_count, tile_size), cols_here, axis=1)
        contrib = jnp.einsum("ktj,tij->tki", pieces, blocks, precision=highest)
        return jnp.einsum("st,tki->ski", place, contrib, precision=highest)

    def gathered(received, onehot):
        return jnp.einsum("rs,ski->kri", onehot, received, precision=highest).reshape(
            problems, run_length * tile_size
        )

    def backward(vector, onehot):
        sent = jnp.einsum(
            "rs,kri->ski", onehot, vector.reshape(problems, run_length, tile_size), precision=highest
        )
        back = exchange(sent.reshape(var_count, per_run, problems, tile_size)).reshape(
            slots, problems, tile_size
        )
        pieces = back[slot]
        contrib = jnp.einsum("tki,tij->tkj", pieces, blocks, precision=highest)
        partial_sum = jnp.einsum("ct,tkj->kcj", col_onehot, contrib, precision=highest).reshape(
            problems, var_cols
        )
        return partial_sum

    def over_con(x):
        copies = jnp.broadcast_to(x[None], (con_count,) + x.shape)
        return jnp.sum(lax.all_to_all(copies, "con", 0, 0, tiled=True), axis=0)

    def over_all(values):
        n = values.size
        rows = -(-n // 128)
        flat = jnp.pad(values.reshape(-1), (0, rows * 128 - n)).reshape(rows, 128)
        copies = jnp.broadcast_to(flat[None], (con_count * var_count, rows, 128))
        total = jnp.sum(lax.all_to_all(copies, ("con", "var"), 0, 0, tiled=True), axis=0)
        return total.reshape(-1)[:n].reshape(values.shape)

    hg = (mine(hist_gx), hist_gw)
    hs = (mine(hist_sx), hist_sw)
    p0 = (mine(prev_gx), prev_gw)
    s0 = (mine(state_x - prev_x), state_w - prev_w)
    early = sum(
        jnp.concatenate(
            [
                dots(g, g).reshape(problems, -1),
                dots(g, p[None])[:, :, 0],
                jnp.sum(h * h, axis=2).T,
                jnp.sum(s * s, axis=1)[:, None],
            ],
            axis=1,
        )
        for g, h, p, s in zip(hg, hs, p0, s0)
    )
    width = early.shape[1]
    extra = jnp.pad(early, ((0, 0), (0, tile_size - width)))
    meta = jnp.broadcast_to(
        local_row.astype(jnp.float32).reshape(var_count, 1, per_run), (var_count, problems, per_run)
    )
    extra = jnp.concatenate(
        [jnp.broadcast_to(extra[None, :, : tile_size - per_run], (var_count, problems, tile_size - per_run)), meta],
        axis=2,
    )

    identity = jnp.eye(memory, dtype=jnp.float32)
    index = jnp.arange(memory, dtype=jnp.int32)
    state_a, state_b = (state_x, state_w)
    base_sum = None
    known = None
    for step_index in range(STEPS):
        chosen = index == slot_order[step_index]
        chosen_f = chosen.astype(jnp.float32)
        pick = chosen[:, None, None]
        slack = jnp.clip(state_b, lower_bound, upper_bound)
        dual = rho * (state_b - slack)
        sent = products(state_a).reshape(var_count, per_run, problems, tile_size)
        if step_index == 0:
            got = exchange(jnp.concatenate([sent, extra[:, None]], axis=1))
            received = got[:, :per_run]
            side = got[:, per_run]
            rows_asked = side[:, 0, tile_size - per_run :].reshape(-1).astype(jnp.int32)
            onehot = (
                jnp.arange(run_length, dtype=jnp.int32)[:, None] == rows_asked[None, :]
            ).astype(jnp.float32)
            early_group = jnp.sum(side, axis=0)
        else:
            received = exchange(sent)
        image_start = gathered(received.reshape(slots, problems, tile_size), onehot)
        partial_sum = backward(rho * (slack - image_start) - dual, onehot)
        if step_index == 0:
            both = over_con(jnp.concatenate([partial_sum, early_group], axis=1))
            partial_sum, early_all = both[:, :var_cols], both[:, var_cols : var_cols + width]
            at = memory * memory
            known = early_all[:, :at].reshape(problems, memory, memory)
            known_p = early_all[:, at : at + memory]
            known_s = early_all[:, at + memory : at + 2 * memory]
            known_s = jnp.where(chosen[None, :], early_all[:, at + 2 * memory :], known_s)
        else:
            partial_sum = over_con(partial_sum)
        resid = -linear_cost - diag_cost * state_a + partial_sum
        received = exchange(products(resid).reshape(var_count, per_run, problems, tile_size))
        image = gathered(received.reshape(slots, problems, tile_size), onehot)

        u = (-mine(prev_gx), relax * (image_start - slack) - prev_gw)
        v = (relax * mine(resid), relax * image)
        p = (mine(prev_gx), prev_gw)
        s = (mine(state_a - prev_x), state_b - prev_w)
        basis = tuple(jnp.where(pick, b[None], h) for b, h in zip(u, (mine(hist_gx), hist_gw)))
        late = sum(
            jnp.concatenate(
                [
                    jnp.sum(b * uu[None], axis=2).T,
                    jnp.sum(b * vv[None], axis=2).T,
                    jnp.sum(jnp.stack([uu * pp, vv * pp, vv * vv, ss * ss]), axis=2).T,
                ],
                axis=1,
            )
            for b, uu, vv, pp, ss in zip(basis, u, v, p, s)
        )
        r = mine(resid)
        norm_part = jnp.sum(r * r, axis=1)
        curve_part = jnp.sum((mine(diag_cost) + sigma) * r * r, axis=1) + jnp.sum(
            rho * image * image, axis=1
        )
        late = over_all(jnp.concatenate([late, norm_part[:, None], curve_part[:, None]], axis=1))
        u_b, v_b = late[:, :memory], late[:, memory : 2 * memory]
        u_p, v_p, v_v, s_s, norm, curve = [late[:, 2 * memory + i] for i in range(6)]
        step = (norm / curve)[:, None]
        row, col = chosen[None, :, None], chosen[None, None, :]
        v_u = jnp.sum(v_b * chosen_f, axis=1, keepdims=True)
        u_u = jnp.sum(u_b * chosen_f, axis=1, keepdims=True)
        new_dot = u_b + step * v_b
        new_new = u_u + 2.0 * step * v_u + step * step * v_v[:, None]
        gram = jnp.where(row, new_dot[:, None, :], jnp.where(col, new_dot[:, :, None], known))
        gram = jnp.where(row & col, new_new[:, :, None], gram)
        dot_p = jnp.where(chosen[None, :], u_p[:, None] + step * v_p[:, None], known_p)
        rhs = dot_p + jnp.sum(gram * chosen_f[None, None, :], axis=2)
        if step_index > 0:
            known_s = jnp.where(chosen[None, :], s_s[:, None], known_s)
        frob = jnp.sum(known_s, axis=1) + jnp.sum(gram * identity[None], axis=(1, 2))
        coef = solve_small(gram + (ridge * frob)[:, None, None] * identity, rhs)
        known, known_p = gram, rhs

        resid_a = relax * step * resid
        resid_b = relax * (image_start + step * image - slack)
        hist_sx = jnp.where(pick, (state_a - prev_x)[None], hist_sx)
        hist_sw = jnp.where(pick, (state_b - prev_w)[None], hist_sw)
        hist_gx = jnp.where(pick, (resid_a - prev_gx)[None], hist_gx)
        hist_gw = jnp.where(pick, (resid_b - prev_gw)[None], hist_gw)
        prev_x, prev_w, prev_gx, prev_gw = (state_a, state_b, resid_a, resid_b)
        state_a = (
            state_a + resid_a - jnp.einsum("km,mkn->kn", coef, hist_sx + hist_gx, precision=highest)
        )
        state_b = (
            state_b + resid_b - jnp.einsum("km,mkn->kn", coef, hist_sw + hist_gw, precision=highest)
        )
    return (state_a, state_b)


def solution(mesh):
    in_specs = (
        P("con", "var", None, None, None),
        P("con", "var", None),
        P("con", "var", None),
        P("var"),
        P(None, "var"),
        P(None, ("con", "var")),
        P(None, ("con", "var")),
        P(("con", "var")),
        P(),
        P(None, "var"),
        P(None, ("con", "var")),
        P(None, "var"),
        P(None, ("con", "var")),
        P(None, "var"),
        P(None, ("con", "var")),
        P(None, None, "var"),
        P(None, None, ("con", "var")),
        P(None, None, "var"),
        P(None, None, ("con", "var")),
        P(),
    )
    out_specs = (P(None, "var"), P(None, ("con", "var")))
    return jax.shard_map(
        per_device, mesh=mesh, in_specs=in_specs, out_specs=out_specs, check_vma=False
    )
```

```python
import functools

import jax
import jax.numpy as jnp
from jax import lax
from jax.experimental import pallas as pl
from jax.experimental.pallas import tpu as pltpu
from jax.sharding import PartitionSpec as P

STEPS = 2
LANES = 128
UNROLL = 24

relax = 1.6
ridge = 0.01

f32 = jnp.float32
bf16 = jnp.bfloat16

U_H, V_H, U_U, U_V, U_P, V_P, V_V, S_S, R_R, C_C, U_D, V_D, SCALARS = 0, 8, 16, 17, 18, 19, 20, 21, 22, 23, 24, 25, 26


def halves(value):
    high = value.astype(bf16)
    return high, (value - high.astype(f32)).astype(bf16)


def stacked(piece):
    high, low = halves(piece)
    return jnp.concatenate(
        [
            jnp.concatenate([high, high], axis=1),
            jnp.concatenate([low, jnp.zeros_like(low)], axis=1),
        ],
        axis=0,
    )


def times(left, right, contract):
    both = lax.dot_general(left, right, (((1,), (contract,)), ((), ())), preferred_element_type=f32)
    half = both.shape[0] // 2
    return both[:half] + both[half:]


def at(ref, block):
    return ref[:, pl.ds(pl.multiple_of(block * LANES, LANES), LANES)]


def tile_loop(count, body):
    step = max(d for d in range(1, UNROLL + 1) if count % d == 0)

    def some(i, _):
        for j in range(step):
            body(i * step + j)
        return 0

    lax.fori_loop(0, count // step, some, 0)


def lane_ids(shape):
    return lax.broadcasted_iota(jnp.int32, shape, len(shape) - 1)


def send_products(x_ref, cols, where, tiles, send, left):
    for block in range(x_ref.shape[1] // LANES):
        left[block] = stacked(x_ref[:, block * LANES : (block + 1) * LANES])
    send[...] = jnp.zeros_like(send)

    def one(t):
        high, low = halves(tiles[t])
        send[where(t)] = times(left[cols[t]], jnp.concatenate([high, low], axis=1), 1)

    tile_loop(tiles.shape[0], one)


def add_rows(got, index, rows, runs, sums):
    for ref in sums:
        ref[...] = jnp.zeros_like(ref)
    for s in range(rows.shape[0]):
        ref = sums[s % len(sums)]
        row = rows[s]
        ref[row] = ref[row] + got[index(s)]
    return lambda b: functools.reduce(lambda p, q: p + q, [ref[b] for ref in sums])


def block_of(ref, b):
    return ref[:, b * LANES : (b + 1) * LANES]


def rho_of(level_ref, b):
    return 0.4 * (1.0 + block_of(level_ref, b).astype(f32))


def slack_of(w, center, width):
    return jnp.minimum(jnp.maximum(w, center - width), center + width)


def total(value):
    return jnp.sum(value, axis=1, keepdims=True)


def open_kernel(
    per_run, run_length, rows, cols, con, tiles, x, px, w, pw, pgx, pgw, hsx, hsw, hgx, hgw, send, slot, left, count, asked
):
    memory = hgx.shape[0]
    problems = x.shape[0]
    runs = send.shape[0] // (per_run + 1)
    wide = per_run + 1
    share = x.shape[1] // LANES // con[1]

    def clear(i, _):
        count[i] = 0
        return 0

    lax.fori_loop(0, runs, clear, 0)

    def clear_asked(i, _):
        asked[i] = 0
        return 0

    lax.fori_loop(0, runs * per_run, clear_asked, 0)

    def assign(t, _):
        owner = rows[t] // run_length
        rank = count[owner]
        count[owner] = rank + 1
        slot[t] = owner * per_run + rank
        asked[owner * per_run + rank] = rows[t] - owner * run_length
        return 0

    lax.fori_loop(0, tiles.shape[0], assign, 0)

    def where(t):
        owner = slot[t] // per_run
        return slot[t] + owner

    send_products(x, cols, where, tiles, send, left)

    lanes = lane_ids((problems, LANES))
    first = con[0] * share
    out = jnp.zeros((problems, LANES), f32)

    def both(f):
        acc = None
        for b in range(w.shape[1] // LANES):
            v = f(False, b)
            acc = v if acc is None else acc + v
        for b in range(share):
            acc = acc + f(True, first + b)
        return total(acc)

    def hist(ref_x, ref_w, m, is_x, b):
        if is_x:
            return ref_x[m, :, pl.ds(pl.multiple_of(b * LANES, LANES), LANES)]
        return ref_w[m, :, b * LANES : (b + 1) * LANES]

    def plain(ref_x, ref_w, is_x, b):
        return at(ref_x, b) if is_x else block_of(ref_w, b)

    for m in range(memory):
        for n in range(m, memory):
            value = both(lambda q, b: hist(hgx, hgw, m, q, b) * hist(hgx, hgw, n, q, b))
            out = jnp.where((lanes == m * memory + n) | (lanes == n * memory + m), value, out)
        value = both(lambda q, b: hist(hgx, hgw, m, q, b) * plain(pgx, pgw, q, b))
        out = jnp.where(lanes == memory * memory + m, value, out)

        def square(q, b):
            h = hist(hsx, hsw, m, q, b)
            return h * h

        out = jnp.where(lanes == memory * (memory + 1) + m, both(square), out)
    for r in range(runs):
        mark = out
        for s in range(per_run):
            mark = jnp.where(lanes == LANES - per_run + s, asked[r * per_run + s].astype(f32), mark)
        send[r * wide + per_run] = mark


def penalty_kernel(first, per_run, *refs):
    if first:
        got, w, center, width, level, send, image, early, rows, marks, marks_int, sem, *sums = refs
    else:
        got, rows, w, center, width, level, send, image, *sums = refs
    slots = send.shape[0]
    runs = slots // per_run
    if first:
        wide = per_run + 1
        early_sum = None
        for r in range(runs):
            side = got[r * wide + per_run]
            early_sum = side if early_sum is None else early_sum + side
            marks_int[r : r + 1, :] = side[:1].astype(jnp.int32)
        early[...] = early_sum
        copy = pltpu.make_async_copy(marks_int, marks, sem)
        copy.start()
        copy.wait()
        for s in range(slots):
            rows[s] = marks[s // per_run, LANES - per_run + s % per_run]
        result = add_rows(got, lambda s: s // per_run * wide + s % per_run, rows, runs, sums)
    else:
        result = add_rows(got, lambda s: s, rows, runs, sums)
    blocks = w.shape[1] // LANES
    for b in range(blocks):
        start = result(b)
        image[:, b * LANES : (b + 1) * LANES] = start
        here = block_of(w, b)
        slack = slack_of(here, block_of(center, b), block_of(width, b))
        rho = rho_of(level, b)
        sums[0][b] = rho * (slack - start) - rho * (here - slack)
    for s in range(slots):
        send[s] = sums[0][rows[s]]


def transpose_kernel(first, *refs):
    if first:
        back, slot, cols, tiles, early, send, acc = refs
    else:
        back, slot, cols, tiles, send, acc = refs
    acc[...] = jnp.zeros_like(acc)

    def one(t):
        high, low = halves(tiles[t])
        term = times(stacked(back[slot[t]]), jnp.concatenate([high, low], axis=0), 0)
        col = cols[t]
        acc[col] = acc[col] + term

    tile_loop(tiles.shape[0], one)
    columns = acc.shape[0]
    for b in range(columns):
        value = acc[b]
        for c in range(send.shape[0]):
            send[c, :, b * LANES : (b + 1) * LANES] = value
    if first:
        value = early[...]
        for c in range(send.shape[0]):
            send[c, :, columns * LANES :] = value


def residual_kernel(first, got, x, linear, diag, cols, slot, tiles, send, resid, *refs):
    columns = x.shape[1] // LANES
    if first:
        early, left = refs
    else:
        (left,) = refs
    for b in range(columns):
        lo, hi = b * LANES, (b + 1) * LANES
        value = -linear[:, lo:hi] - diag[:, lo:hi] * x[:, lo:hi]
        part = got[0, :, lo:hi]
        for c in range(1, got.shape[0]):
            part = part + got[c, :, lo:hi]
        resid[:, lo:hi] = value + part
    if first:
        part = got[0, :, columns * LANES :]
        for c in range(1, got.shape[0]):
            part = part + got[c, :, columns * LANES :]
        early[...] = part
    send_products(resid, cols, lambda t: slot[t], tiles, send, left)


def scalar_kernel(
    per_run, got, rows, con, start, w, center, width, level, pw, pgw, x, px, pgx, resid, diag, hgx, hgw, qgx, qgw, send, image, *sums
):
    problems = w.shape[0]
    result = add_rows(got, lambda s: s, rows, sums[0].shape[0], sums)
    memory = hgx.shape[0]
    acc = [None] * SCALARS

    def add(i, value):
        acc[i] = value if acc[i] is None else acc[i] + value

    def terms(u, v, p, s, d, hist):
        for m in range(memory):
            h = hist(m)
            add(U_H + m, u * h)
            add(V_H + m, v * h)
        for i, value in ((U_U, u * u), (U_V, u * v), (U_P, u * p), (V_P, v * p), (V_V, v * v), (S_S, s * s), (U_D, u * d), (V_D, v * d)):
            add(i, value)

    for b in range(w.shape[1] // LANES):
        ar = result(b)
        image[:, b * LANES : (b + 1) * LANES] = ar
        here = block_of(w, b)
        slack = slack_of(here, block_of(center, b), block_of(width, b))
        p = block_of(pgw, b)
        u = relax * (block_of(start, b) - slack) - p
        add(C_C, rho_of(level, b) * ar * ar)
        terms(u, relax * ar, p, here - block_of(pw, b), p - block_of(qgw, b), lambda m: hgw[m, :, b * LANES : (b + 1) * LANES])
    share = x.shape[1] // LANES // con[1]
    for i in range(share):
        b = con[0] * share + i
        r = at(resid, b)
        p = at(pgx, b)
        add(R_R, r * r)
        add(C_C, at(diag, b) * r * r)
        terms(-p, relax * r, p, at(x, b) - at(px, b), p - at(qgx, b), lambda m: hgx[m, :, pl.ds(pl.multiple_of(b * LANES, LANES), LANES)])
    lanes = lane_ids((problems, LANES))
    lane_of = 16 * lax.broadcasted_iota(jnp.int32, (problems, LANES), 0)
    packed = []
    for row in range(2):
        tile = jnp.zeros((problems, LANES), f32)
        for i in range(16):
            if row * 16 + i < SCALARS:
                tile = jnp.where(lanes == lane_of + i, total(acc[row * 16 + i]), tile)
        packed.append(jnp.sum(tile, axis=0, keepdims=True))
    both = jnp.concatenate(packed, axis=0)
    send[...] = jnp.broadcast_to(both[None], send.shape)


def update_kernel(last, steps_before, *refs):
    (late, known, order, sigma_level, x, px, pgx, resid, hsx, hgx, w, pw, pgw, start, image, center, width, hsw, hgw) = refs[:19]
    refs = refs[19:]
    if steps_before:
        dx, dw = refs[:2]
        refs = refs[2:]
    if last:
        x_out, w_out = refs
    else:
        cols, slot, tiles, x_out, w_out, gx_out, gw_out, dx_out, dw_out, known_out, send, left = refs
    problems = x.shape[0]
    memory = hgx.shape[0]
    shape = (problems, LANES)
    lanes = lane_ids(shape)
    program = lax.broadcasted_iota(jnp.int32, shape, 0)
    rows = late[0]
    for i in range(1, late.shape[0]):
        rows = rows + late[i]

    def scalar(i):
        row = jnp.broadcast_to(rows[i // 16 : i // 16 + 1], shape)
        picked = jnp.where(lanes == program * 16 + i % 16, row, 0.0)
        return jnp.broadcast_to(total(picked), shape)

    def given(i):
        return jnp.broadcast_to(known[:, i : i + 1], shape)

    new = [jnp.where(order[steps_before] == m, 1.0, 0.0) for m in range(memory)]
    keep = [1.0 - f for f in new]
    if steps_before:
        old = [jnp.where(order[0] == m, 1.0, 0.0) for m in range(memory)]
    sigma = jnp.zeros(shape, f32)
    for k in range(problems):
        sigma = jnp.where(program == k, 0.2 * (1.0 + sigma_level[k].astype(f32)), sigma)
    norm = scalar(R_R)
    step = norm / (scalar(C_C) + sigma * norm)
    u_h = [scalar(U_H + m) for m in range(memory)]
    v_h = [scalar(V_H + m) for m in range(memory)]
    if steps_before:
        u_d, v_d = scalar(U_D), scalar(V_D)
        u_h = [h * (1.0 - f) + u_d * f for h, f in zip(u_h, old)]
        v_h = [h * (1.0 - f) + v_d * f for h, f in zip(v_h, old)]
    dot = [u + step * v for u, v in zip(u_h, v_h)]
    own = scalar(U_U) + 2.0 * step * scalar(U_V) + step * step * scalar(V_V)
    with_p = scalar(U_P) + step * scalar(V_P)
    gram = [[None] * memory for _ in range(memory)]
    for m in range(memory):
        gram[m][m] = given(m * memory + m) * keep[m] + own * new[m]
        for n in range(m + 1, memory):
            value = given(m * memory + n) * (keep[m] * keep[n]) + dot[n] * new[m] + dot[m] * new[n]
            gram[m][n] = gram[n][m] = value
    at_p, at_s = memory * memory, memory * (memory + 1)
    rhs = []
    for m in range(memory):
        value = given(at_p + m) * keep[m] + with_p * new[m]
        for n in range(memory):
            value = value + gram[m][n] * new[n]
        rhs.append(value)
    s_s = scalar(S_S)
    squares = [given(at_s + m) * keep[m] + s_s * new[m] for m in range(memory)]
    frob = functools.reduce(lambda p, q: p + q, squares + [gram[m][m] for m in range(memory)])
    damp = ridge * frob
    if not last:
        out = jnp.zeros(shape, f32)
        for m in range(memory):
            for n in range(m, memory):
                out = jnp.where((lanes == m * memory + n) | (lanes == n * memory + m), gram[m][n], out)
            out = jnp.where(lanes == at_p + m, rhs[m], out)
            out = jnp.where(lanes == at_s + m, squares[m], out)
        known_out[...] = out
    low = [[None] * memory for _ in range(memory)]
    inverse = []
    for j in range(memory):
        value = gram[j][j] + damp
        for k in range(j):
            value = value - low[j][k] * low[j][k]
        inverse.append(1.0 / jnp.sqrt(value))
        for i in range(j + 1, memory):
            value = gram[i][j]
            for k in range(j):
                value = value - low[i][k] * low[j][k]
            low[i][j] = value * inverse[j]
    half = []
    for i in range(memory):
        value = rhs[i]
        for k in range(i):
            value = value - low[i][k] * half[k]
        half.append(value * inverse[i])
    coef = [None] * memory
    for i in reversed(range(memory)):
        value = half[i]
        for k in range(i + 1, memory):
            value = value - low[k][i] * coef[k]
        coef[i] = value * inverse[i]

    newest = functools.reduce(lambda p, q: p + q, [c * f for c, f in zip(coef, new)])
    left_over = [c * f for c, f in zip(coef, keep)]
    if steps_before:
        older = functools.reduce(lambda p, q: p + q, [c * f for c, f in zip(left_over, old)])
        left_over = [c * (1.0 - f) for c, f in zip(left_over, old)]

    def advance(b, state, previous, g, previous_g, hs, hg, kept, out, g_out, d_out):
        lo, hi = b * LANES, (b + 1) * LANES
        here = state[:, lo:hi]
        fresh = (here - previous[:, lo:hi]) + (g - previous_g[:, lo:hi])
        value = here + g - newest * fresh
        for m in range(memory):
            value = value - left_over[m] * (hs[m, :, lo:hi] + hg[m, :, lo:hi])
        if steps_before:
            value = value - older * kept[:, lo:hi]
        out[:, lo:hi] = value
        if not last:
            g_out[:, lo:hi] = g
            d_out[:, lo:hi] = fresh

    scaled = relax * step
    for b in range(x.shape[1] // LANES):
        g = scaled * block_of(resid, b)
        advance(b, x, px, g, pgx, hsx, hgx, dx if steps_before else None, x_out, None if last else gx_out, None if last else dx_out)
    for b in range(w.shape[1] // LANES):
        slack = slack_of(block_of(w, b), block_of(center, b), block_of(width, b))
        g = relax * (block_of(start, b) + step * block_of(image, b) - slack)
        advance(b, w, pw, g, pgw, hsw, hgw, dw if steps_before else None, w_out, None if last else gw_out, None if last else dw_out)
    if not last:
        send_products(x_out, cols, lambda t: slot[t], tiles, send, left)


def call(kernel, name, ins, outs, scratch=()):
    spaces = {"v": pltpu.VMEM, "s": pltpu.SMEM}
    return pl.pallas_call(
        kernel,
        out_shape=[jax.ShapeDtypeStruct(shape, dtype) for shape, dtype, _ in outs],
        in_specs=[pl.BlockSpec(memory_space=spaces[space]) for _, space in ins],
        out_specs=[pl.BlockSpec(memory_space=spaces[space]) for _, _, space in outs],
        scratch_shapes=list(scratch),
        compiler_params=pltpu.CompilerParams(vmem_limit_bytes=24 * 1024 * 1024),
        name=name,
    )(*[array for array, _ in ins])


def per_device(
    tiles,
    row_tile,
    col_tile,
    diag_cost,
    linear_cost,
    bound_center,
    bound_width,
    rho_level,
    sigma_level,
    state_x,
    state_w,
    prev_x,
    prev_w,
    prev_gx,
    prev_gw,
    hist_sx,
    hist_sw,
    hist_gx,
    hist_gw,
    slot_order,
):
    problems, var_cols = state_x.shape
    con_cols = state_w.shape[1]
    tile_size = tiles.shape[-1]
    var_count, con_count = lax.axis_size("var"), lax.axis_size("con")
    col_count = var_cols // tile_size
    run_length = con_cols // tile_size
    blocks = tiles.reshape(-1, tile_size, tile_size)
    count = blocks.shape[0]
    per_run = -(-count // var_count)
    slots = var_count * per_run
    rows_here = row_tile.reshape(-1)
    cols_here = col_tile.reshape(-1)
    diag = diag_cost.reshape(1, -1)
    level = rho_level.reshape(1, -1)
    con = jnp.stack([lax.axis_index("con").astype(jnp.int32), jnp.int32(con_count)])

    x_like = ((problems, var_cols), f32, "v")
    w_like = ((problems, con_cols), f32, "v")
    panel = ((slots, problems, tile_size), f32, "v")
    wide_panel = ((slots + var_count, problems, tile_size), f32, "v")
    one_tile = ((problems, tile_size), f32, "v")
    left = pltpu.VMEM((col_count, 2 * problems, 2 * tile_size), bf16)
    sums = [pltpu.VMEM((run_length, problems, tile_size), f32)] * 4
    bounds = [(bound_center, "v"), (bound_width, "v")]
    vs = lambda *arrays: [(a, "v") for a in arrays]
    ss = lambda *arrays: [(a, "s") for a in arrays]

    def exchange(x):
        return lax.all_to_all(x, "var", 0, 0, tiled=True)

    def open_with_sizes(rows, cols, where, *refs):
        return open_kernel(per_run, run_length, rows, cols, (where[0], con_count), *refs)

    sent, slot = call(
        open_with_sizes,
        "open",
        ss(rows_here, cols_here, con)
        + vs(blocks, state_x, prev_x, state_w, prev_w, prev_gx, prev_gw, hist_sx, hist_sw, hist_gx, hist_gw),
        [wide_panel, ((count,), jnp.int32, "s")],
        [left, pltpu.SMEM((var_count,), jnp.int32), pltpu.SMEM((slots,), jnp.int32)],
    )
    got = exchange(sent)
    x, w, px, pw, pgx, pgw = state_x, state_w, prev_x, prev_w, prev_gx, prev_gw
    qgx, qgw = pgx, pgw
    kept = []
    known = None
    for step in range(STEPS):
        first, last = step == 0, step == STEPS - 1
        if first:
            sent, start, early, rows = call(
                functools.partial(penalty_kernel, True, per_run),
                "penalty_first",
                vs(got, w, bound_center, bound_width, level),
                [panel, w_like, one_tile, ((slots,), jnp.int32, "s")],
                [pltpu.SMEM((var_count, tile_size), jnp.int32), pltpu.VMEM((var_count, tile_size), jnp.int32), pltpu.SemaphoreType.DMA(())]
                + sums,
            )
        else:
            sent, start = call(
                functools.partial(penalty_kernel, False, per_run),
                "penalty",
                vs(got) + ss(rows) + vs(w, bound_center, bound_width, level),
                [panel, w_like],
                sums,
            )
        back = exchange(sent)
        width = var_cols + (tile_size if first else 0)
        (sent,) = call(
            functools.partial(transpose_kernel, first),
            "transpose",
            vs(back) + ss(slot, cols_here) + vs(blocks) + (vs(early) if first else []),
            [((con_count, problems, width), f32, "v")],
            [pltpu.VMEM((col_count, problems, tile_size), f32)],
        )
        got = lax.all_to_all(sent, "con", 0, 0, tiled=True)
        outs = call(
            functools.partial(residual_kernel, first),
            "residual",
            vs(got, x, linear_cost, diag) + ss(cols_here, slot) + vs(blocks),
            [panel, x_like] + ([one_tile] if first else []),
            [left],
        )
        sent, resid = outs[:2]
        if first:
            known = outs[2]
        got = exchange(sent)

        def scalars_with_sizes(got, rows, where, *refs):
            return scalar_kernel(per_run, got, rows, (where[0], con_count), *refs)

        sent, image = call(
            scalars_with_sizes,
            "scalars",
            vs(got)
            + ss(rows, con)
            + vs(start, w, bound_center, bound_width, level, pw, pgw, x, px, pgx, resid, diag, hist_gx, hist_gw, qgx, qgw),
            [((con_count * var_count, 2, LANES), f32, "v"), w_like],
            sums,
        )
        late = lax.all_to_all(sent, ("con", "var"), 0, 0, tiled=True)
        outs = call(
            functools.partial(update_kernel, last, step),
            "update",
            vs(late, known)
            + ss(slot_order, sigma_level)
            + vs(x, px, pgx, resid, hist_sx, hist_gx, w, pw, pgw, start, image, bound_center, bound_width, hist_sw, hist_gw)
            + vs(*kept)
            + ([] if last else ss(cols_here, slot) + vs(blocks)),
            [x_like, w_like] + ([] if last else [x_like, w_like, x_like, w_like, one_tile, panel]),
            [] if last else [left],
        )
        if last:
            return outs[0], outs[1]
        qgx, qgw = pgx, pgw
        px, pw = x, w
        x, w, pgx, pgw, dx, dw, known, sent = outs
        kept = [dx, dw]
        got = exchange(sent)


def solution(mesh):
    in_specs = (
        P("con", "var", None, None, None),
        P("con", "var", None),
        P("con", "var", None),
        P("var"),
        P(None, "var"),
        P(None, ("con", "var")),
        P(None, ("con", "var")),
        P(("con", "var")),
        P(),
        P(None, "var"),
        P(None, ("con", "var")),
        P(None, "var"),
        P(None, ("con", "var")),
        P(None, "var"),
        P(None, ("con", "var")),
        P(None, None, "var"),
        P(None, None, ("con", "var")),
        P(None, None, "var"),
        P(None, None, ("con", "var")),
        P(),
    )
    out_specs = (P(None, "var"), P(None, ("con", "var")))
    return jax.shard_map(
        per_device, mesh=mesh, in_specs=in_specs, out_specs=out_specs, check_vma=False
    )
```

```python
import functools

import jax
import jax.numpy as jnp
from jax import lax
from jax.experimental import pallas as pl
from jax.experimental.pallas import tpu as pltpu
from jax.sharding import PartitionSpec as P

STEPS = 2
LANES = 128
UNROLL = 24

relax = 1.6
ridge = 0.01

f32 = jnp.float32
bf16 = jnp.bfloat16

U_H, V_H, U_U, U_V, U_P, V_P, V_V, S_S, R_R, C_C, U_D, V_D, SCALARS = 0, 8, 16, 17, 18, 19, 20, 21, 22, 23, 24, 25, 26


def halves(value):
    high = value.astype(bf16)
    return high, (value - high.astype(f32)).astype(bf16)


def stacked(piece):
    high, low = halves(piece)
    return jnp.concatenate(
        [
            jnp.concatenate([high, high], axis=1),
            jnp.concatenate([low, jnp.zeros_like(low)], axis=1),
        ],
        axis=0,
    )


def times(left, right, contract):
    both = lax.dot_general(left, right, (((1,), (contract,)), ((), ())), preferred_element_type=f32)
    half = both.shape[0] // 2
    return both[:half] + both[half:]


def at(ref, block):
    return ref[:, pl.ds(pl.multiple_of(block * LANES, LANES), LANES)]


def tile_loop(count, body):
    step = max(d for d in range(1, UNROLL + 1) if count % d == 0)

    def some(i, _):
        for j in range(step):
            body(i * step + j)
        return 0

    lax.fori_loop(0, count // step, some, 0)


def lane_ids(shape):
    return lax.broadcasted_iota(jnp.int32, shape, len(shape) - 1)


def send_products(x_ref, cols, where, tiles, send, left, waits=(None,)):
    for block in range(x_ref.shape[1] // LANES):
        left[block] = stacked(x_ref[:, block * LANES : (block + 1) * LANES])
    send[...] = jnp.zeros_like(send)

    def one(t):
        high, low = halves(tiles[t])
        send[where(t)] = times(left[cols[t]], jnp.concatenate([high, low], axis=1), 1)

    size = tiles.shape[0] // len(waits)
    for i, wait in enumerate(waits):
        if wait is not None:
            wait()
        tile_loop(size, lambda t, i=i: one(t + i * size))


def add_rows(got, index, rows, runs, sums):
    for ref in sums:
        ref[...] = jnp.zeros_like(ref)
    for s in range(rows.shape[0]):
        ref = sums[s % len(sums)]
        row = rows[s]
        ref[row] = ref[row] + got[index(s)]
    return lambda b: functools.reduce(lambda p, q: p + q, [ref[b] for ref in sums])


def block_of(ref, b):
    return ref[:, b * LANES : (b + 1) * LANES]


def rho_of(level_ref, b):
    return 0.4 * (1.0 + block_of(level_ref, b).astype(f32))


def slack_of(w, center, width):
    return jnp.minimum(jnp.maximum(w, center - width), center + width)


def total(value):
    return jnp.sum(value, axis=1, keepdims=True)


def open_kernel(per_run, run_length, share, parts, *refs):
    (hbm_rows, hbm_cols, hbm_x, hbm_tiles, *far), (send, slot), refs = refs[:13], refs[13:15], refs[15:]
    rows_buf, cols_buf, x, tiles, px, w, pw, pgx, pgw, hsx, hsw, hgx, hgw, left, count, asked, sem = refs
    memory = hgx.shape[0]
    problems = x.shape[0]
    runs = send.shape[0] // (per_run + 1)
    wide = per_run + 1
    first = lax.axis_index("con") * share
    mine = pl.ds(pl.multiple_of(first * LANES, LANES), share * LANES)
    far_px, far_w, far_pw, far_pgx, far_pgw, far_hsx, far_hsw, far_hgx, far_hgw = far
    size = tiles.shape[0] // parts
    moves = [(hbm_rows, rows_buf), (hbm_cols, cols_buf), (hbm_x, x)]
    moves += [(hbm_tiles.at[pl.ds(i * size, size)], tiles.at[pl.ds(i * size, size)]) for i in range(parts)]
    moves += [(far_w, w), (far_pw, pw), (far_pgw, pgw), (far_hsw, hsw), (far_hgw, hgw)]
    moves += [(far_px.at[:, mine], px), (far_pgx.at[:, mine], pgx), (far_hsx.at[:, :, mine], hsx), (far_hgx.at[:, :, mine], hgx)]
    copies = [pltpu.make_async_copy(a, b, sem.at[i]) for i, (a, b) in enumerate(moves)]
    for copy in copies:
        copy.start()
    rows, cols = rows_buf.at[0], cols_buf.at[0]

    def clear(i, _):
        count[i] = 0
        return 0

    lax.fori_loop(0, runs, clear, 0)

    def clear_asked(i, _):
        asked[i] = 0
        return 0

    lax.fori_loop(0, runs * per_run, clear_asked, 0)
    copies[0].wait()
    copies[1].wait()

    def assign(t, _):
        owner = rows[t] // run_length
        rank = count[owner]
        count[owner] = rank + 1
        slot[t] = owner * per_run + rank
        asked[owner * per_run + rank] = rows[t] - owner * run_length
        return 0

    lax.fori_loop(0, tiles.shape[0], assign, 0)

    def where(t):
        owner = slot[t] // per_run
        return slot[t] + owner

    copies[2].wait()
    send_products(x, cols, where, tiles, send, left, [copy.wait for copy in copies[3 : 3 + parts]])
    for copy in copies[3 + parts :]:
        copy.wait()

    lanes = lane_ids((problems, LANES))
    out = jnp.zeros((problems, LANES), f32)

    def both(f):
        acc = None
        for b in range(w.shape[1] // LANES):
            v = f(False, b)
            acc = v if acc is None else acc + v
        for b in range(share):
            acc = acc + f(True, b)
        return total(acc)

    def hist(ref_x, ref_w, m, is_x, b):
        return (ref_x if is_x else ref_w)[m, :, b * LANES : (b + 1) * LANES]

    def plain(ref_x, ref_w, is_x, b):
        return block_of(ref_x if is_x else ref_w, b)

    for m in range(memory):
        for n in range(m, memory):
            value = both(lambda q, b: hist(hgx, hgw, m, q, b) * hist(hgx, hgw, n, q, b))
            out = jnp.where((lanes == m * memory + n) | (lanes == n * memory + m), value, out)
        value = both(lambda q, b: hist(hgx, hgw, m, q, b) * plain(pgx, pgw, q, b))
        out = jnp.where(lanes == memory * memory + m, value, out)

        def square(q, b):
            h = hist(hsx, hsw, m, q, b)
            return h * h

        out = jnp.where(lanes == memory * (memory + 1) + m, both(square), out)
    for r in range(runs):
        mark = out
        for s in range(per_run):
            mark = jnp.where(lanes == LANES - per_run + s, asked[r * per_run + s].astype(f32), mark)
        send[r * wide + per_run] = mark


def penalty_kernel(first, per_run, *refs):
    if first:
        got, w, center, width, level, send, image, early, rows, marks, marks_int, sem, *sums = refs
    else:
        got, rows, w, center, width, level, send, image, *sums = refs
    slots = send.shape[0]
    runs = slots // per_run
    if first:
        wide = per_run + 1
        early_sum = None
        for r in range(runs):
            side = got[r * wide + per_run]
            early_sum = side if early_sum is None else early_sum + side
            marks_int[r : r + 1, :] = side[:1].astype(jnp.int32)
        early[...] = early_sum
        copy = pltpu.make_async_copy(marks_int, marks, sem)
        copy.start()
        copy.wait()
        for s in range(slots):
            rows[s] = marks[s // per_run, LANES - per_run + s % per_run]
        result = add_rows(got, lambda s: s // per_run * wide + s % per_run, rows, runs, sums)
    else:
        result = add_rows(got, lambda s: s, rows, runs, sums)
    blocks = w.shape[1] // LANES
    for b in range(blocks):
        start = result(b)
        image[:, b * LANES : (b + 1) * LANES] = start
        here = block_of(w, b)
        slack = slack_of(here, block_of(center, b), block_of(width, b))
        rho = rho_of(level, b)
        sums[0][b] = rho * (slack - start) - rho * (here - slack)
    for s in range(slots):
        send[s] = sums[0][rows[s]]


def transpose_kernel(first, *refs):
    if first:
        back, slot, cols, tiles, early, send, acc = refs
    else:
        back, slot, cols, tiles, send, acc = refs
    acc[...] = jnp.zeros_like(acc)

    def one(t):
        high, low = halves(tiles[t])
        term = times(stacked(back[slot[t]]), jnp.concatenate([high, low], axis=0), 0)
        col = cols[t]
        acc[col] = acc[col] + term

    tile_loop(tiles.shape[0], one)
    columns = acc.shape[0]
    for b in range(columns):
        send[:, b * LANES : (b + 1) * LANES] = acc[b]
    if first:
        send[:, columns * LANES :] = early[...]


def residual_kernel(first, own, other, x, linear, diag, cols, slot, tiles, send, resid, *refs):
    columns = x.shape[1] // LANES
    if first:
        early, left = refs
    else:
        (left,) = refs
    for b in range(columns):
        lo, hi = b * LANES, (b + 1) * LANES
        value = -linear[:, lo:hi] - diag[:, lo:hi] * x[:, lo:hi]
        resid[:, lo:hi] = value + (own[:, lo:hi] + other[:, lo:hi])
    if first:
        early[...] = own[:, columns * LANES :] + other[:, columns * LANES :]
    send_products(resid, cols, lambda t: slot[t], tiles, send, left)


def scalar_kernel(
    share, got, rows, start, w, center, width, level, pw, pgw, x, px, pgx, resid, diag, hgx, hgw, qgx, qgw, send, image, *sums
):
    problems = w.shape[0]
    result = add_rows(got, lambda s: s, rows, sums[0].shape[0], sums)
    memory = hgx.shape[0]
    acc = [None] * SCALARS

    def add(i, value):
        acc[i] = value if acc[i] is None else acc[i] + value

    def terms(u, v, p, s, d, hist):
        for m in range(memory):
            h = hist(m)
            add(U_H + m, u * h)
            add(V_H + m, v * h)
        for i, value in ((U_U, u * u), (U_V, u * v), (U_P, u * p), (V_P, v * p), (V_V, v * v), (S_S, s * s), (U_D, u * d), (V_D, v * d)):
            add(i, value)

    for b in range(w.shape[1] // LANES):
        ar = result(b)
        image[:, b * LANES : (b + 1) * LANES] = ar
        here = block_of(w, b)
        slack = slack_of(here, block_of(center, b), block_of(width, b))
        p = block_of(pgw, b)
        u = relax * (block_of(start, b) - slack) - p
        add(C_C, rho_of(level, b) * ar * ar)
        terms(u, relax * ar, p, here - block_of(pw, b), p - block_of(qgw, b), lambda m: hgw[m, :, b * LANES : (b + 1) * LANES])
    for i in range(share):
        b = lax.axis_index("con") * share + i
        r = at(resid, b)
        p = at(pgx, b)
        add(R_R, r * r)
        add(C_C, at(diag, b) * r * r)
        terms(-p, relax * r, p, at(x, b) - at(px, b), p - at(qgx, b), lambda m: hgx[m, :, pl.ds(pl.multiple_of(b * LANES, LANES), LANES)])
    lanes = lane_ids((problems, LANES))
    lane_of = 16 * lax.broadcasted_iota(jnp.int32, (problems, LANES), 0)
    packed = []
    for row in range(2):
        tile = jnp.zeros((problems, LANES), f32)
        for i in range(16):
            if row * 16 + i < SCALARS:
                tile = jnp.where(lanes == lane_of + i, total(acc[row * 16 + i]), tile)
        packed.append(jnp.sum(tile, axis=0, keepdims=True))
    both = jnp.concatenate(packed, axis=0)
    send[...] = jnp.broadcast_to(both[None], send.shape)


def update_kernel(last, steps_before, *refs):
    (late, known, order, sigma_level, x, px, pgx, resid, hsx, hgx) = refs[:10]
    refs = refs[10:]
    if last:
        (w, pw, pgw, start, image, center, width, hsw, hgw) = refs[:9]
        refs = refs[9:]
    if steps_before:
        dx, dw = refs[:2]
        refs = refs[2:]
    if last:
        x_out, w_out = refs
    else:
        cols, slot, tiles, x_out, gx_out, dx_out, known_out, factors, send, left = refs
    problems = x.shape[0]
    memory = hgx.shape[0]
    shape = (problems, LANES)
    lanes = lane_ids(shape)
    program = lax.broadcasted_iota(jnp.int32, shape, 0)
    chains = [late[i] for i in range(8)]
    for i in range(8, late.shape[0]):
        chains[i % 8] = chains[i % 8] + late[i]
    rows = functools.reduce(lambda p, q: p + q, chains)

    def scalar(i):
        row = jnp.broadcast_to(rows[i // 16 : i // 16 + 1], shape)
        picked = jnp.where(lanes == program * 16 + i % 16, row, 0.0)
        return jnp.broadcast_to(total(picked), shape)

    def given(i):
        return jnp.broadcast_to(known[:, i : i + 1], shape)

    new = [jnp.where(order[steps_before] == m, 1.0, 0.0) for m in range(memory)]
    keep = [1.0 - f for f in new]
    if steps_before:
        old = [jnp.where(order[0] == m, 1.0, 0.0) for m in range(memory)]
    sigma = jnp.zeros(shape, f32)
    for k in range(problems):
        sigma = jnp.where(program == k, 0.2 * (1.0 + sigma_level[k].astype(f32)), sigma)
    norm = scalar(R_R)
    step = norm / (scalar(C_C) + sigma * norm)
    u_h = [scalar(U_H + m) for m in range(memory)]
    v_h = [scalar(V_H + m) for m in range(memory)]
    if steps_before:
        u_d, v_d = scalar(U_D), scalar(V_D)
        u_h = [h * (1.0 - f) + u_d * f for h, f in zip(u_h, old)]
        v_h = [h * (1.0 - f) + v_d * f for h, f in zip(v_h, old)]
    dot = [u + step * v for u, v in zip(u_h, v_h)]
    own = scalar(U_U) + 2.0 * step * scalar(U_V) + step * step * scalar(V_V)
    with_p = scalar(U_P) + step * scalar(V_P)
    gram = [[None] * memory for _ in range(memory)]
    for m in range(memory):
        gram[m][m] = given(m * memory + m) * keep[m] + own * new[m]
        for n in range(m + 1, memory):
            value = given(m * memory + n) * (keep[m] * keep[n]) + dot[n] * new[m] + dot[m] * new[n]
            gram[m][n] = gram[n][m] = value
    at_p, at_s = memory * memory, memory * (memory + 1)
    rhs = []
    for m in range(memory):
        value = given(at_p + m) * keep[m] + with_p * new[m]
        for n in range(memory):
            value = value + gram[m][n] * new[n]
        rhs.append(value)
    s_s = scalar(S_S)
    squares = [given(at_s + m) * keep[m] + s_s * new[m] for m in range(memory)]
    frob = functools.reduce(lambda p, q: p + q, squares + [gram[m][m] for m in range(memory)])
    damp = ridge * frob
    if not last:
        out = jnp.zeros(shape, f32)
        for m in range(memory):
            for n in range(m, memory):
                out = jnp.where((lanes == m * memory + n) | (lanes == n * memory + m), gram[m][n], out)
            out = jnp.where(lanes == at_p + m, rhs[m], out)
            out = jnp.where(lanes == at_s + m, squares[m], out)
        known_out[...] = out
    low = [[None] * memory for _ in range(memory)]
    inverse = []
    for j in range(memory):
        value = gram[j][j] + damp
        for k in range(j):
            value = value - low[j][k] * low[j][k]
        inverse.append(1.0 / jnp.sqrt(value))
        for i in range(j + 1, memory):
            value = gram[i][j]
            for k in range(j):
                value = value - low[i][k] * low[j][k]
            low[i][j] = value * inverse[j]
    half = []
    for i in range(memory):
        value = rhs[i]
        for k in range(i):
            value = value - low[i][k] * half[k]
        half.append(value * inverse[i])
    coef = [None] * memory
    for i in reversed(range(memory)):
        value = half[i]
        for k in range(i + 1, memory):
            value = value - low[k][i] * coef[k]
        coef[i] = value * inverse[i]

    newest = functools.reduce(lambda p, q: p + q, [c * f for c, f in zip(coef, new)])
    left_over = [c * f for c, f in zip(coef, keep)]
    if steps_before:
        older = functools.reduce(lambda p, q: p + q, [c * f for c, f in zip(left_over, old)])
        left_over = [c * (1.0 - f) for c, f in zip(left_over, old)]

    scaled = relax * step
    older = older if steps_before else None
    for b in range(x.shape[1] // LANES):
        g = scaled * block_of(resid, b)
        advance(b, newest, left_over, older, x, px, g, pgx, hsx, hgx, dx if steps_before else None, x_out, None if last else gx_out, None if last else dx_out)
    if last:
        for b in range(w.shape[1] // LANES):
            slack = slack_of(block_of(w, b), block_of(center, b), block_of(width, b))
            g = relax * (block_of(start, b) + step * block_of(image, b) - slack)
            advance(b, newest, left_over, older, w, pw, g, pgw, hsw, hgw, dw if steps_before else None, w_out, None, None)
    else:
        for i, value in enumerate([step, newest] + left_over):
            factors[i] = value
        send_products(x_out, cols, lambda t: slot[t], tiles, send, left)


def advance(b, newest, left_over, older, state, previous, g, previous_g, hs, hg, kept, out, g_out, d_out):
    lo, hi = b * LANES, (b + 1) * LANES
    here = state[:, lo:hi]
    fresh = (here - previous[:, lo:hi]) + (g - previous_g[:, lo:hi])
    value = here + g - newest * fresh
    for m in range(len(left_over)):
        value = value - left_over[m] * (hs[m, :, lo:hi] + hg[m, :, lo:hi])
    if kept is not None:
        value = value - older * kept[:, lo:hi]
    out[:, lo:hi] = value
    if g_out is not None:
        g_out[:, lo:hi] = g
        d_out[:, lo:hi] = fresh


def constraint_kernel(factors, w, pw, pgw, start, image, center, width, hsw, hgw, w_out, gw_out, dw_out):
    step, newest = factors[0], factors[1]
    left_over = [factors[2 + m] for m in range(hgw.shape[0])]
    for b in range(w.shape[1] // LANES):
        slack = slack_of(block_of(w, b), block_of(center, b), block_of(width, b))
        g = relax * (block_of(start, b) + step * block_of(image, b) - slack)
        advance(b, newest, left_over, None, w, pw, g, pgw, hsw, hgw, None, w_out, gw_out, dw_out)


def call(kernel, name, ins, outs, scratch=()):
    spaces = {"v": pltpu.VMEM, "s": pltpu.SMEM, "h": pltpu.HBM}
    return pl.pallas_call(
        kernel,
        out_shape=[jax.ShapeDtypeStruct(shape, dtype) for shape, dtype, _ in outs],
        in_specs=[pl.BlockSpec(memory_space=spaces[space]) for _, space in ins],
        out_specs=[pl.BlockSpec(memory_space=spaces[space]) for _, _, space in outs],
        scratch_shapes=list(scratch),
        compiler_params=pltpu.CompilerParams(vmem_limit_bytes=24 * 1024 * 1024),
        name=name,
    )(*[array for array, _ in ins])


def per_device(
    tiles,
    row_tile,
    col_tile,
    diag_cost,
    linear_cost,
    bound_center,
    bound_width,
    rho_level,
    sigma_level,
    state_x,
    state_w,
    prev_x,
    prev_w,
    prev_gx,
    prev_gw,
    hist_sx,
    hist_sw,
    hist_gx,
    hist_gw,
    slot_order,
):
    problems, var_cols = state_x.shape
    con_cols = state_w.shape[1]
    tile_size = tiles.shape[-1]
    var_count, con_count = lax.axis_size("var"), lax.axis_size("con")
    col_count = var_cols // tile_size
    run_length = con_cols // tile_size
    blocks = tiles.reshape(-1, tile_size, tile_size)
    count = blocks.shape[0]
    per_run = -(-count // var_count)
    slots = var_count * per_run
    rows_here = row_tile.reshape(-1)
    cols_here = col_tile.reshape(-1)
    diag = diag_cost.reshape(1, -1)
    level = rho_level.reshape(1, -1)

    x_like = ((problems, var_cols), f32, "v")
    w_like = ((problems, con_cols), f32, "v")
    panel = ((slots, problems, tile_size), f32, "v")
    wide_panel = ((slots + var_count, problems, tile_size), f32, "v")
    one_tile = ((problems, tile_size), f32, "v")
    left = pltpu.VMEM((col_count, 2 * problems, 2 * tile_size), bf16)
    sums = [pltpu.VMEM((run_length, problems, tile_size), f32)] * 4
    bounds = [(bound_center, "v"), (bound_width, "v")]
    vs = lambda *arrays: [(a, "v") for a in arrays]
    ss = lambda *arrays: [(a, "s") for a in arrays]

    def exchange(x):
        return lax.all_to_all(x, "var", 0, 0, tiled=True)

    def over_con(x):
        def partner(x, k):
            return lax.ppermute(x, "con", [(i, i ^ k) for i in range(con_count)])

        others = [partner(x, k) for k in range(2, con_count, 2)]
        terms = [x] + others
        while len(terms) > 1:
            terms = [a + b for a, b in zip(terms[::2], terms[1::2])]
        return terms[0], partner(terms[0], 1)

    share = col_count // con_count
    parts = max(d for d in range(1, 4) if count % d == 0)
    far = [state_x, blocks, prev_x, state_w, prev_w, prev_gx, prev_gw, hist_sx, hist_sw, hist_gx, hist_gw]
    x_mine, w_mine = pltpu.VMEM((problems, share * tile_size), f32), pltpu.VMEM((problems, con_cols), f32)
    memory = hist_gx.shape[0]
    hx_mine = pltpu.VMEM((memory, problems, share * tile_size), f32)
    hw_mine = pltpu.VMEM((memory, problems, con_cols), f32)
    sent, slot = call(
        functools.partial(open_kernel, per_run, run_length, share, parts),
        "open",
        [(pltpu.with_memory_space_constraint(a, pltpu.HBM), "h") for a in [row_tile[0], col_tile[0]] + far],
        [wide_panel, ((count,), jnp.int32, "s")],
        [
            pltpu.SMEM((1, count), jnp.int32),
            pltpu.SMEM((1, count), jnp.int32),
            pltpu.VMEM((problems, var_cols), f32),
            pltpu.VMEM(blocks.shape, f32),
            x_mine, w_mine, w_mine, x_mine, w_mine, hx_mine, hw_mine, hx_mine, hw_mine,
            left,
            pltpu.SMEM((var_count,), jnp.int32),
            pltpu.SMEM((slots,), jnp.int32),
            pltpu.SemaphoreType.DMA((3 + parts + 9,)),
        ],
    )
    got = exchange(sent)
    x, w, px, pw, pgx, pgw = state_x, state_w, prev_x, prev_w, prev_gx, prev_gw
    qgx, qgw = pgx, pgw
    kept = []
    known = None
    for step in range(STEPS):
        first, last = step == 0, step == STEPS - 1
        if first:
            sent, start, early, rows = call(
                functools.partial(penalty_kernel, True, per_run),
                "penalty_first",
                vs(got, w, bound_center, bound_width, level),
                [panel, w_like, one_tile, ((slots,), jnp.int32, "s")],
                [pltpu.SMEM((var_count, tile_size), jnp.int32), pltpu.VMEM((var_count, tile_size), jnp.int32), pltpu.SemaphoreType.DMA(())]
                + sums,
            )
        else:
            sent, start = call(
                functools.partial(penalty_kernel, False, per_run),
                "penalty",
                vs(got) + ss(rows) + vs(w, bound_center, bound_width, level),
                [panel, w_like],
                sums,
            )
        back = exchange(sent)
        width = var_cols + (tile_size if first else 0)
        (sent,) = call(
            functools.partial(transpose_kernel, first),
            "transpose",
            vs(back) + ss(slot, cols_here) + vs(blocks) + (vs(early) if first else []),
            [((problems, width), f32, "v")],
            [pltpu.VMEM((col_count, problems, tile_size), f32)],
        )
        own, other = over_con(sent)
        outs = call(
            functools.partial(residual_kernel, first),
            "residual",
            vs(own, other, x, linear_cost, diag) + ss(cols_here, slot) + vs(blocks),
            [panel, x_like] + ([one_tile] if first else []),
            [left],
        )
        sent, resid = outs[:2]
        if first:
            known = outs[2]
        got = exchange(sent)

        sent, image = call(
            functools.partial(scalar_kernel, share),
            "scalars",
            vs(got)
            + ss(rows)
            + vs(start, w, bound_center, bound_width, level, pw, pgw, x, px, pgx, resid, diag, hist_gx, hist_gw, qgx, qgw),
            [((con_count * var_count, 2, LANES), f32, "v"), w_like],
            sums,
        )
        late = lax.all_to_all(sent, ("con", "var"), 0, 0, tiled=True)
        con_part = vs(w, pw, pgw, start, image, bound_center, bound_width, hist_sw, hist_gw)
        outs = call(
            functools.partial(update_kernel, last, step),
            "update",
            vs(late, known)
            + ss(slot_order, sigma_level)
            + vs(x, px, pgx, resid, hist_sx, hist_gx)
            + (con_part if last else [])
            + vs(*kept)
            + ([] if last else ss(cols_here, slot) + vs(blocks)),
            [x_like, w_like] if last else [x_like, x_like, x_like, one_tile, ((memory + 2, problems, tile_size), f32, "v"), panel],
            [] if last else [left],
        )
        if last:
            return outs[0], outs[1]
        new_x, new_gx, dx, known, factors, sent = outs
        got = exchange(sent)
        new_w, new_gw, dw = call(constraint_kernel, "constraints", vs(factors) + con_part, [w_like] * 3)
        qgx, qgw = pgx, pgw
        px, pw, pgx, pgw = x, w, new_gx, new_gw
        x, w = new_x, new_w
        kept = [dx, dw]


def solution(mesh):
    in_specs = (
        P("con", "var", None, None, None),
        P("con", "var", None),
        P("con", "var", None),
        P("var"),
        P(None, "var"),
        P(None, ("con", "var")),
        P(None, ("con", "var")),
        P(("con", "var")),
        P(),
        P(None, "var"),
        P(None, ("con", "var")),
        P(None, "var"),
        P(None, ("con", "var")),
        P(None, "var"),
        P(None, ("con", "var")),
        P(None, None, "var"),
        P(None, None, ("con", "var")),
        P(None, None, "var"),
        P(None, None, ("con", "var")),
        P(),
    )
    out_specs = (P(None, "var"), P(None, ("con", "var")))
    return jax.shard_map(
        per_device, mesh=mesh, in_specs=in_specs, out_specs=out_specs, check_vma=False
    )
```

```python
import functools

import jax
import jax.numpy as jnp
from jax import lax
from jax.experimental import pallas as pl
from jax.experimental.pallas import tpu as pltpu
from jax.sharding import PartitionSpec as P

STEPS = 2
LANES = 128
UNROLL = 24

relax = 1.6
ridge = 0.01

f32 = jnp.float32
bf16 = jnp.bfloat16

U_H, V_H, U_U, U_V, U_P, V_P, V_V, S_S, R_R, C_C, U_D, V_D, SCALARS = 0, 8, 16, 17, 18, 19, 20, 21, 22, 23, 24, 25, 26


def halves(value):
    high = value.astype(bf16)
    return high, (value - high.astype(f32)).astype(bf16)


def stacked(piece):
    high, low = halves(piece)
    return jnp.concatenate(
        [
            jnp.concatenate([high, high], axis=1),
            jnp.concatenate([low, jnp.zeros_like(low)], axis=1),
        ],
        axis=0,
    )


def times(left, right, contract):
    both = lax.dot_general(left, right, (((1,), (contract,)), ((), ())), preferred_element_type=f32)
    half = both.shape[0] // 2
    return both[:half] + both[half:]


def at(ref, block):
    return ref[:, pl.ds(pl.multiple_of(block * LANES, LANES), LANES)]


def tile_loop(count, body):
    step = max(d for d in range(1, UNROLL + 1) if count % d == 0)

    def some(i, _):
        for j in range(step):
            body(i * step + j)
        return 0

    lax.fori_loop(0, count // step, some, 0)


def lane_ids(shape):
    return lax.broadcasted_iota(jnp.int32, shape, len(shape) - 1)


def send_products(x_ref, cols, where, tiles, send, left, waits=(None,)):
    for block in range(x_ref.shape[1] // LANES):
        left[block] = stacked(x_ref[:, block * LANES : (block + 1) * LANES])
    send[...] = jnp.zeros_like(send)

    def one(t):
        high, low = halves(tiles[t])
        send[where(t)] = times(left[cols[t]], jnp.concatenate([high, low], axis=1), 1)

    size = tiles.shape[0] // len(waits)
    for i, wait in enumerate(waits):
        if wait is not None:
            wait()
        tile_loop(size, lambda t, i=i: one(t + i * size))


def add_rows(got, index, rows, runs, sums):
    for ref in sums:
        ref[...] = jnp.zeros_like(ref)
    for s in range(rows.shape[0]):
        ref = sums[s % len(sums)]
        row = rows[s]
        ref[row] = ref[row] + got[index(s)]
    return lambda b: functools.reduce(lambda p, q: p + q, [ref[b] for ref in sums])


def block_of(ref, b):
    return ref[:, b * LANES : (b + 1) * LANES]


def rho_of(level_ref, b):
    return 0.4 * (1.0 + block_of(level_ref, b).astype(f32))


def slack_of(w, center, width):
    return jnp.minimum(jnp.maximum(w, center - width), center + width)


def total(value):
    return jnp.sum(value, axis=1, keepdims=True)


def open_kernel(per_run, run_length, share, parts, *refs):
    (hbm_rows, hbm_cols, hbm_x, hbm_tiles, *far), (send, slot), refs = refs[:13], refs[13:15], refs[15:]
    rows_buf, cols_buf, x, tiles, px, w, pw, pgx, pgw, hsx, hsw, hgx, hgw, left, count, asked, sem = refs
    memory = hgx.shape[0]
    problems = x.shape[0]
    runs = send.shape[0] // (per_run + 1)
    wide = per_run + 1
    first = lax.axis_index("con") * share
    mine = pl.ds(pl.multiple_of(first * LANES, LANES), share * LANES)
    far_px, far_w, far_pw, far_pgx, far_pgw, far_hsx, far_hsw, far_hgx, far_hgw = far
    size = tiles.shape[0] // parts
    moves = [(hbm_rows, rows_buf), (hbm_cols, cols_buf), (hbm_x, x)]
    moves += [(hbm_tiles.at[pl.ds(i * size, size)], tiles.at[pl.ds(i * size, size)]) for i in range(parts)]
    moves += [(far_w, w), (far_pw, pw), (far_pgw, pgw), (far_hsw, hsw), (far_hgw, hgw)]
    moves += [(far_px.at[:, mine], px), (far_pgx.at[:, mine], pgx), (far_hsx.at[:, :, mine], hsx), (far_hgx.at[:, :, mine], hgx)]
    copies = [pltpu.make_async_copy(a, b, sem.at[i]) for i, (a, b) in enumerate(moves)]
    for copy in copies:
        copy.start()
    rows, cols = rows_buf.at[0], cols_buf.at[0]

    def clear(i, _):
        count[i] = 0
        return 0

    lax.fori_loop(0, runs, clear, 0)

    def clear_asked(i, _):
        asked[i] = 0
        return 0

    lax.fori_loop(0, runs * per_run, clear_asked, 0)
    copies[0].wait()
    copies[1].wait()

    def assign(t, _):
        owner = rows[t] // run_length
        rank = count[owner]
        count[owner] = rank + 1
        slot[t] = owner * per_run + rank
        asked[owner * per_run + rank] = rows[t] - owner * run_length
        return 0

    lax.fori_loop(0, tiles.shape[0], assign, 0)

    def where(t):
        owner = slot[t] // per_run
        return slot[t] + owner

    copies[2].wait()
    send_products(x, cols, where, tiles, send, left, [copy.wait for copy in copies[3 : 3 + parts]])
    for copy in copies[3 + parts :]:
        copy.wait()

    lanes = lane_ids((problems, LANES))
    out = jnp.zeros((problems, LANES), f32)

    def both(f):
        acc = None
        for b in range(w.shape[1] // LANES):
            v = f(False, b)
            acc = v if acc is None else acc + v
        for b in range(share):
            acc = acc + f(True, b)
        return total(acc)

    def hist(ref_x, ref_w, m, is_x, b):
        return (ref_x if is_x else ref_w)[m, :, b * LANES : (b + 1) * LANES]

    def plain(ref_x, ref_w, is_x, b):
        return block_of(ref_x if is_x else ref_w, b)

    for m in range(memory):
        for n in range(m, memory):
            value = both(lambda q, b: hist(hgx, hgw, m, q, b) * hist(hgx, hgw, n, q, b))
            out = jnp.where((lanes == m * memory + n) | (lanes == n * memory + m), value, out)
        value = both(lambda q, b: hist(hgx, hgw, m, q, b) * plain(pgx, pgw, q, b))
        out = jnp.where(lanes == memory * memory + m, value, out)

        def square(q, b):
            h = hist(hsx, hsw, m, q, b)
            return h * h

        out = jnp.where(lanes == memory * (memory + 1) + m, both(square), out)
    for r in range(runs):
        mark = out
        for s in range(per_run):
            mark = jnp.where(lanes == LANES - per_run + s, asked[r * per_run + s].astype(f32), mark)
        send[r * wide + per_run] = mark


def penalty_kernel(first, per_run, *refs):
    if first:
        got, w, center, width, level, send, image, early, rows, marks, marks_int, sem, *sums = refs
    else:
        got, rows, w, center, width, level, send, image, *sums = refs
    slots = send.shape[0]
    runs = slots // per_run
    if first:
        wide = per_run + 1
        early_sum = None
        for r in range(runs):
            side = got[r * wide + per_run]
            early_sum = side if early_sum is None else early_sum + side
            marks_int[r : r + 1, :] = side[:1].astype(jnp.int32)
        early[...] = early_sum
        copy = pltpu.make_async_copy(marks_int, marks, sem)
        copy.start()
        copy.wait()
        for s in range(slots):
            rows[s] = marks[s // per_run, LANES - per_run + s % per_run]
        result = add_rows(got, lambda s: s // per_run * wide + s % per_run, rows, runs, sums)
    else:
        result = add_rows(got, lambda s: s, rows, runs, sums)
    blocks = w.shape[1] // LANES
    for b in range(blocks):
        start = result(b)
        image[:, b * LANES : (b + 1) * LANES] = start
        here = block_of(w, b)
        slack = slack_of(here, block_of(center, b), block_of(width, b))
        rho = rho_of(level, b)
        sums[0][b] = rho * (slack - start) - rho * (here - slack)
    for s in range(slots):
        send[s] = sums[0][rows[s]]


def transpose_kernel(first, *refs):
    if first:
        back, slot, cols, tiles, early, send, acc = refs
    else:
        back, slot, cols, tiles, send, acc = refs
    acc[...] = jnp.zeros_like(acc)

    def one(t):
        high, low = halves(tiles[t])
        term = times(stacked(back[slot[t]]), jnp.concatenate([high, low], axis=0), 0)
        col = cols[t]
        acc[col] = acc[col] + term

    tile_loop(tiles.shape[0], one)
    columns = acc.shape[0]
    for b in range(columns):
        send[:, b * LANES : (b + 1) * LANES] = acc[b]
    if first:
        send[:, columns * LANES :] = early[...]


def residual_kernel(first, own, other, x, linear, diag, cols, slot, tiles, send, resid, *refs):
    columns = x.shape[1] // LANES
    if first:
        early, left = refs
    else:
        (left,) = refs
    for b in range(columns):
        lo, hi = b * LANES, (b + 1) * LANES
        value = -linear[:, lo:hi] - diag[:, lo:hi] * x[:, lo:hi]
        resid[:, lo:hi] = value + (own[:, lo:hi] + other[:, lo:hi])
    if first:
        early[...] = own[:, columns * LANES :] + other[:, columns * LANES :]
    send_products(resid, cols, lambda t: slot[t], tiles, send, left)


def scalar_kernel(
    share, got, rows, start, w, center, width, level, pw, pgw, x, px, pgx, resid, diag, hgx, hgw, qgx, qgw, send, image, *sums
):
    problems = w.shape[0]
    result = add_rows(got, lambda s: s, rows, sums[0].shape[0], sums)
    memory = hgx.shape[0]
    acc = [None] * SCALARS

    def add(i, value):
        acc[i] = value if acc[i] is None else acc[i] + value

    def terms(u, v, p, s, d, hist):
        for m in range(memory):
            h = hist(m)
            add(U_H + m, u * h)
            add(V_H + m, v * h)
        for i, value in ((U_U, u * u), (U_V, u * v), (U_P, u * p), (V_P, v * p), (V_V, v * v), (S_S, s * s), (U_D, u * d), (V_D, v * d)):
            add(i, value)

    for b in range(w.shape[1] // LANES):
        ar = result(b)
        image[:, b * LANES : (b + 1) * LANES] = ar
        here = block_of(w, b)
        slack = slack_of(here, block_of(center, b), block_of(width, b))
        p = block_of(pgw, b)
        u = relax * (block_of(start, b) - slack) - p
        add(C_C, rho_of(level, b) * ar * ar)
        terms(u, relax * ar, p, here - block_of(pw, b), p - block_of(qgw, b), lambda m: hgw[m, :, b * LANES : (b + 1) * LANES])
    for i in range(share):
        b = lax.axis_index("con") * share + i
        r = at(resid, b)
        p = at(pgx, b)
        add(R_R, r * r)
        add(C_C, at(diag, b) * r * r)
        terms(-p, relax * r, p, at(x, b) - at(px, b), p - at(qgx, b), lambda m: hgx[m, :, pl.ds(pl.multiple_of(b * LANES, LANES), LANES)])
    lanes = lane_ids((problems, LANES))
    lane_of = 16 * lax.broadcasted_iota(jnp.int32, (problems, LANES), 0)
    packed = []
    for row in range(2):
        tile = jnp.zeros((problems, LANES), f32)
        for i in range(16):
            if row * 16 + i < SCALARS:
                tile = jnp.where(lanes == lane_of + i, total(acc[row * 16 + i]), tile)
        packed.append(jnp.sum(tile, axis=0, keepdims=True))
    both = jnp.concatenate(packed, axis=0)
    send[...] = both


def update_kernel(last, steps_before, *refs):
    (late, known, order, sigma_level, x, px, pgx, resid, hsx, hgx) = refs[:10]
    (w, pw, pgw, start, image, center, width, hsw, hgw) = refs[10:19]
    refs = refs[19:]
    if steps_before:
        dx, dw = refs[:2]
        refs = refs[2:]
    if last:
        x_out, w_out = refs
    else:
        cols, slot, tiles, x_out, w_out, gx_out, gw_out, dx_out, dw_out, known_out, send, left = refs
    problems = x.shape[0]
    memory = hgx.shape[0]
    shape = (problems, LANES)
    lanes = lane_ids(shape)
    program = lax.broadcasted_iota(jnp.int32, shape, 0)
    chains = [late[i] for i in range(8)]
    for i in range(8, late.shape[0]):
        chains[i % 8] = chains[i % 8] + late[i]
    rows = functools.reduce(lambda p, q: p + q, chains)

    def scalar(i):
        row = jnp.broadcast_to(rows[i // 16 : i // 16 + 1], shape)
        picked = jnp.where(lanes == program * 16 + i % 16, row, 0.0)
        return jnp.broadcast_to(total(picked), shape)

    def given(i):
        return jnp.broadcast_to(known[:, i : i + 1], shape)

    new = [jnp.where(order[steps_before] == m, 1.0, 0.0) for m in range(memory)]
    keep = [1.0 - f for f in new]
    if steps_before:
        old = [jnp.where(order[0] == m, 1.0, 0.0) for m in range(memory)]
    sigma = jnp.zeros(shape, f32)
    for k in range(problems):
        sigma = jnp.where(program == k, 0.2 * (1.0 + sigma_level[k].astype(f32)), sigma)
    norm = scalar(R_R)
    step = norm / (scalar(C_C) + sigma * norm)
    u_h = [scalar(U_H + m) for m in range(memory)]
    v_h = [scalar(V_H + m) for m in range(memory)]
    if steps_before:
        u_d, v_d = scalar(U_D), scalar(V_D)
        u_h = [h * (1.0 - f) + u_d * f for h, f in zip(u_h, old)]
        v_h = [h * (1.0 - f) + v_d * f for h, f in zip(v_h, old)]
    dot = [u + step * v for u, v in zip(u_h, v_h)]
    own = scalar(U_U) + 2.0 * step * scalar(U_V) + step * step * scalar(V_V)
    with_p = scalar(U_P) + step * scalar(V_P)
    gram = [[None] * memory for _ in range(memory)]
    for m in range(memory):
        gram[m][m] = given(m * memory + m) * keep[m] + own * new[m]
        for n in range(m + 1, memory):
            value = given(m * memory + n) * (keep[m] * keep[n]) + dot[n] * new[m] + dot[m] * new[n]
            gram[m][n] = gram[n][m] = value
    at_p, at_s = memory * memory, memory * (memory + 1)
    rhs = []
    for m in range(memory):
        value = given(at_p + m) * keep[m] + with_p * new[m]
        for n in range(memory):
            value = value + gram[m][n] * new[n]
        rhs.append(value)
    s_s = scalar(S_S)
    squares = [given(at_s + m) * keep[m] + s_s * new[m] for m in range(memory)]
    frob = functools.reduce(lambda p, q: p + q, squares + [gram[m][m] for m in range(memory)])
    damp = ridge * frob
    if not last:
        out = jnp.zeros(shape, f32)
        for m in range(memory):
            for n in range(m, memory):
                out = jnp.where((lanes == m * memory + n) | (lanes == n * memory + m), gram[m][n], out)
            out = jnp.where(lanes == at_p + m, rhs[m], out)
            out = jnp.where(lanes == at_s + m, squares[m], out)
        known_out[...] = out
    low = [[None] * memory for _ in range(memory)]
    inverse = []
    for j in range(memory):
        value = gram[j][j] + damp
        for k in range(j):
            value = value - low[j][k] * low[j][k]
        inverse.append(1.0 / jnp.sqrt(value))
        for i in range(j + 1, memory):
            value = gram[i][j]
            for k in range(j):
                value = value - low[i][k] * low[j][k]
            low[i][j] = value * inverse[j]
    half = []
    for i in range(memory):
        value = rhs[i]
        for k in range(i):
            value = value - low[i][k] * half[k]
        half.append(value * inverse[i])
    coef = [None] * memory
    for i in reversed(range(memory)):
        value = half[i]
        for k in range(i + 1, memory):
            value = value - low[k][i] * coef[k]
        coef[i] = value * inverse[i]

    newest = functools.reduce(lambda p, q: p + q, [c * f for c, f in zip(coef, new)])
    left_over = [c * f for c, f in zip(coef, keep)]
    if steps_before:
        older = functools.reduce(lambda p, q: p + q, [c * f for c, f in zip(left_over, old)])
        left_over = [c * (1.0 - f) for c, f in zip(left_over, old)]

    scaled = relax * step
    older = older if steps_before else None
    for b in range(x.shape[1] // LANES):
        g = scaled * block_of(resid, b)
        advance(b, newest, left_over, older, x, px, g, pgx, hsx, hgx, dx if steps_before else None, x_out, None if last else gx_out, None if last else dx_out)
    for b in range(w.shape[1] // LANES):
        slack = slack_of(block_of(w, b), block_of(center, b), block_of(width, b))
        g = relax * (block_of(start, b) + step * block_of(image, b) - slack)
        advance(b, newest, left_over, older, w, pw, g, pgw, hsw, hgw, dw if steps_before else None, w_out, None if last else gw_out, None if last else dw_out)
    if not last:
        send_products(x_out, cols, lambda t: slot[t], tiles, send, left)


def advance(b, newest, left_over, older, state, previous, g, previous_g, hs, hg, kept, out, g_out, d_out):
    lo, hi = b * LANES, (b + 1) * LANES
    here = state[:, lo:hi]
    fresh = (here - previous[:, lo:hi]) + (g - previous_g[:, lo:hi])
    value = here + g - newest * fresh
    for m in range(len(left_over)):
        value = value - left_over[m] * (hs[m, :, lo:hi] + hg[m, :, lo:hi])
    if kept is not None:
        value = value - older * kept[:, lo:hi]
    out[:, lo:hi] = value
    if g_out is not None:
        g_out[:, lo:hi] = g
        d_out[:, lo:hi] = fresh


def call(kernel, name, ins, outs, scratch=()):
    spaces = {"v": pltpu.VMEM, "s": pltpu.SMEM, "h": pltpu.HBM}
    return pl.pallas_call(
        kernel,
        out_shape=[jax.ShapeDtypeStruct(shape, dtype) for shape, dtype, _ in outs],
        in_specs=[pl.BlockSpec(memory_space=spaces[space]) for _, space in ins],
        out_specs=[pl.BlockSpec(memory_space=spaces[space]) for _, _, space in outs],
        scratch_shapes=list(scratch),
        compiler_params=pltpu.CompilerParams(vmem_limit_bytes=24 * 1024 * 1024),
        name=name,
    )(*[array for array, _ in ins])


def per_device(
    tiles,
    row_tile,
    col_tile,
    diag_cost,
    linear_cost,
    bound_center,
    bound_width,
    rho_level,
    sigma_level,
    state_x,
    state_w,
    prev_x,
    prev_w,
    prev_gx,
    prev_gw,
    hist_sx,
    hist_sw,
    hist_gx,
    hist_gw,
    slot_order,
):
    problems, var_cols = state_x.shape
    con_cols = state_w.shape[1]
    tile_size = tiles.shape[-1]
    var_count, con_count = lax.axis_size("var"), lax.axis_size("con")
    col_count = var_cols // tile_size
    run_length = con_cols // tile_size
    blocks = tiles.reshape(-1, tile_size, tile_size)
    count = blocks.shape[0]
    per_run = -(-count // var_count)
    slots = var_count * per_run
    rows_here = row_tile.reshape(-1)
    cols_here = col_tile.reshape(-1)
    diag = diag_cost.reshape(1, -1)
    level = rho_level.reshape(1, -1)

    x_like = ((problems, var_cols), f32, "v")
    w_like = ((problems, con_cols), f32, "v")
    panel = ((slots, problems, tile_size), f32, "v")
    wide_panel = ((slots + var_count, problems, tile_size), f32, "v")
    one_tile = ((problems, tile_size), f32, "v")
    left = pltpu.VMEM((col_count, 2 * problems, 2 * tile_size), bf16)
    sums = [pltpu.VMEM((run_length, problems, tile_size), f32)] * 4
    bounds = [(bound_center, "v"), (bound_width, "v")]
    vs = lambda *arrays: [(a, "v") for a in arrays]
    ss = lambda *arrays: [(a, "s") for a in arrays]

    def exchange(x):
        return lax.all_to_all(x, "var", 0, 0, tiled=True)

    def over_con(x):
        def partner(x, k):
            return lax.ppermute(x, "con", [(i, i ^ k) for i in range(con_count)])

        others = [partner(x, k) for k in range(2, con_count, 2)]
        terms = [x] + others
        while len(terms) > 1:
            terms = [a + b for a, b in zip(terms[::2], terms[1::2])]
        return terms[0], partner(terms[0], 1)

    one_core = [list(range(k, con_count * var_count, 2)) for k in range(2)]
    share = col_count // con_count
    parts = max(d for d in range(1, 4) if count % d == 0)
    far = [state_x, blocks, prev_x, state_w, prev_w, prev_gx, prev_gw, hist_sx, hist_sw, hist_gx, hist_gw]
    x_mine, w_mine = pltpu.VMEM((problems, share * tile_size), f32), pltpu.VMEM((problems, con_cols), f32)
    memory = hist_gx.shape[0]
    hx_mine = pltpu.VMEM((memory, problems, share * tile_size), f32)
    hw_mine = pltpu.VMEM((memory, problems, con_cols), f32)
    sent, slot = call(
        functools.partial(open_kernel, per_run, run_length, share, parts),
        "open",
        [(pltpu.with_memory_space_constraint(a, pltpu.HBM), "h") for a in [row_tile[0], col_tile[0]] + far],
        [wide_panel, ((count,), jnp.int32, "s")],
        [
            pltpu.SMEM((1, count), jnp.int32),
            pltpu.SMEM((1, count), jnp.int32),
            pltpu.VMEM((problems, var_cols), f32),
            pltpu.VMEM(blocks.shape, f32),
            x_mine, w_mine, w_mine, x_mine, w_mine, hx_mine, hw_mine, hx_mine, hw_mine,
            left,
            pltpu.SMEM((var_count,), jnp.int32),
            pltpu.SMEM((slots,), jnp.int32),
            pltpu.SemaphoreType.DMA((3 + parts + 9,)),
        ],
    )
    got = exchange(sent)
    x, w, px, pw, pgx, pgw = state_x, state_w, prev_x, prev_w, prev_gx, prev_gw
    qgx, qgw = pgx, pgw
    kept = []
    known = None
    for step in range(STEPS):
        first, last = step == 0, step == STEPS - 1
        if first:
            sent, start, early, rows = call(
                functools.partial(penalty_kernel, True, per_run),
                "penalty_first",
                vs(got, w, bound_center, bound_width, level),
                [panel, w_like, one_tile, ((slots,), jnp.int32, "s")],
                [pltpu.SMEM((var_count, tile_size), jnp.int32), pltpu.VMEM((var_count, tile_size), jnp.int32), pltpu.SemaphoreType.DMA(())]
                + sums,
            )
        else:
            sent, start = call(
                functools.partial(penalty_kernel, False, per_run),
                "penalty",
                vs(got) + ss(rows) + vs(w, bound_center, bound_width, level),
                [panel, w_like],
                sums,
            )
        back = exchange(sent)
        width = var_cols + (tile_size if first else 0)
        (sent,) = call(
            functools.partial(transpose_kernel, first),
            "transpose",
            vs(back) + ss(slot, cols_here) + vs(blocks) + (vs(early) if first else []),
            [((problems, width), f32, "v")],
            [pltpu.VMEM((col_count, problems, tile_size), f32)],
        )
        own, other = over_con(sent)
        outs = call(
            functools.partial(residual_kernel, first),
            "residual",
            vs(own, other, x, linear_cost, diag) + ss(cols_here, slot) + vs(blocks),
            [panel, x_like] + ([one_tile] if first else []),
            [left],
        )
        sent, resid = outs[:2]
        if first:
            known = outs[2]
        got = exchange(sent)

        sent, image = call(
            functools.partial(scalar_kernel, share),
            "scalars",
            vs(got)
            + ss(rows)
            + vs(start, w, bound_center, bound_width, level, pw, pgw, x, px, pgx, resid, diag, hist_gx, hist_gw, qgx, qgw),
            [((2, LANES), f32, "v"), w_like],
            sums,
        )
        pair = sent + lax.ppermute(sent, "var", [(i, i ^ 1) for i in range(var_count)])
        copies = jnp.broadcast_to(pair[None], (con_count * var_count // 2, 2, LANES))
        late = lax.all_to_all(copies, ("con", "var"), 0, 0, tiled=True, axis_index_groups=one_core)
        outs = call(
            functools.partial(update_kernel, last, step),
            "update",
            vs(late, known)
            + ss(slot_order, sigma_level)
            + vs(x, px, pgx, resid, hist_sx, hist_gx, w, pw, pgw, start, image, bound_center, bound_width, hist_sw, hist_gw)
            + vs(*kept)
            + ([] if last else ss(cols_here, slot) + vs(blocks)),
            [x_like, w_like] + ([] if last else [x_like, w_like, x_like, w_like, one_tile, panel]),
            [] if last else [left],
        )
        if last:
            return outs[0], outs[1]
        qgx, qgw = pgx, pgw
        px, pw = x, w
        x, w, pgx, pgw, dx, dw, known, sent = outs
        kept = [dx, dw]
        got = exchange(sent)


def solution(mesh):
    in_specs = (
        P("con", "var", None, None, None),
        P("con", "var", None),
        P("con", "var", None),
        P("var"),
        P(None, "var"),
        P(None, ("con", "var")),
        P(None, ("con", "var")),
        P(("con", "var")),
        P(),
        P(None, "var"),
        P(None, ("con", "var")),
        P(None, "var"),
        P(None, ("con", "var")),
        P(None, "var"),
        P(None, ("con", "var")),
        P(None, None, "var"),
        P(None, None, ("con", "var")),
        P(None, None, "var"),
        P(None, None, ("con", "var")),
        P(),
    )
    out_specs = (P(None, "var"), P(None, ("con", "var")))
    return jax.shard_map(
        per_device, mesh=mesh, in_specs=in_specs, out_specs=out_specs, check_vma=False
    )
```

```python
import functools

import jax
import jax.numpy as jnp
from jax import lax
from jax.experimental import pallas as pl
from jax.experimental.pallas import tpu as pltpu
from jax.sharding import PartitionSpec as P

STEPS = 2
LANES = 128
UNROLL = 72

relax = 1.6
ridge = 0.01

f32 = jnp.float32
bf16 = jnp.bfloat16

U_H, V_H, U_U, U_V, U_P, V_P, V_V, S_S, R_R, C_C, U_D, V_D, SCALARS = 0, 8, 16, 17, 18, 19, 20, 21, 22, 23, 24, 25, 26


def halves(value):
    high = value.astype(bf16)
    return high, (value - high.astype(f32)).astype(bf16)


def stacked(piece):
    high, low = halves(piece)
    return jnp.concatenate(
        [
            jnp.concatenate([high, high], axis=1),
            jnp.concatenate([low, jnp.zeros_like(low)], axis=1),
        ],
        axis=0,
    )


def times(left, right, contract):
    both = lax.dot_general(left, right, (((1,), (contract,)), ((), ())), preferred_element_type=f32)
    half = both.shape[0] // 2
    return both[:half] + both[half:]


def at(ref, block):
    return ref[:, pl.ds(pl.multiple_of(block * LANES, LANES), LANES)]


def tile_loop(count, body):
    step = max(d for d in range(1, UNROLL + 1) if count % d == 0)

    if step == count:
        for j in range(count):
            body(j)
        return

    def some(i, _):
        for j in range(step):
            body(i * step + j)
        return 0

    lax.fori_loop(0, count // step, some, 0)


def lane_ids(shape):
    return lax.broadcasted_iota(jnp.int32, shape, len(shape) - 1)


def send_products(x_ref, cols, where, tiles, send, left, waits=(None,)):
    for block in range(x_ref.shape[1] // LANES):
        left[block] = stacked(x_ref[:, block * LANES : (block + 1) * LANES])
    send[...] = jnp.zeros_like(send)

    def one(t):
        high, low = halves(tiles[t])
        send[where(t)] = times(left[cols[t]], jnp.concatenate([high, low], axis=1), 1)

    size = tiles.shape[0] // len(waits)
    for i, wait in enumerate(waits):
        if wait is not None:
            wait()
        tile_loop(size, lambda t, i=i: one(t + i * size))


def add_rows(got, index, rows, runs, sums):
    for ref in sums:
        ref[...] = jnp.zeros_like(ref)
    for s in range(rows.shape[0]):
        ref = sums[s % len(sums)]
        row = rows[s]
        ref[row] = ref[row] + got[index(s)]
    return lambda b: functools.reduce(lambda p, q: p + q, [ref[b] for ref in sums])


def block_of(ref, b):
    return ref[:, b * LANES : (b + 1) * LANES]


def rho_of(level_ref, b):
    return 0.4 * (1.0 + block_of(level_ref, b).astype(f32))


def slack_of(w, center, width):
    return jnp.minimum(jnp.maximum(w, center - width), center + width)


def total(value):
    return jnp.sum(value, axis=1, keepdims=True)


def open_kernel(per_run, run_length, share, parts, *refs):
    (hbm_rows, hbm_cols, hbm_x, hbm_tiles, *far), (send, slot), refs = refs[:13], refs[13:15], refs[15:]
    rows_buf, cols_buf, x, tiles, px, w, pw, pgx, pgw, hsx, hsw, hgx, hgw, left, count, asked, spot, sem = refs
    memory = hgx.shape[0]
    problems = x.shape[0]
    runs = send.shape[0] // (per_run + 1)
    wide = per_run + 1
    first = lax.axis_index("con") * share
    mine = pl.ds(pl.multiple_of(first * LANES, LANES), share * LANES)
    far_px, far_w, far_pw, far_pgx, far_pgw, far_hsx, far_hsw, far_hgx, far_hgw = far
    size = tiles.shape[0] // parts
    moves = [(hbm_rows, rows_buf), (hbm_cols, cols_buf), (hbm_x, x)]
    moves += [(hbm_tiles.at[pl.ds(i * size, size)], tiles.at[pl.ds(i * size, size)]) for i in range(parts)]
    moves += [(far_w, w), (far_pw, pw), (far_pgw, pgw), (far_hsw, hsw), (far_hgw, hgw)]
    moves += [(far_px.at[:, mine], px), (far_pgx.at[:, mine], pgx), (far_hsx.at[:, :, mine], hsx), (far_hgx.at[:, :, mine], hgx)]
    copies = [pltpu.make_async_copy(a, b, sem.at[i]) for i, (a, b) in enumerate(moves)]
    for copy in copies:
        copy.start()
    rows, cols = rows_buf.at[0], cols_buf.at[0]

    for i in range(runs):
        count[i] = 0
    for i in range(runs * per_run):
        asked[i] = 0
    copies[0].wait()
    copies[1].wait()
    for t in range(tiles.shape[0]):
        row = rows[t]
        owner = row >> (run_length.bit_length() - 1)
        rank = count[owner]
        count[owner] = rank + 1
        place = owner * per_run + rank
        slot[t] = place
        spot[t] = place + owner
        asked[place] = row & (run_length - 1)

    def where(t):
        return spot[t]

    copies[2].wait()
    send_products(x, cols, where, tiles, send, left, [copy.wait for copy in copies[3 : 3 + parts]])
    for copy in copies[3 + parts :]:
        copy.wait()

    lanes = lane_ids((problems, LANES))
    out = jnp.zeros((problems, LANES), f32)

    def both(f):
        acc = None
        for b in range(w.shape[1] // LANES):
            v = f(False, b)
            acc = v if acc is None else acc + v
        for b in range(share):
            acc = acc + f(True, b)
        return total(acc)

    def hist(ref_x, ref_w, m, is_x, b):
        return (ref_x if is_x else ref_w)[m, :, b * LANES : (b + 1) * LANES]

    def plain(ref_x, ref_w, is_x, b):
        return block_of(ref_x if is_x else ref_w, b)

    for m in range(memory):
        for n in range(m, memory):
            value = both(lambda q, b: hist(hgx, hgw, m, q, b) * hist(hgx, hgw, n, q, b))
            out = jnp.where((lanes == m * memory + n) | (lanes == n * memory + m), value, out)
        value = both(lambda q, b: hist(hgx, hgw, m, q, b) * plain(pgx, pgw, q, b))
        out = jnp.where(lanes == memory * memory + m, value, out)

        def square(q, b):
            h = hist(hsx, hsw, m, q, b)
            return h * h

        out = jnp.where(lanes == memory * (memory + 1) + m, both(square), out)
    index = entry_ids(runs * per_run, problems) - lax.axis_index("var") * per_run
    for r in range(runs):
        mark = out
        for i in range(per_run):
            mark = jnp.where(index == i, asked[r * per_run + i].astype(f32), mark)
        send[r * wide + per_run] = mark


def entry_ids(entries, problems):
    shape = (problems, LANES)
    base = LANES - -(-entries // problems)
    return (lane_ids(shape) - base) * problems + lax.broadcasted_iota(jnp.int32, shape, 0)


def penalty_kernel(first, per_run, *refs):
    if first:
        got, w, center, width, level, send, image, early, rows, marks, marks_int, sem, *sums = refs
    else:
        got, rows, w, center, width, level, send, image, *sums = refs
    slots = send.shape[0]
    runs = slots // per_run
    if first:
        wide = per_run + 1
        early_sum = functools.reduce(lambda p, q: p + q, [got[r * wide + per_run] for r in range(runs)])
        early[...] = early_sum
        marks_int[...] = early_sum.astype(jnp.int32)
        copy = pltpu.make_async_copy(marks_int, marks, sem)
        copy.start()
        copy.wait()
        problems = w.shape[0]
        base = LANES - -(-slots // problems)
        for s in range(slots):
            rows[s] = marks[s % problems, base + s // problems]
        result = add_rows(got, lambda s: s // per_run * wide + s % per_run, rows, runs, sums)
    else:
        result = add_rows(got, lambda s: s, rows, runs, sums)
    blocks = w.shape[1] // LANES
    for b in range(blocks):
        start = result(b)
        image[:, b * LANES : (b + 1) * LANES] = start
        here = block_of(w, b)
        slack = slack_of(here, block_of(center, b), block_of(width, b))
        rho = rho_of(level, b)
        sums[0][b] = rho * (slack - start) - rho * (here - slack)
    for s in range(slots):
        send[s] = sums[0][rows[s]]


def transpose_kernel(first, *refs):
    if first:
        back, slot, cols, tiles, early, send, acc = refs
    else:
        back, slot, cols, tiles, send, acc = refs
    acc[...] = jnp.zeros_like(acc)

    def one(t):
        high, low = halves(tiles[t])
        term = times(stacked(back[slot[t]]), jnp.concatenate([high, low], axis=0), 0)
        col = cols[t]
        acc[col] = acc[col] + term

    tile_loop(tiles.shape[0], one)
    columns = acc.shape[0]
    for b in range(columns):
        send[:, b * LANES : (b + 1) * LANES] = acc[b]
    if first:
        send[:, columns * LANES :] = early[...]


def residual_kernel(first, own, other, x, linear, diag, cols, slot, tiles, send, resid, *refs):
    columns = x.shape[1] // LANES
    if first:
        early, left = refs
    else:
        (left,) = refs
    for b in range(columns):
        lo, hi = b * LANES, (b + 1) * LANES
        value = -linear[:, lo:hi] - diag[:, lo:hi] * x[:, lo:hi]
        resid[:, lo:hi] = value + (own[:, lo:hi] + other[:, lo:hi])
    if first:
        early[...] = own[:, columns * LANES :] + other[:, columns * LANES :]
    send_products(resid, cols, lambda t: slot[t], tiles, send, left)


def scalar_kernel(
    share, got, rows, start, w, center, width, level, pw, pgw, x, px, pgx, resid, diag, hgx, hgw, qgx, qgw, send, image, *sums
):
    problems = w.shape[0]
    result = add_rows(got, lambda s: s, rows, sums[0].shape[0], sums)
    memory = hgx.shape[0]
    acc = [None] * SCALARS

    def add(i, value):
        acc[i] = value if acc[i] is None else acc[i] + value

    def terms(u, v, p, s, d, hist):
        for m in range(memory):
            h = hist(m)
            add(U_H + m, u * h)
            add(V_H + m, v * h)
        for i, value in ((U_U, u * u), (U_V, u * v), (U_P, u * p), (V_P, v * p), (V_V, v * v), (S_S, s * s), (U_D, u * d), (V_D, v * d)):
            add(i, value)

    for b in range(w.shape[1] // LANES):
        ar = result(b)
        image[:, b * LANES : (b + 1) * LANES] = ar
        here = block_of(w, b)
        slack = slack_of(here, block_of(center, b), block_of(width, b))
        p = block_of(pgw, b)
        u = relax * (block_of(start, b) - slack) - p
        add(C_C, rho_of(level, b) * ar * ar)
        terms(u, relax * ar, p, here - block_of(pw, b), p - block_of(qgw, b), lambda m: hgw[m, :, b * LANES : (b + 1) * LANES])
    for i in range(share):
        b = lax.axis_index("con") * share + i
        r = at(resid, b)
        p = at(pgx, b)
        add(R_R, r * r)
        add(C_C, at(diag, b) * r * r)
        terms(-p, relax * r, p, at(x, b) - at(px, b), p - at(qgx, b), lambda m: hgx[m, :, pl.ds(pl.multiple_of(b * LANES, LANES), LANES)])
    lanes = lane_ids((problems, LANES))
    lane_of = (LANES - 16 * lax.broadcasted_iota(jnp.int32, (problems, LANES), 0)) & (LANES - 1)
    packed = []
    for row in range(2):
        tile = jnp.zeros((problems, LANES), f32)
        for i in range(16):
            if row * 16 + i < SCALARS:
                tile = jnp.where(lanes == lane_of + i, total(acc[row * 16 + i]), tile)
        packed.append(jnp.sum(tile, axis=0, keepdims=True))
    both = jnp.concatenate(packed, axis=0)
    send[...] = both


def update_kernel(last, steps_before, *refs):
    (late, known, order, sigma_level, x, px, pgx, resid, hsx, hgx) = refs[:10]
    (w, pw, pgw, start, image, center, width, hsw, hgw) = refs[10:19]
    refs = refs[19:]
    if steps_before:
        dx, dw = refs[:2]
        refs = refs[2:]
    if last:
        x_out, w_out = refs
    else:
        cols, slot, tiles, x_out, w_out, gx_out, gw_out, dx_out, dw_out, known_out, send, left = refs
    problems = x.shape[0]
    memory = hgx.shape[0]
    shape = (problems, LANES)
    lanes = lane_ids(shape)
    program = lax.broadcasted_iota(jnp.int32, shape, 0)
    chains = [late[i] for i in range(8)]
    for i in range(8, late.shape[0]):
        chains[i % 8] = chains[i % 8] + late[i]
    rows = functools.reduce(lambda p, q: p + q, chains)

    aligned = [
        pltpu.roll(jnp.broadcast_to(rows[i : i + 1], shape), 0, 1, stride=16, stride_axis=0) for i in range(2)
    ]

    def scalar(i):
        return jnp.broadcast_to(aligned[i // 16][:, i % 16 : i % 16 + 1], shape)

    def given(i):
        return jnp.broadcast_to(known[:, i : i + 1], shape)

    new = [jnp.where(order[steps_before] == m, 1.0, 0.0) for m in range(memory)]
    keep = [1.0 - f for f in new]
    if steps_before:
        old = [jnp.where(order[0] == m, 1.0, 0.0) for m in range(memory)]
    sigma = jnp.zeros(shape, f32)
    for k in range(problems):
        sigma = jnp.where(program == k, 0.2 * (1.0 + sigma_level[k].astype(f32)), sigma)
    norm = scalar(R_R)
    step = norm / (scalar(C_C) + sigma * norm)
    u_h = [scalar(U_H + m) for m in range(memory)]
    v_h = [scalar(V_H + m) for m in range(memory)]
    if steps_before:
        u_d, v_d = scalar(U_D), scalar(V_D)
        u_h = [h * (1.0 - f) + u_d * f for h, f in zip(u_h, old)]
        v_h = [h * (1.0 - f) + v_d * f for h, f in zip(v_h, old)]
    dot = [u + step * v for u, v in zip(u_h, v_h)]
    own = scalar(U_U) + 2.0 * step * scalar(U_V) + step * step * scalar(V_V)
    with_p = scalar(U_P) + step * scalar(V_P)
    gram = [[None] * memory for _ in range(memory)]
    for m in range(memory):
        gram[m][m] = given(m * memory + m) * keep[m] + own * new[m]
        for n in range(m + 1, memory):
            value = given(m * memory + n) * (keep[m] * keep[n]) + dot[n] * new[m] + dot[m] * new[n]
            gram[m][n] = gram[n][m] = value
    at_p, at_s = memory * memory, memory * (memory + 1)
    rhs = []
    for m in range(memory):
        value = given(at_p + m) * keep[m] + with_p * new[m]
        for n in range(memory):
            value = value + gram[m][n] * new[n]
        rhs.append(value)
    s_s = scalar(S_S)
    squares = [given(at_s + m) * keep[m] + s_s * new[m] for m in range(memory)]
    frob = functools.reduce(lambda p, q: p + q, squares + [gram[m][m] for m in range(memory)])
    damp = ridge * frob
    if not last:
        out = jnp.zeros(shape, f32)
        for m in range(memory):
            for n in range(m, memory):
                out = jnp.where((lanes == m * memory + n) | (lanes == n * memory + m), gram[m][n], out)
            out = jnp.where(lanes == at_p + m, rhs[m], out)
            out = jnp.where(lanes == at_s + m, squares[m], out)
        known_out[...] = out
    low = [[None] * memory for _ in range(memory)]
    inverse = []
    for j in range(memory):
        value = gram[j][j] + damp
        for k in range(j):
            value = value - low[j][k] * low[j][k]
        inverse.append(1.0 / jnp.sqrt(value))
        for i in range(j + 1, memory):
            value = gram[i][j]
            for k in range(j):
                value = value - low[i][k] * low[j][k]
            low[i][j] = value * inverse[j]
    half = []
    for i in range(memory):
        value = rhs[i]
        for k in range(i):
            value = value - low[i][k] * half[k]
        half.append(value * inverse[i])
    coef = [None] * memory
    for i in reversed(range(memory)):
        value = half[i]
        for k in range(i + 1, memory):
            value = value - low[k][i] * coef[k]
        coef[i] = value * inverse[i]

    newest = functools.reduce(lambda p, q: p + q, [c * f for c, f in zip(coef, new)])
    left_over = [c * f for c, f in zip(coef, keep)]
    if steps_before:
        older = functools.reduce(lambda p, q: p + q, [c * f for c, f in zip(left_over, old)])
        left_over = [c * (1.0 - f) for c, f in zip(left_over, old)]

    scaled = relax * step
    older = older if steps_before else None
    for b in range(x.shape[1] // LANES):
        g = scaled * block_of(resid, b)
        advance(b, newest, left_over, older, x, px, g, pgx, hsx, hgx, dx if steps_before else None, x_out, None if last else gx_out, None if last else dx_out)
    for b in range(w.shape[1] // LANES):
        slack = slack_of(block_of(w, b), block_of(center, b), block_of(width, b))
        g = relax * (block_of(start, b) + step * block_of(image, b) - slack)
        advance(b, newest, left_over, older, w, pw, g, pgw, hsw, hgw, dw if steps_before else None, w_out, None if last else gw_out, None if last else dw_out)
    if not last:
        send_products(x_out, cols, lambda t: slot[t], tiles, send, left)


def advance(b, newest, left_over, older, state, previous, g, previous_g, hs, hg, kept, out, g_out, d_out):
    lo, hi = b * LANES, (b + 1) * LANES
    here = state[:, lo:hi]
    fresh = (here - previous[:, lo:hi]) + (g - previous_g[:, lo:hi])
    value = here + g - newest * fresh
    for m in range(len(left_over)):
        value = value - left_over[m] * (hs[m, :, lo:hi] + hg[m, :, lo:hi])
    if kept is not None:
        value = value - older * kept[:, lo:hi]
    out[:, lo:hi] = value
    if g_out is not None:
        g_out[:, lo:hi] = g
        d_out[:, lo:hi] = fresh


def call(kernel, name, ins, outs, scratch=()):
    spaces = {"v": pltpu.VMEM, "s": pltpu.SMEM, "h": pltpu.HBM}
    return pl.pallas_call(
        kernel,
        out_shape=[jax.ShapeDtypeStruct(shape, dtype) for shape, dtype, _ in outs],
        in_specs=[pl.BlockSpec(memory_space=spaces[space]) for _, space in ins],
        out_specs=[pl.BlockSpec(memory_space=spaces[space]) for _, _, space in outs],
        scratch_shapes=list(scratch),
        compiler_params=pltpu.CompilerParams(vmem_limit_bytes=24 * 1024 * 1024),
        name=name,
    )(*[array for array, _ in ins])


def per_device(
    tiles,
    row_tile,
    col_tile,
    diag_cost,
    linear_cost,
    bound_center,
    bound_width,
    rho_level,
    sigma_level,
    state_x,
    state_w,
    prev_x,
    prev_w,
    prev_gx,
    prev_gw,
    hist_sx,
    hist_sw,
    hist_gx,
    hist_gw,
    slot_order,
):
    problems, var_cols = state_x.shape
    con_cols = state_w.shape[1]
    tile_size = tiles.shape[-1]
    var_count, con_count = lax.axis_size("var"), lax.axis_size("con")
    col_count = var_cols // tile_size
    run_length = con_cols // tile_size
    blocks = tiles.reshape(-1, tile_size, tile_size)
    count = blocks.shape[0]
    per_run = -(-count // var_count)
    slots = var_count * per_run
    rows_here = row_tile.reshape(-1)
    cols_here = col_tile.reshape(-1)
    diag = diag_cost.reshape(1, -1)
    level = rho_level.reshape(1, -1)

    x_like = ((problems, var_cols), f32, "v")
    w_like = ((problems, con_cols), f32, "v")
    panel = ((slots, problems, tile_size), f32, "v")
    wide_panel = ((slots + var_count, problems, tile_size), f32, "v")
    one_tile = ((problems, tile_size), f32, "v")
    left = pltpu.VMEM((col_count, 2 * problems, 2 * tile_size), bf16)
    sums = [pltpu.VMEM((run_length, problems, tile_size), f32)] * 4
    bounds = [(bound_center, "v"), (bound_width, "v")]
    vs = lambda *arrays: [(a, "v") for a in arrays]
    ss = lambda *arrays: [(a, "s") for a in arrays]

    def exchange(x):
        return lax.all_to_all(x, "var", 0, 0, tiled=True)

    def over_con(x):
        def partner(x, k):
            return lax.ppermute(x, "con", [(i, i ^ k) for i in range(con_count)])

        others = [partner(x, k) for k in range(2, con_count, 2)]
        terms = [x] + others
        while len(terms) > 1:
            terms = [a + b for a, b in zip(terms[::2], terms[1::2])]
        return terms[0], partner(terms[0], 1)

    one_core = [list(range(k, con_count * var_count, 2)) for k in range(2)]
    share = col_count // con_count
    parts = max(d for d in range(1, 4) if count % d == 0)
    far = [state_x, blocks, prev_x, state_w, prev_w, prev_gx, prev_gw, hist_sx, hist_sw, hist_gx, hist_gw]
    x_mine, w_mine = pltpu.VMEM((problems, share * tile_size), f32), pltpu.VMEM((problems, con_cols), f32)
    memory = hist_gx.shape[0]
    hx_mine = pltpu.VMEM((memory, problems, share * tile_size), f32)
    hw_mine = pltpu.VMEM((memory, problems, con_cols), f32)
    sent, slot = call(
        functools.partial(open_kernel, per_run, run_length, share, parts),
        "open",
        [(pltpu.with_memory_space_constraint(a, pltpu.HBM), "h") for a in [row_tile[0], col_tile[0]] + far],
        [wide_panel, ((count,), jnp.int32, "s")],
        [
            pltpu.SMEM((1, count), jnp.int32),
            pltpu.SMEM((1, count), jnp.int32),
            pltpu.VMEM((problems, var_cols), f32),
            pltpu.VMEM(blocks.shape, f32),
            x_mine, w_mine, w_mine, x_mine, w_mine, hx_mine, hw_mine, hx_mine, hw_mine,
            left,
            pltpu.SMEM((var_count,), jnp.int32),
            pltpu.SMEM((slots,), jnp.int32),
            pltpu.SMEM((count,), jnp.int32),
            pltpu.SemaphoreType.DMA((3 + parts + 9,)),
        ],
    )
    got = exchange(sent)
    x, w, px, pw, pgx, pgw = state_x, state_w, prev_x, prev_w, prev_gx, prev_gw
    qgx, qgw = pgx, pgw
    kept = []
    known = None
    for step in range(STEPS):
        first, last = step == 0, step == STEPS - 1
        if first:
            sent, start, early, rows = call(
                functools.partial(penalty_kernel, True, per_run),
                "penalty_first",
                vs(got, w, bound_center, bound_width, level),
                [panel, w_like, one_tile, ((slots,), jnp.int32, "s")],
                [pltpu.SMEM((problems, tile_size), jnp.int32), pltpu.VMEM((problems, tile_size), jnp.int32), pltpu.SemaphoreType.DMA(())]
                + sums,
            )
        else:
            sent, start = call(
                functools.partial(penalty_kernel, False, per_run),
                "penalty",
                vs(got) + ss(rows) + vs(w, bound_center, bound_width, level),
                [panel, w_like],
                sums,
            )
        back = exchange(sent)
        width = var_cols + (tile_size if first else 0)
        (sent,) = call(
            functools.partial(transpose_kernel, first),
            "transpose",
            vs(back) + ss(slot, cols_here) + vs(blocks) + (vs(early) if first else []),
            [((problems, width), f32, "v")],
            [pltpu.VMEM((col_count, problems, tile_size), f32)],
        )
        own, other = over_con(sent)
        outs = call(
            functools.partial(residual_kernel, first),
            "residual",
            vs(own, other, x, linear_cost, diag) + ss(cols_here, slot) + vs(blocks),
            [panel, x_like] + ([one_tile] if first else []),
            [left],
        )
        sent, resid = outs[:2]
        if first:
            known = outs[2]
        got = exchange(sent)

        sent, image = call(
            functools.partial(scalar_kernel, share),
            "scalars",
            vs(got)
            + ss(rows)
            + vs(start, w, bound_center, bound_width, level, pw, pgw, x, px, pgx, resid, diag, hist_gx, hist_gw, qgx, qgw),
            [((2, LANES), f32, "v"), w_like],
            sums,
        )
        pair = sent + lax.ppermute(sent, "var", [(i, i ^ 1) for i in range(var_count)])
        copies = jnp.broadcast_to(pair[None], (con_count * var_count // 2, 2, LANES))
        late = lax.all_to_all(copies, ("con", "var"), 0, 0, tiled=True, axis_index_groups=one_core)
        outs = call(
            functools.partial(update_kernel, last, step),
            "update",
            vs(late, known)
            + ss(slot_order, sigma_level)
            + vs(x, px, pgx, resid, hist_sx, hist_gx, w, pw, pgw, start, image, bound_center, bound_width, hist_sw, hist_gw)
            + vs(*kept)
            + ([] if last else ss(cols_here, slot) + vs(blocks)),
            [x_like, w_like] + ([] if last else [x_like, w_like, x_like, w_like, one_tile, panel]),
            [] if last else [left],
        )
        if last:
            return outs[0], outs[1]
        qgx, qgw = pgx, pgw
        px, pw = x, w
        x, w, pgx, pgw, dx, dw, known, sent = outs
        kept = [dx, dw]
        got = exchange(sent)


def solution(mesh):
    in_specs = (
        P("con", "var", None, None, None),
        P("con", "var", None),
        P("con", "var", None),
        P("var"),
        P(None, "var"),
        P(None, ("con", "var")),
        P(None, ("con", "var")),
        P(("con", "var")),
        P(),
        P(None, "var"),
        P(None, ("con", "var")),
        P(None, "var"),
        P(None, ("con", "var")),
        P(None, "var"),
        P(None, ("con", "var")),
        P(None, None, "var"),
        P(None, None, ("con", "var")),
        P(None, None, "var"),
        P(None, None, ("con", "var")),
        P(),
    )
    out_specs = (P(None, "var"), P(None, ("con", "var")))
    return jax.shard_map(
        per_device, mesh=mesh, in_specs=in_specs, out_specs=out_specs, check_vma=False
    )
```

```python
import functools

import jax
import jax.numpy as jnp
from jax import lax
from jax.experimental import pallas as pl
from jax.experimental.pallas import tpu as pltpu
from jax.sharding import PartitionSpec as P

STEPS = 2
LANES = 128
UNROLL = 72

relax = 1.6
ridge = 0.01

f32 = jnp.float32
bf16 = jnp.bfloat16

U_H, V_H, U_U, U_V, U_P, V_P, V_V, S_S, R_R, C_C, U_D, V_D, SCALARS = 0, 8, 16, 17, 18, 19, 20, 21, 22, 23, 24, 25, 26


def halves(value):
    high = value.astype(bf16)
    return high, (value - high.astype(f32)).astype(bf16)


def stacked(piece):
    high, low = halves(piece)
    return jnp.concatenate(
        [
            jnp.concatenate([high, high], axis=1),
            jnp.concatenate([low, jnp.zeros_like(low)], axis=1),
        ],
        axis=0,
    )


def times(left, right, contract):
    both = lax.dot_general(left, right, (((1,), (contract,)), ((), ())), preferred_element_type=f32)
    half = both.shape[0] // 2
    return both[:half] + both[half:]


def at(ref, block):
    return ref[:, pl.ds(pl.multiple_of(block * LANES, LANES), LANES)]


def tile_loop(count, body):
    step = max(d for d in range(1, UNROLL + 1) if count % d == 0)

    if step == count:
        for j in range(count):
            body(j)
        return

    def some(i, _):
        for j in range(step):
            body(i * step + j)
        return 0

    lax.fori_loop(0, count // step, some, 0)


def lane_ids(shape):
    return lax.broadcasted_iota(jnp.int32, shape, len(shape) - 1)


def send_products(x_ref, cols, where, tiles, send, left, waits=(None,), flipped=True):
    for block in range(x_ref.shape[1] // LANES):
        left[block] = stacked(x_ref[:, block * LANES : (block + 1) * LANES])
    send[...] = jnp.zeros_like(send)

    def one(t):
        axis = 0 if flipped else 1
        send[where(t)] = times(left[cols[t]], jnp.concatenate(halves(tiles[t]), axis=axis), axis)

    size = tiles.shape[0] // len(waits)
    for i, wait in enumerate(waits):
        if wait is not None:
            wait()
        tile_loop(size, lambda t, i=i: one(t + i * size))


def add_rows(got, index, rows, runs, sums):
    for ref in sums:
        ref[...] = jnp.zeros_like(ref)
    for s in range(rows.shape[0]):
        ref = sums[s % len(sums)]
        row = rows[s]
        ref[row] = ref[row] + got[index(s)]
    return lambda b: functools.reduce(lambda p, q: p + q, [ref[b] for ref in sums])


def block_of(ref, b):
    return ref[:, b * LANES : (b + 1) * LANES]


def rho_of(level_ref, b):
    return 0.4 * (1.0 + block_of(level_ref, b).astype(f32))


def slack_of(w, center, width):
    return jnp.minimum(jnp.maximum(w, center - width), center + width)


def total(value):
    return jnp.sum(value, axis=1, keepdims=True)


def open_kernel(per_run, run_length, share, parts, *refs):
    (hbm_rows, hbm_cols, hbm_x, hbm_tiles, *far), (send, slot), refs = refs[:13], refs[13:15], refs[15:]
    rows_buf, cols_buf, x, tiles, px, w, pw, pgx, pgw, hsx, hsw, hgx, hgw, left, count, asked, spot, sem = refs
    memory = hgx.shape[0]
    problems = x.shape[0]
    runs = send.shape[0] // (per_run + 1)
    wide = per_run + 1
    first = lax.axis_index("con") * share
    mine = pl.ds(pl.multiple_of(first * LANES, LANES), share * LANES)
    far_px, far_w, far_pw, far_pgx, far_pgw, far_hsx, far_hsw, far_hgx, far_hgw = far
    size = tiles.shape[0] // parts
    moves = [(hbm_rows, rows_buf), (hbm_cols, cols_buf), (hbm_x, x)]
    moves += [(hbm_tiles.at[pl.ds(i * size, size)], tiles.at[pl.ds(i * size, size)]) for i in range(parts)]
    moves += [(far_w, w), (far_pw, pw), (far_pgw, pgw), (far_hsw, hsw), (far_hgw, hgw)]
    moves += [(far_px.at[:, mine], px), (far_pgx.at[:, mine], pgx), (far_hsx.at[:, :, mine], hsx), (far_hgx.at[:, :, mine], hgx)]
    copies = [pltpu.make_async_copy(a, b, sem.at[i]) for i, (a, b) in enumerate(moves)]
    for copy in copies:
        copy.start()
    rows, cols = rows_buf.at[0], cols_buf.at[0]

    for i in range(runs):
        count[i] = 0
    for i in range(runs * per_run):
        asked[i] = 0
    copies[0].wait()
    copies[1].wait()
    for t in range(tiles.shape[0]):
        row = rows[t]
        owner = row >> (run_length.bit_length() - 1)
        rank = count[owner]
        count[owner] = rank + 1
        place = owner * per_run + rank
        slot[t] = place
        spot[t] = place + owner
        asked[place] = row & (run_length - 1)

    def where(t):
        return spot[t]

    copies[2].wait()
    send_products(x, cols, where, tiles, send, left, [copy.wait for copy in copies[3 : 3 + parts]], flipped=False)
    for copy in copies[3 + parts :]:
        copy.wait()

    lanes = lane_ids((problems, LANES))
    out = jnp.zeros((problems, LANES), f32)

    def both(f):
        acc = None
        for b in range(w.shape[1] // LANES):
            v = f(False, b)
            acc = v if acc is None else acc + v
        for b in range(share):
            acc = acc + f(True, b)
        return total(acc)

    def hist(ref_x, ref_w, m, is_x, b):
        return (ref_x if is_x else ref_w)[m, :, b * LANES : (b + 1) * LANES]

    def plain(ref_x, ref_w, is_x, b):
        return block_of(ref_x if is_x else ref_w, b)

    for m in range(memory):
        for n in range(m, memory):
            value = both(lambda q, b: hist(hgx, hgw, m, q, b) * hist(hgx, hgw, n, q, b))
            out = jnp.where((lanes == m * memory + n) | (lanes == n * memory + m), value, out)
        value = both(lambda q, b: hist(hgx, hgw, m, q, b) * plain(pgx, pgw, q, b))
        out = jnp.where(lanes == memory * memory + m, value, out)

        def square(q, b):
            h = hist(hsx, hsw, m, q, b)
            return h * h

        out = jnp.where(lanes == memory * (memory + 1) + m, both(square), out)
    index = entry_ids(runs * per_run, problems) - lax.axis_index("var") * per_run
    for r in range(runs):
        mark = out
        for i in range(per_run):
            mark = jnp.where(index == i, asked[r * per_run + i].astype(f32), mark)
        send[r * wide + per_run] = mark


def entry_ids(entries, problems):
    shape = (problems, LANES)
    base = LANES - -(-entries // problems)
    return (lane_ids(shape) - base) * problems + lax.broadcasted_iota(jnp.int32, shape, 0)


def penalty_kernel(first, per_run, *refs):
    if first:
        got, w, center, width, level, send, image, early, rows, marks, marks_int, sem, *sums = refs
    else:
        got, rows, w, center, width, level, send, image, *sums = refs
    slots = send.shape[0]
    runs = slots // per_run
    if first:
        wide = per_run + 1
        early_sum = functools.reduce(lambda p, q: p + q, [got[r * wide + per_run] for r in range(runs)])
        early[...] = early_sum
        marks_int[...] = early_sum.astype(jnp.int32)
        copy = pltpu.make_async_copy(marks_int, marks, sem)
        copy.start()
        copy.wait()
        problems = w.shape[0]
        base = LANES - -(-slots // problems)
        for s in range(slots):
            rows[s] = marks[s % problems, base + s // problems]
        result = add_rows(got, lambda s: s // per_run * wide + s % per_run, rows, runs, sums)
    else:
        result = add_rows(got, lambda s: s, rows, runs, sums)
    blocks = w.shape[1] // LANES
    for b in range(blocks):
        start = result(b)
        image[:, b * LANES : (b + 1) * LANES] = start
        here = block_of(w, b)
        slack = slack_of(here, block_of(center, b), block_of(width, b))
        rho = rho_of(level, b)
        sums[0][b] = rho * (slack - start) - rho * (here - slack)
    for s in range(slots):
        send[s] = sums[0][rows[s]]


def transpose_kernel(first, *refs):
    if first:
        back, slot, cols, tiles, early, send, acc = refs
    else:
        back, slot, cols, tiles, send, acc = refs
    acc[...] = jnp.zeros_like(acc)

    def one(t):
        high, low = halves(tiles[t])
        term = times(stacked(back[slot[t]]), jnp.concatenate([high, low], axis=0), 0)
        col = cols[t]
        acc[col] = acc[col] + term

    tile_loop(tiles.shape[0], one)
    columns = acc.shape[0]
    for b in range(columns):
        send[:, b * LANES : (b + 1) * LANES] = acc[b]
    if first:
        send[:, columns * LANES :] = early[...]


def prepare_kernel(tiles, hsx, hgx, hsw, hgw, _, flipped, hx, hw):
    tile_loop(tiles.shape[0], lambda t: flipped.__setitem__(t, tiles[t].T))
    for m in range(hx.shape[0]):
        hx[m] = hsx[m] + hgx[m]
        hw[m] = hsw[m] + hgw[m]


def residual_kernel(first, own, other, x, linear, diag, cols, slot, tiles, send, resid, *refs):
    columns = x.shape[1] // LANES
    if first:
        early, left = refs
    else:
        (left,) = refs
    for b in range(columns):
        lo, hi = b * LANES, (b + 1) * LANES
        value = -linear[:, lo:hi] - diag[:, lo:hi] * x[:, lo:hi]
        resid[:, lo:hi] = value + (own[:, lo:hi] + other[:, lo:hi])
    if first:
        early[...] = own[:, columns * LANES :] + other[:, columns * LANES :]
    send_products(resid, cols, lambda t: slot[t], tiles, send, left)


def scalar_kernel(
    share, got, rows, start, w, center, width, level, pw, pgw, x, px, pgx, resid, diag, hgx, hgw, qgx, qgw, send, image, *sums
):
    problems = w.shape[0]
    result = add_rows(got, lambda s: s, rows, sums[0].shape[0], sums)
    memory = hgx.shape[0]
    acc = [None] * SCALARS

    def add(i, value):
        acc[i] = value if acc[i] is None else acc[i] + value

    def terms(u, v, p, s, d, hist):
        for m in range(memory):
            h = hist(m)
            add(U_H + m, u * h)
            add(V_H + m, v * h)
        for i, value in ((U_U, u * u), (U_V, u * v), (U_P, u * p), (V_P, v * p), (V_V, v * v), (S_S, s * s), (U_D, u * d), (V_D, v * d)):
            add(i, value)

    for b in range(w.shape[1] // LANES):
        ar = result(b)
        image[:, b * LANES : (b + 1) * LANES] = ar
        here = block_of(w, b)
        slack = slack_of(here, block_of(center, b), block_of(width, b))
        p = block_of(pgw, b)
        u = relax * (block_of(start, b) - slack) - p
        add(C_C, rho_of(level, b) * ar * ar)
        terms(u, relax * ar, p, here - block_of(pw, b), p - block_of(qgw, b), lambda m: hgw[m, :, b * LANES : (b + 1) * LANES])
    for i in range(share):
        b = lax.axis_index("con") * share + i
        r = at(resid, b)
        p = at(pgx, b)
        add(R_R, r * r)
        add(C_C, at(diag, b) * r * r)
        terms(-p, relax * r, p, at(x, b) - at(px, b), p - at(qgx, b), lambda m: hgx[m, :, pl.ds(pl.multiple_of(b * LANES, LANES), LANES)])
    lanes = lane_ids((problems, LANES))
    lane_of = (LANES - 16 * lax.broadcasted_iota(jnp.int32, (problems, LANES), 0)) & (LANES - 1)
    packed = []
    for row in range(2):
        tile = jnp.zeros((problems, LANES), f32)
        for i in range(16):
            if row * 16 + i < SCALARS:
                tile = jnp.where(lanes == lane_of + i, total(acc[row * 16 + i]), tile)
        packed.append(jnp.sum(tile, axis=0, keepdims=True))
    both = jnp.concatenate(packed, axis=0)
    send[...] = both


def update_kernel(last, steps_before, *refs):
    (late, known, order, sigma_level, x, px, pgx, resid, hx) = refs[:9]
    (w, pw, pgw, start, image, center, width, hw) = refs[9:17]
    refs = refs[17:]
    if steps_before:
        dx, dw = refs[:2]
        refs = refs[2:]
    if last:
        x_out, w_out = refs
    else:
        cols, slot, tiles, x_out, w_out, gx_out, gw_out, dx_out, dw_out, known_out, send, left = refs
    problems = x.shape[0]
    memory = hx.shape[0]
    shape = (problems, LANES)
    lanes = lane_ids(shape)
    program = lax.broadcasted_iota(jnp.int32, shape, 0)
    chains = [late[i] for i in range(min(8, late.shape[0]))]
    for i in range(len(chains), late.shape[0]):
        chains[i % 8] = chains[i % 8] + late[i]
    rows = functools.reduce(lambda p, q: p + q, chains)

    aligned = [
        pltpu.roll(jnp.broadcast_to(rows[i : i + 1], shape), 0, 1, stride=16, stride_axis=0) for i in range(2)
    ]

    def scalar(i):
        return jnp.broadcast_to(aligned[i // 16][:, i % 16 : i % 16 + 1], shape)

    def given(i):
        return jnp.broadcast_to(known[:, i : i + 1], shape)

    new = [jnp.where(order[steps_before] == m, 1.0, 0.0) for m in range(memory)]
    keep = [1.0 - f for f in new]
    if steps_before:
        old = [jnp.where(order[0] == m, 1.0, 0.0) for m in range(memory)]
    sigma = jnp.zeros(shape, f32)
    for k in range(problems):
        sigma = jnp.where(program == k, 0.2 * (1.0 + sigma_level[k].astype(f32)), sigma)
    norm = scalar(R_R)
    step = norm / (scalar(C_C) + sigma * norm)
    u_h = [scalar(U_H + m) for m in range(memory)]
    v_h = [scalar(V_H + m) for m in range(memory)]
    if steps_before:
        u_d, v_d = scalar(U_D), scalar(V_D)
        u_h = [h * (1.0 - f) + u_d * f for h, f in zip(u_h, old)]
        v_h = [h * (1.0 - f) + v_d * f for h, f in zip(v_h, old)]
    dot = [u + step * v for u, v in zip(u_h, v_h)]
    own = scalar(U_U) + 2.0 * step * scalar(U_V) + step * step * scalar(V_V)
    with_p = scalar(U_P) + step * scalar(V_P)
    gram = [[None] * memory for _ in range(memory)]
    for m in range(memory):
        gram[m][m] = given(m * memory + m) * keep[m] + own * new[m]
        for n in range(m + 1, memory):
            value = given(m * memory + n) * (keep[m] * keep[n]) + dot[n] * new[m] + dot[m] * new[n]
            gram[m][n] = gram[n][m] = value
    at_p, at_s = memory * memory, memory * (memory + 1)
    rhs = []
    for m in range(memory):
        value = given(at_p + m) * keep[m] + with_p * new[m]
        for n in range(memory):
            value = value + gram[m][n] * new[n]
        rhs.append(value)
    s_s = scalar(S_S)
    squares = [given(at_s + m) * keep[m] + s_s * new[m] for m in range(memory)]
    frob = functools.reduce(lambda p, q: p + q, squares + [gram[m][m] for m in range(memory)])
    damp = ridge * frob
    if not last:
        out = jnp.zeros(shape, f32)
        for m in range(memory):
            for n in range(m, memory):
                out = jnp.where((lanes == m * memory + n) | (lanes == n * memory + m), gram[m][n], out)
            out = jnp.where(lanes == at_p + m, rhs[m], out)
            out = jnp.where(lanes == at_s + m, squares[m], out)
        known_out[...] = out
    low = [[None] * memory for _ in range(memory)]
    inverse = []
    for j in range(memory):
        value = gram[j][j] + damp
        for k in range(j):
            value = value - low[j][k] * low[j][k]
        inverse.append(1.0 / jnp.sqrt(value))
        for i in range(j + 1, memory):
            value = gram[i][j]
            for k in range(j):
                value = value - low[i][k] * low[j][k]
            low[i][j] = value * inverse[j]
    half = []
    for i in range(memory):
        value = rhs[i]
        for k in range(i):
            value = value - low[i][k] * half[k]
        half.append(value * inverse[i])
    coef = [None] * memory
    for i in reversed(range(memory)):
        value = half[i]
        for k in range(i + 1, memory):
            value = value - low[k][i] * coef[k]
        coef[i] = value * inverse[i]

    newest = functools.reduce(lambda p, q: p + q, [c * f for c, f in zip(coef, new)])
    left_over = [c * f for c, f in zip(coef, keep)]
    if steps_before:
        older = functools.reduce(lambda p, q: p + q, [c * f for c, f in zip(left_over, old)])
        left_over = [c * (1.0 - f) for c, f in zip(left_over, old)]

    scaled = relax * step
    older = older if steps_before else None
    for b in range(x.shape[1] // LANES):
        g = scaled * block_of(resid, b)
        advance(b, newest, left_over, older, x, px, g, pgx, hx, dx if steps_before else None, x_out, None if last else gx_out, None if last else dx_out)
    for b in range(w.shape[1] // LANES):
        slack = slack_of(block_of(w, b), block_of(center, b), block_of(width, b))
        g = relax * (block_of(start, b) + step * block_of(image, b) - slack)
        advance(b, newest, left_over, older, w, pw, g, pgw, hw, dw if steps_before else None, w_out, None if last else gw_out, None if last else dw_out)
    if not last:
        send_products(x_out, cols, lambda t: slot[t], tiles, send, left)


def advance(b, newest, left_over, older, state, previous, g, previous_g, hist, kept, out, g_out, d_out):
    lo, hi = b * LANES, (b + 1) * LANES
    here = state[:, lo:hi]
    fresh = (here - previous[:, lo:hi]) + (g - previous_g[:, lo:hi])
    value = here + g - newest * fresh
    for m in range(len(left_over)):
        value = value - left_over[m] * hist[m, :, lo:hi]
    if kept is not None:
        value = value - older * kept[:, lo:hi]
    out[:, lo:hi] = value
    if g_out is not None:
        g_out[:, lo:hi] = g
        d_out[:, lo:hi] = fresh


def call(kernel, name, ins, outs, scratch=()):
    spaces = {"v": pltpu.VMEM, "s": pltpu.SMEM, "h": pltpu.HBM}
    return pl.pallas_call(
        kernel,
        out_shape=[jax.ShapeDtypeStruct(shape, dtype) for shape, dtype, _ in outs],
        in_specs=[pl.BlockSpec(memory_space=spaces[space]) for _, space in ins],
        out_specs=[pl.BlockSpec(memory_space=spaces[space]) for _, _, space in outs],
        scratch_shapes=list(scratch),
        compiler_params=pltpu.CompilerParams(vmem_limit_bytes=24 * 1024 * 1024),
        name=name,
    )(*[array for array, _ in ins])


def per_device(
    tiles,
    row_tile,
    col_tile,
    diag_cost,
    linear_cost,
    bound_center,
    bound_width,
    rho_level,
    sigma_level,
    state_x,
    state_w,
    prev_x,
    prev_w,
    prev_gx,
    prev_gw,
    hist_sx,
    hist_sw,
    hist_gx,
    hist_gw,
    slot_order,
):
    problems, var_cols = state_x.shape
    con_cols = state_w.shape[1]
    tile_size = tiles.shape[-1]
    var_count, con_count = lax.axis_size("var"), lax.axis_size("con")
    col_count = var_cols // tile_size
    run_length = con_cols // tile_size
    blocks = tiles.reshape(-1, tile_size, tile_size)
    count = blocks.shape[0]
    per_run = -(-count // var_count)
    slots = var_count * per_run
    rows_here = row_tile.reshape(-1)
    cols_here = col_tile.reshape(-1)
    diag = diag_cost.reshape(1, -1)
    level = rho_level.reshape(1, -1)

    x_like = ((problems, var_cols), f32, "v")
    w_like = ((problems, con_cols), f32, "v")
    panel = ((slots, problems, tile_size), f32, "v")
    wide_panel = ((slots + var_count, problems, tile_size), f32, "v")
    one_tile = ((problems, tile_size), f32, "v")
    left = pltpu.VMEM((col_count, 2 * problems, 2 * tile_size), bf16)
    sums = [pltpu.VMEM((run_length, problems, tile_size), f32)] * 4
    bounds = [(bound_center, "v"), (bound_width, "v")]
    vs = lambda *arrays: [(a, "v") for a in arrays]
    ss = lambda *arrays: [(a, "s") for a in arrays]

    def exchange(x):
        return lax.all_to_all(x, "var", 0, 0, tiled=True)

    def over_con(x):
        def partner(x, k):
            return lax.ppermute(x, "con", [(i, i ^ k) for i in range(con_count)])

        others = [partner(x, k) for k in range(2, con_count, 2)]
        terms = [x] + others
        while len(terms) > 1:
            terms = [a + b for a, b in zip(terms[::2], terms[1::2])]
        return terms[0], partner(terms[0], 1)

    one_core = [list(range(k, con_count * var_count, 2)) for k in range(2)]
    share = col_count // con_count
    parts = max(d for d in range(1, 4) if count % d == 0)
    far = [state_x, blocks, prev_x, state_w, prev_w, prev_gx, prev_gw, hist_sx, hist_sw, hist_gx, hist_gw]
    x_mine, w_mine = pltpu.VMEM((problems, share * tile_size), f32), pltpu.VMEM((problems, con_cols), f32)
    memory = hist_gx.shape[0]
    hx_mine = pltpu.VMEM((memory, problems, share * tile_size), f32)
    hw_mine = pltpu.VMEM((memory, problems, con_cols), f32)
    sent, slot = call(
        functools.partial(open_kernel, per_run, run_length, share, parts),
        "open",
        [(pltpu.with_memory_space_constraint(a, pltpu.HBM), "h") for a in [row_tile[0], col_tile[0]] + far],
        [wide_panel, ((count,), jnp.int32, "s")],
        [
            pltpu.SMEM((1, count), jnp.int32),
            pltpu.SMEM((1, count), jnp.int32),
            pltpu.VMEM((problems, var_cols), f32),
            pltpu.VMEM(blocks.shape, f32),
            x_mine, w_mine, w_mine, x_mine, w_mine, hx_mine, hw_mine, hx_mine, hw_mine,
            left,
            pltpu.SMEM((var_count,), jnp.int32),
            pltpu.SMEM((slots,), jnp.int32),
            pltpu.SMEM((count,), jnp.int32),
            pltpu.SemaphoreType.DMA((3 + parts + 9,)),
        ],
    )
    got = exchange(sent)
    x, w, px, pw, pgx, pgw = state_x, state_w, prev_x, prev_w, prev_gx, prev_gw
    qgx, qgw = pgx, pgw
    kept = []
    known = None
    for step in range(STEPS):
        first, last = step == 0, step == STEPS - 1
        if first:
            sent, start, early, rows = call(
                functools.partial(penalty_kernel, True, per_run),
                "penalty_first",
                vs(got, w, bound_center, bound_width, level),
                [panel, w_like, one_tile, ((slots,), jnp.int32, "s")],
                [pltpu.SMEM((problems, tile_size), jnp.int32), pltpu.VMEM((problems, tile_size), jnp.int32), pltpu.SemaphoreType.DMA(())]
                + sums,
            )
        else:
            sent, start = call(
                functools.partial(penalty_kernel, False, per_run),
                "penalty",
                vs(got) + ss(rows) + vs(w, bound_center, bound_width, level),
                [panel, w_like],
                sums,
            )
        back = exchange(sent)
        width = var_cols + (tile_size if first else 0)
        (sent,) = call(
            functools.partial(transpose_kernel, first),
            "transpose",
            vs(back) + ss(slot, cols_here) + vs(blocks) + (vs(early) if first else []),
            [((problems, width), f32, "v")],
            [pltpu.VMEM((col_count, problems, tile_size), f32)],
        )
        own, other = over_con(sent)
        if first:
            flipped, hist_x, hist_w = call(
                prepare_kernel,
                "prepare",
                vs(blocks, hist_sx, hist_gx, hist_sw, hist_gw, sent),
                [(blocks.shape, f32, "v"), (hist_sx.shape, f32, "v"), (hist_sw.shape, f32, "v")],
            )
        outs = call(
            functools.partial(residual_kernel, first),
            "residual",
            vs(own, other, x, linear_cost, diag) + ss(cols_here, slot) + vs(flipped),
            [panel, x_like] + ([one_tile] if first else []),
            [left],
        )
        sent, resid = outs[:2]
        if first:
            known = outs[2]
        got = exchange(sent)

        sent, image = call(
            functools.partial(scalar_kernel, share),
            "scalars",
            vs(got)
            + ss(rows)
            + vs(start, w, bound_center, bound_width, level, pw, pgw, x, px, pgx, resid, diag, hist_gx, hist_gw, qgx, qgw),
            [((2, LANES), f32, "v"), w_like],
            sums,
        )
        pair = sent + lax.ppermute(sent, "var", [(i, i ^ 1) for i in range(var_count)])
        copies = jnp.broadcast_to(pair[None], (con_count * var_count // 2, 2, LANES))
        late = lax.all_to_all(copies, ("con", "var"), 0, 0, tiled=True, axis_index_groups=one_core)
        outs = call(
            functools.partial(update_kernel, last, step),
            "update",
            vs(late, known)
            + ss(slot_order, sigma_level)
            + vs(x, px, pgx, resid, hist_x, w, pw, pgw, start, image, bound_center, bound_width, hist_w)
            + vs(*kept)
            + ([] if last else ss(cols_here, slot) + vs(flipped)),
            [x_like, w_like] + ([] if last else [x_like, w_like, x_like, w_like, one_tile, panel]),
            [] if last else [left],
        )
        if last:
            return outs[0], outs[1]
        qgx, qgw = pgx, pgw
        px, pw = x, w
        x, w, pgx, pgw, dx, dw, known, sent = outs
        kept = [dx, dw]
        got = exchange(sent)


def solution(mesh):
    in_specs = (
        P("con", "var", None, None, None),
        P("con", "var", None),
        P("con", "var", None),
        P("var"),
        P(None, "var"),
        P(None, ("con", "var")),
        P(None, ("con", "var")),
        P(("con", "var")),
        P(),
        P(None, "var"),
        P(None, ("con", "var")),
        P(None, "var"),
        P(None, ("con", "var")),
        P(None, "var"),
        P(None, ("con", "var")),
        P(None, None, "var"),
        P(None, None, ("con", "var")),
        P(None, None, "var"),
        P(None, None, ("con", "var")),
        P(),
    )
    out_specs = (P(None, "var"), P(None, ("con", "var")))
    return jax.shard_map(
        per_device, mesh=mesh, in_specs=in_specs, out_specs=out_specs, check_vma=False
    )
```

```python
import functools

import jax
import jax.numpy as jnp
from jax import lax
from jax.experimental import pallas as pl
from jax.experimental.pallas import tpu as pltpu
from jax.sharding import PartitionSpec as P

STEPS = 2
LANES = 128
UNROLL = 72

relax = 1.6
ridge = 0.01

f32 = jnp.float32
bf16 = jnp.bfloat16

U_H, V_H, U_U, U_V, U_P, V_P, V_V, S_S, R_R, C_C, U_D, V_D, SCALARS = 0, 8, 16, 17, 18, 19, 20, 21, 22, 23, 24, 25, 26


MEMORY = 8
LANE_P, LANE_S, LANE_ENTRY = 36, 44, 52


def pair_lane(m, n):
    return m * MEMORY - m * (m - 1) // 2 + n - m


def halves(value):
    high = value.astype(bf16)
    return high, (value - high.astype(f32)).astype(bf16)


def stacked(piece):
    high, low = halves(piece)
    return jnp.concatenate(
        [
            jnp.concatenate([high, high], axis=1),
            jnp.concatenate([low, jnp.zeros_like(low)], axis=1),
        ],
        axis=0,
    )


def times(left, right, contract):
    both = lax.dot_general(left, right, (((1,), (contract,)), ((), ())), preferred_element_type=f32)
    half = both.shape[0] // 2
    return both[:half] + both[half:]


def at(ref, block):
    if isinstance(block, int):
        return block_of(ref, block)
    return ref[:, pl.ds(pl.multiple_of(block * LANES, LANES), LANES)]


def tile_loop(count, body):
    step = max(d for d in range(1, UNROLL + 1) if count % d == 0)

    if step == count:
        for j in range(count):
            body(j)
        return

    def some(i, _):
        for j in range(step):
            body(i * step + j)
        return 0

    lax.fori_loop(0, count // step, some, 0)


def lane_ids(shape):
    return lax.broadcasted_iota(jnp.int32, shape, len(shape) - 1)


def send_products(x_ref, cols, where, tiles, send, left, waits=(None,), flipped=True):
    for block in range(x_ref.shape[1] // LANES):
        left[block] = stacked(x_ref[:, block * LANES : (block + 1) * LANES])
    send[...] = jnp.zeros_like(send)

    def one(t):
        axis = 0 if flipped else 1
        value = times(left[cols[t]], jnp.concatenate(halves(tiles[t]), axis=axis), axis)
        if flipped:
            send[where(t)] = value
        else:
            send[where(t)] = value[: value.shape[0] // 2]
            send[where(t) + 1] = value[value.shape[0] // 2 :]

    size = tiles.shape[0] // len(waits)
    for i, wait in enumerate(waits):
        if wait is not None:
            wait()
        tile_loop(size, lambda t, i=i: one(t + i * size))


def add_rows(received, rows, sums):
    for ref in sums:
        ref[...] = jnp.zeros_like(ref)
    for s in range(rows.shape[0]):
        ref = sums[s % len(sums)]
        row = rows[s]
        ref[row] = ref[row] + received(s)
    return lambda b: functools.reduce(lambda p, q: p + q, [ref[b] for ref in sums])


def block_of(ref, b):
    return ref[:, b * LANES : (b + 1) * LANES]


def rho_of(level_ref, b):
    return 0.4 * (1.0 + block_of(level_ref, b).astype(f32))


def slack_of(w, center, width):
    return jnp.minimum(jnp.maximum(w, center - width), center + width)


def total(value):
    return jnp.sum(value, axis=1, keepdims=True)


def open_kernel(per_run, run_length, share, parts, *refs):
    (hbm_rows, hbm_cols, hbm_x, hbm_tiles, *far), (send, slot, tiles), refs = refs[:13], refs[13:16], refs[16:]
    rows_buf, cols_buf, x, px, w, pw, pgx, pgw, hsx, hsw, hgx, hgw, left, count, asked, spot, sem = refs
    memory = hgx.shape[0]
    problems = x.shape[0]
    half = problems // 2
    wide = 2 * per_run + 1
    runs = send.shape[0] // wide
    first = lax.axis_index("con") * share
    mine = pl.ds(pl.multiple_of(first * LANES, LANES), share * LANES)
    far_px, far_w, far_pw, far_pgx, far_pgw, far_hsx, far_hsw, far_hgx, far_hgw = far
    size = tiles.shape[0] // parts
    moves = [(hbm_rows, rows_buf), (hbm_cols, cols_buf), (hbm_x, x)]
    moves += [(hbm_tiles.at[pl.ds(i * size, size)], tiles.at[pl.ds(i * size, size)]) for i in range(parts)]
    moves += [(far_w, w), (far_pw, pw), (far_pgw, pgw), (far_hsw, hsw), (far_hgw, hgw)]
    moves += [(far_px.at[:, mine], px), (far_pgx.at[:, mine], pgx), (far_hsx.at[:, :, mine], hsx), (far_hgx.at[:, :, mine], hgx)]
    copies = [pltpu.make_async_copy(a, b, sem.at[i]) for i, (a, b) in enumerate(moves)]
    for copy in copies:
        copy.start()
    rows, cols = rows_buf.at[0], cols_buf.at[0]

    for i in range(runs):
        count[i] = 0
    for i in range(runs * per_run):
        asked[i] = 0
    copies[0].wait()
    copies[1].wait()
    for t in range(tiles.shape[0]):
        row = rows[t]
        owner = row >> (run_length.bit_length() - 1)
        rank = count[owner]
        count[owner] = rank + 1
        place = owner * per_run + rank
        slot[t] = place
        spot[t] = owner * wide + rank * 2
        asked[place] = row & (run_length - 1)

    def where(t):
        return spot[t]

    copies[2].wait()
    send_products(x, cols, where, tiles, send, left, [copy.wait for copy in copies[3 : 3 + parts]], flipped=False)
    for copy in copies[3 + parts :]:
        copy.wait()

    lanes = lane_ids((problems, LANES))
    out = jnp.zeros((problems, LANES), f32)

    places = [(False, b) for b in range(w.shape[1] // LANES)] + [(True, b) for b in range(share)]

    def read(ref_x, ref_w, place):
        is_x, b = place
        ref = ref_x if is_x else ref_w
        return ref[..., b * LANES : (b + 1) * LANES]

    acc = {}

    def add(lane, value):
        acc[lane] = acc[lane] + value if lane in acc else value

    for place in places:
        g = [read(hgx.at[m], hgw.at[m], place) for m in range(memory)]
        for m in range(memory):
            for n in range(m, memory):
                add(pair_lane(m, n), g[m] * g[n])
    for place in places:
        p = read(pgx, pgw, place)
        for m in range(memory):
            add(LANE_P + m, read(hgx.at[m], hgw.at[m], place) * p)
            h = read(hsx.at[m], hsw.at[m], place)
            add(LANE_S + m, h * h)
    for lane, value in acc.items():
        out = jnp.where(lanes == lane, total(value), out)
    index = entry_ids(problems) - lax.axis_index("var") * per_run
    for r in range(runs):
        mark = out
        for i in range(per_run):
            mark = jnp.where(index == i, asked[r * per_run + i].astype(f32), mark)
        turned = pltpu.roll(mark, LANES // 2, 1)
        send[r * wide + 2 * per_run] = jnp.where(lanes[:half] < LANES // 2, mark[:half], turned[half:])


def entry_ids(problems):
    shape = (problems, LANES)
    return (lane_ids(shape) - LANE_ENTRY) * problems + lax.broadcasted_iota(jnp.int32, shape, 0)


def penalty_kernel(first, per_run, *refs):
    if first:
        got, w, center, width, level, send, image, early, rows, marks, marks_int, sem, *sums = refs
    else:
        got, rows, w, center, width, level, send, image, *sums = refs
    slots = send.shape[0]
    runs = slots // per_run
    if first:
        wide = 2 * per_run + 1
        folded = functools.reduce(lambda p, q: p + q, [got[r * wide + 2 * per_run] for r in range(runs)])
        early_sum = jnp.concatenate([folded, pltpu.roll(folded, LANES // 2, 1)], axis=0)
        early[...] = early_sum
        marks_int[...] = early_sum.astype(jnp.int32)
        copy = pltpu.make_async_copy(marks_int, marks, sem)
        copy.start()
        copy.wait()
        problems = w.shape[0]
        for s in range(slots):
            rows[s] = marks[s % problems, LANE_ENTRY + s // problems]

        def received(s):
            unit = s // per_run * wide + s % per_run * 2
            return jnp.concatenate([got[unit], got[unit + 1]], axis=0)

        result = add_rows(received, rows, sums)
    else:
        result = add_rows(lambda s: got[s], rows, sums)
    blocks = w.shape[1] // LANES
    for b in range(blocks):
        start = result(b)
        image[:, b * LANES : (b + 1) * LANES] = start
        here = block_of(w, b)
        slack = slack_of(here, block_of(center, b), block_of(width, b))
        rho = rho_of(level, b)
        sums[0][b] = rho * (slack - start) - rho * (here - slack)
    for s in range(slots):
        send[s] = sums[0][rows[s]]


def transpose_kernel(first, *refs):
    if first:
        back, slot, cols, tiles, early, send, acc = refs
    else:
        back, slot, cols, tiles, send, acc = refs
    acc[...] = jnp.zeros_like(acc)

    def one(t):
        high, low = halves(tiles[t])
        term = times(stacked(back[slot[t]]), jnp.concatenate([high, low], axis=0), 0)
        col = cols[t]
        acc[col] = acc[col] + term

    tile_loop(tiles.shape[0], one)
    columns = acc.shape[0]
    for b in range(columns):
        send[:, b * LANES : (b + 1) * LANES] = acc[b]
    if first:
        send[:, columns * LANES :] = early[...]


def prepare_kernel(tiles, hsx, hgx, hsw, hgw, _, flipped, hx, hw):
    tile_loop(tiles.shape[0], lambda t: flipped.__setitem__(t, tiles[t].T))
    for m in range(hx.shape[0]):
        hx[m] = hsx[m] + hgx[m]
        hw[m] = hsw[m] + hgw[m]


def residual_kernel(first, own, other, x, linear, diag, cols, slot, tiles, send, resid, *refs):
    columns = x.shape[1] // LANES
    if first:
        early, left = refs
    else:
        (left,) = refs
    for b in range(columns):
        lo, hi = b * LANES, (b + 1) * LANES
        value = -linear[:, lo:hi] - diag[:, lo:hi] * x[:, lo:hi]
        resid[:, lo:hi] = value + (own[:, lo:hi] + other[:, lo:hi])
    if first:
        early[...] = own[:, columns * LANES :] + other[:, columns * LANES :]
    send_products(resid, cols, lambda t: slot[t], tiles, send, left)


class Sums:
    def __init__(self, problems):
        self.shape = (problems, LANES)
        self.acc = {}

    def add(self, i, value):
        self.acc[i] = self.acc[i] + value if i in self.acc else value

    def tiles(self, tiles):
        turn = (LANES - 16 * lax.broadcasted_iota(jnp.int32, self.shape, 0)) & (LANES - 1)
        lanes = lane_ids(self.shape)
        tiles = list(tiles)
        for i, value in self.acc.items():
            tiles[i // 16] = jnp.where(lanes == turn + i % 16, total(value), tiles[i // 16])
        return tiles


def blocks_of(w, share):
    first = lax.axis_index("con") * share
    return [(False, b) for b in range(w.shape[1] // LANES)] + [(True, first + b) for b in range(share)]


def before_kernel(share, start, w, center, width, pw, pgw, x, px, pgx, hgx, hgw, qgx, qgw, _, out):
    sums = Sums(w.shape[0])
    for is_x, b in blocks_of(w, share):
        if is_x:
            p = at(pgx, b)
            u, s, d = -p, at(x, b) - at(px, b), p - at(qgx, b)
        else:
            p, here = block_of(pgw, b), block_of(w, b)
            slack = slack_of(here, block_of(center, b), block_of(width, b))
            u, s, d = relax * (block_of(start, b) - slack) - p, here - block_of(pw, b), p - block_of(qgw, b)
        for m in range(MEMORY):
            sums.add(U_H + m, u * at(hgx.at[m] if is_x else hgw.at[m], b))
        for i, value in ((U_U, u * u), (U_P, u * p), (S_S, s * s), (U_D, u * d)):
            sums.add(i, value)
    zero = jnp.zeros(sums.shape, f32)
    out[0], out[1] = sums.tiles([zero, zero])


def scalar_kernel(
    share, got, rows, start, w, center, width, level, pgw, pgx, resid, diag, hgx, hgw, qgx, qgw, before, send, image, *scratch
):
    result = add_rows(lambda s: got[s], rows, scratch)
    sums = Sums(w.shape[0])
    for is_x, b in blocks_of(w, share):
        if is_x:
            r, p = at(resid, b), at(pgx, b)
            u, v, d = -p, relax * r, p - at(qgx, b)
            sums.add(R_R, r * r)
            sums.add(C_C, at(diag, b) * r * r)
        else:
            ar, p = result(b), block_of(pgw, b)
            image[:, b * LANES : (b + 1) * LANES] = ar
            slack = slack_of(block_of(w, b), block_of(center, b), block_of(width, b))
            u, v, d = relax * (block_of(start, b) - slack) - p, relax * ar, p - block_of(qgw, b)
            sums.add(C_C, rho_of(level, b) * ar * ar)
        for m in range(MEMORY):
            sums.add(V_H + m, v * at(hgx.at[m] if is_x else hgw.at[m], b))
        for i, value in ((U_V, u * v), (V_P, v * p), (V_V, v * v), (V_D, v * d)):
            sums.add(i, value)
    rows_out = [jnp.sum(tile, axis=0, keepdims=True) for tile in sums.tiles([before[0], before[1]])]
    send[...] = jnp.concatenate(rows_out, axis=0)


def update_kernel(last, steps_before, *refs):
    (late, known, order, sigma_level, x, px, pgx, resid, hx) = refs[:9]
    (w, pw, pgw, start, image, center, width, hw) = refs[9:17]
    refs = refs[17:]
    if steps_before:
        dx, dw = refs[:2]
        refs = refs[2:]
    if last:
        x_out, w_out = refs
    else:
        cols, slot, tiles, x_out, w_out, gx_out, gw_out, dx_out, dw_out, known_out, send, left = refs
    problems = x.shape[0]
    memory = hx.shape[0]
    shape = (problems, LANES)
    lanes = lane_ids(shape)
    program = lax.broadcasted_iota(jnp.int32, shape, 0)
    chains = [late[i] for i in range(min(8, late.shape[0]))]
    for i in range(len(chains), late.shape[0]):
        chains[i % 8] = chains[i % 8] + late[i]
    rows = functools.reduce(lambda p, q: p + q, chains)

    aligned = [
        pltpu.roll(jnp.broadcast_to(rows[i : i + 1], shape), 0, 1, stride=16, stride_axis=0) for i in range(2)
    ]

    def scalar(i):
        return jnp.broadcast_to(aligned[i // 16][:, i % 16 : i % 16 + 1], shape)

    def given(i):
        return jnp.broadcast_to(known[:, i : i + 1], shape)

    new = [jnp.where(order[steps_before] == m, 1.0, 0.0) for m in range(memory)]
    keep = [1.0 - f for f in new]
    if steps_before:
        old = [jnp.where(order[0] == m, 1.0, 0.0) for m in range(memory)]
    sigma = jnp.zeros(shape, f32)
    for k in range(problems):
        sigma = jnp.where(program == k, 0.2 * (1.0 + sigma_level[k].astype(f32)), sigma)
    norm = scalar(R_R)
    step = norm / (scalar(C_C) + sigma * norm)
    u_h = [scalar(U_H + m) for m in range(memory)]
    v_h = [scalar(V_H + m) for m in range(memory)]
    if steps_before:
        u_d, v_d = scalar(U_D), scalar(V_D)
        u_h = [h * (1.0 - f) + u_d * f for h, f in zip(u_h, old)]
        v_h = [h * (1.0 - f) + v_d * f for h, f in zip(v_h, old)]
    dot = [u + step * v for u, v in zip(u_h, v_h)]
    own = scalar(U_U) + 2.0 * step * scalar(U_V) + step * step * scalar(V_V)
    with_p = scalar(U_P) + step * scalar(V_P)
    gram = [[None] * memory for _ in range(memory)]
    for m in range(memory):
        gram[m][m] = given(pair_lane(m, m)) * keep[m] + own * new[m]
        for n in range(m + 1, memory):
            value = given(pair_lane(m, n)) * (keep[m] * keep[n]) + dot[n] * new[m] + dot[m] * new[n]
            gram[m][n] = gram[n][m] = value
    rhs = []
    for m in range(memory):
        value = given(LANE_P + m) * keep[m] + with_p * new[m]
        for n in range(memory):
            value = value + gram[m][n] * new[n]
        rhs.append(value)
    s_s = scalar(S_S)
    squares = [given(LANE_S + m) * keep[m] + s_s * new[m] for m in range(memory)]
    frob = functools.reduce(lambda p, q: p + q, squares + [gram[m][m] for m in range(memory)])
    damp = ridge * frob
    if not last:
        out = jnp.zeros(shape, f32)
        for m in range(memory):
            for n in range(m, memory):
                out = jnp.where(lanes == pair_lane(m, n), gram[m][n], out)
            out = jnp.where(lanes == LANE_P + m, rhs[m], out)
            out = jnp.where(lanes == LANE_S + m, squares[m], out)
        known_out[...] = out
    low = [[None] * memory for _ in range(memory)]
    inverse = []
    for j in range(memory):
        value = gram[j][j] + damp
        for k in range(j):
            value = value - low[j][k] * low[j][k]
        inverse.append(1.0 / jnp.sqrt(value))
        for i in range(j + 1, memory):
            value = gram[i][j]
            for k in range(j):
                value = value - low[i][k] * low[j][k]
            low[i][j] = value * inverse[j]
    half = []
    for i in range(memory):
        value = rhs[i]
        for k in range(i):
            value = value - low[i][k] * half[k]
        half.append(value * inverse[i])
    coef = [None] * memory
    for i in reversed(range(memory)):
        value = half[i]
        for k in range(i + 1, memory):
            value = value - low[k][i] * coef[k]
        coef[i] = value * inverse[i]

    newest = functools.reduce(lambda p, q: p + q, [c * f for c, f in zip(coef, new)])
    left_over = [c * f for c, f in zip(coef, keep)]
    if steps_before:
        older = functools.reduce(lambda p, q: p + q, [c * f for c, f in zip(left_over, old)])
        left_over = [c * (1.0 - f) for c, f in zip(left_over, old)]

    scaled = relax * step
    older = older if steps_before else None
    for b in range(x.shape[1] // LANES):
        g = scaled * block_of(resid, b)
        advance(b, newest, left_over, older, x, px, g, pgx, hx, dx if steps_before else None, x_out, None if last else gx_out, None if last else dx_out)
    for b in range(w.shape[1] // LANES):
        slack = slack_of(block_of(w, b), block_of(center, b), block_of(width, b))
        g = relax * (block_of(start, b) + step * block_of(image, b) - slack)
        advance(b, newest, left_over, older, w, pw, g, pgw, hw, dw if steps_before else None, w_out, None if last else gw_out, None if last else dw_out)
    if not last:
        send_products(x_out, cols, lambda t: slot[t], tiles, send, left)


def advance(b, newest, left_over, older, state, previous, g, previous_g, hist, kept, out, g_out, d_out):
    lo, hi = b * LANES, (b + 1) * LANES
    here = state[:, lo:hi]
    fresh = (here - previous[:, lo:hi]) + (g - previous_g[:, lo:hi])
    value = here + g - newest * fresh
    for m in range(len(left_over)):
        value = value - left_over[m] * hist[m, :, lo:hi]
    if kept is not None:
        value = value - older * kept[:, lo:hi]
    out[:, lo:hi] = value
    if g_out is not None:
        g_out[:, lo:hi] = g
        d_out[:, lo:hi] = fresh


def call(kernel, name, ins, outs, scratch=()):
    spaces = {"v": pltpu.VMEM, "s": pltpu.SMEM, "h": pltpu.HBM}
    return pl.pallas_call(
        kernel,
        out_shape=[jax.ShapeDtypeStruct(shape, dtype) for shape, dtype, _ in outs],
        in_specs=[pl.BlockSpec(memory_space=spaces[space]) for _, space in ins],
        out_specs=[pl.BlockSpec(memory_space=spaces[space]) for _, _, space in outs],
        scratch_shapes=list(scratch),
        compiler_params=pltpu.CompilerParams(vmem_limit_bytes=24 * 1024 * 1024),
        name=name,
    )(*[array for array, _ in ins])


def per_device(
    tiles,
    row_tile,
    col_tile,
    diag_cost,
    linear_cost,
    bound_center,
    bound_width,
    rho_level,
    sigma_level,
    state_x,
    state_w,
    prev_x,
    prev_w,
    prev_gx,
    prev_gw,
    hist_sx,
    hist_sw,
    hist_gx,
    hist_gw,
    slot_order,
):
    problems, var_cols = state_x.shape
    con_cols = state_w.shape[1]
    tile_size = tiles.shape[-1]
    var_count, con_count = lax.axis_size("var"), lax.axis_size("con")
    col_count = var_cols // tile_size
    run_length = con_cols // tile_size
    blocks = tiles.reshape(-1, tile_size, tile_size)
    count = blocks.shape[0]
    per_run = -(-count // var_count)
    slots = var_count * per_run
    rows_here = row_tile.reshape(-1)
    cols_here = col_tile.reshape(-1)
    diag = diag_cost.reshape(1, -1)
    level = rho_level.reshape(1, -1)

    x_like = ((problems, var_cols), f32, "v")
    w_like = ((problems, con_cols), f32, "v")
    panel = ((slots, problems, tile_size), f32, "v")
    wide_panel = (((2 * per_run + 1) * var_count, problems // 2, tile_size), f32, "v")
    one_tile = ((problems, tile_size), f32, "v")
    left = pltpu.VMEM((col_count, 2 * problems, 2 * tile_size), bf16)
    sums = [pltpu.VMEM((run_length, problems, tile_size), f32)] * 4
    bounds = [(bound_center, "v"), (bound_width, "v")]
    vs = lambda *arrays: [(a, "v") for a in arrays]
    ss = lambda *arrays: [(a, "s") for a in arrays]

    def exchange(x):
        return lax.all_to_all(x, "var", 0, 0, tiled=True)

    def over_con(x):
        def partner(x, k):
            return lax.ppermute(x, "con", [(i, i ^ k) for i in range(con_count)])

        others = [partner(x, k) for k in range(2, con_count, 2)]
        terms = [x] + others
        while len(terms) > 1:
            terms = [a + b for a, b in zip(terms[::2], terms[1::2])]
        return terms[0], partner(terms[0], 1)

    one_core = [list(range(k, con_count * var_count, 2)) for k in range(2)]
    share = col_count // con_count
    parts = max(d for d in range(1, 4) if count % d == 0)
    far = [state_x, blocks, prev_x, state_w, prev_w, prev_gx, prev_gw, hist_sx, hist_sw, hist_gx, hist_gw]
    x_mine, w_mine = pltpu.VMEM((problems, share * tile_size), f32), pltpu.VMEM((problems, con_cols), f32)
    memory = hist_gx.shape[0]
    hx_mine = pltpu.VMEM((memory, problems, share * tile_size), f32)
    hw_mine = pltpu.VMEM((memory, problems, con_cols), f32)
    sent, slot, blocks = call(
        functools.partial(open_kernel, per_run, run_length, share, parts),
        "open",
        [(pltpu.with_memory_space_constraint(a, pltpu.HBM), "h") for a in [row_tile[0], col_tile[0]] + far],
        [wide_panel, ((count,), jnp.int32, "s"), (blocks.shape, f32, "v")],
        [
            pltpu.SMEM((1, count), jnp.int32),
            pltpu.SMEM((1, count), jnp.int32),
            pltpu.VMEM((problems, var_cols), f32),
            x_mine, w_mine, w_mine, x_mine, w_mine, hx_mine, hw_mine, hx_mine, hw_mine,
            left,
            pltpu.SMEM((var_count,), jnp.int32),
            pltpu.SMEM((slots,), jnp.int32),
            pltpu.SMEM((count,), jnp.int32),
            pltpu.SemaphoreType.DMA((3 + parts + 9,)),
        ],
    )
    got = exchange(sent)
    x, w, px, pw, pgx, pgw = state_x, state_w, prev_x, prev_w, prev_gx, prev_gw
    qgx, qgw = pgx, pgw
    kept = []
    known = None
    for step in range(STEPS):
        first, last = step == 0, step == STEPS - 1
        if first:
            sent, start, early, rows = call(
                functools.partial(penalty_kernel, True, per_run),
                "penalty_first",
                vs(got, w, bound_center, bound_width, level),
                [panel, w_like, one_tile, ((slots,), jnp.int32, "s")],
                [pltpu.SMEM((problems, tile_size), jnp.int32), pltpu.VMEM((problems, tile_size), jnp.int32), pltpu.SemaphoreType.DMA(())]
                + sums,
            )
        else:
            sent, start = call(
                functools.partial(penalty_kernel, False, per_run),
                "penalty",
                vs(got) + ss(rows) + vs(w, bound_center, bound_width, level),
                [panel, w_like],
                sums,
            )
        back = exchange(sent)
        width = var_cols + (tile_size if first else 0)
        (sent,) = call(
            functools.partial(transpose_kernel, first),
            "transpose",
            vs(back) + ss(slot, cols_here) + vs(blocks) + (vs(early) if first else []),
            [((problems, width), f32, "v")],
            [pltpu.VMEM((col_count, problems, tile_size), f32)],
        )
        own, other = over_con(sent)
        (before,) = call(
            functools.partial(before_kernel, share),
            "before",
            vs(start, w, bound_center, bound_width, pw, pgw, x, px, pgx, hist_gx, hist_gw, qgx, qgw, sent),
            [((2, problems, tile_size), f32, "v")],
        )
        if first:
            flipped, hist_x, hist_w = call(
                prepare_kernel,
                "prepare",
                vs(blocks, hist_sx, hist_gx, hist_sw, hist_gw, sent),
                [(blocks.shape, f32, "v"), (hist_sx.shape, f32, "v"), (hist_sw.shape, f32, "v")],
            )
        outs = call(
            functools.partial(residual_kernel, first),
            "residual",
            vs(own, other, x, linear_cost, diag) + ss(cols_here, slot) + vs(flipped),
            [panel, x_like] + ([one_tile] if first else []),
            [left],
        )
        sent, resid = outs[:2]
        if first:
            known = outs[2]
        got = exchange(sent)

        sent, image = call(
            functools.partial(scalar_kernel, share),
            "scalars",
            vs(got)
            + ss(rows)
            + vs(start, w, bound_center, bound_width, level, pgw, pgx, resid, diag, hist_gx, hist_gw, qgx, qgw, before),
            [((2, LANES), f32, "v"), w_like],
            sums,
        )
        pair = sent + lax.ppermute(sent, "var", [(i, i ^ 1) for i in range(var_count)])
        copies = jnp.broadcast_to(pair[None], (con_count * var_count // 2, 2, LANES))
        late = lax.all_to_all(copies, ("con", "var"), 0, 0, tiled=True, axis_index_groups=one_core)
        outs = call(
            functools.partial(update_kernel, last, step),
            "update",
            vs(late, known)
            + ss(slot_order, sigma_level)
            + vs(x, px, pgx, resid, hist_x, w, pw, pgw, start, image, bound_center, bound_width, hist_w)
            + vs(*kept)
            + ([] if last else ss(cols_here, slot) + vs(flipped)),
            [x_like, w_like] + ([] if last else [x_like, w_like, x_like, w_like, one_tile, panel]),
            [] if last else [left],
        )
        if last:
            return outs[0], outs[1]
        qgx, qgw = pgx, pgw
        px, pw = x, w
        x, w, pgx, pgw, dx, dw, known, sent = outs
        kept = [dx, dw]
        got = exchange(sent)


def solution(mesh):
    in_specs = (
        P("con", "var", None, None, None),
        P("con", "var", None),
        P("con", "var", None),
        P("var"),
        P(None, "var"),
        P(None, ("con", "var")),
        P(None, ("con", "var")),
        P(("con", "var")),
        P(),
        P(None, "var"),
        P(None, ("con", "var")),
        P(None, "var"),
        P(None, ("con", "var")),
        P(None, "var"),
        P(None, ("con", "var")),
        P(None, None, "var"),
        P(None, None, ("con", "var")),
        P(None, None, "var"),
        P(None, None, ("con", "var")),
        P(),
    )
    out_specs = (P(None, "var"), P(None, ("con", "var")))
    return jax.shard_map(
        per_device, mesh=mesh, in_specs=in_specs, out_specs=out_specs, check_vma=False
    )
```

```python
import functools

import jax
import jax.numpy as jnp
from jax import lax
from jax.experimental import pallas as pl
from jax.experimental.pallas import tpu as pltpu
from jax.sharding import PartitionSpec as P

STEPS = 2
LANES = 128
UNROLL = 72

relax = 1.6
ridge = 0.01

f32 = jnp.float32
bf16 = jnp.bfloat16

U_H, V_H, U_U, U_V, U_P, V_P, V_V, S_S, R_R, C_C, U_D, V_D, SCALARS = 0, 8, 16, 17, 18, 19, 20, 21, 22, 23, 24, 25, 26


MEMORY = 8
LANE_P, LANE_S, LANE_ENTRY = 36, 44, 52


def pair_lane(m, n):
    return m * MEMORY - m * (m - 1) // 2 + n - m


def halves(value):
    high = value.astype(bf16)
    return high, (value - high.astype(f32)).astype(bf16)


def stacked(piece):
    high, low = halves(piece)
    return jnp.concatenate(
        [
            jnp.concatenate([high, high], axis=1),
            jnp.concatenate([low, jnp.zeros_like(low)], axis=1),
        ],
        axis=0,
    )


def times(left, right, contract):
    both = lax.dot_general(left, right, (((1,), (contract,)), ((), ())), preferred_element_type=f32)
    half = both.shape[0] // 2
    return both[:half] + both[half:]


def at(ref, block):
    if isinstance(block, int):
        return block_of(ref, block)
    return ref[:, pl.ds(pl.multiple_of(block * LANES, LANES), LANES)]


def tile_loop(count, body):
    step = max(d for d in range(1, UNROLL + 1) if count % d == 0)

    if step == count:
        for j in range(count):
            body(j)
        return

    def some(i, _):
        for j in range(step):
            body(i * step + j)
        return 0

    lax.fori_loop(0, count // step, some, 0)


def lane_ids(shape):
    return lax.broadcasted_iota(jnp.int32, shape, len(shape) - 1)


def send_products(x_ref, cols, where, tiles, send, left, waits=(None,), flipped=True):
    for block in range(x_ref.shape[1] // LANES):
        left[block] = stacked(x_ref[:, block * LANES : (block + 1) * LANES])
    send[...] = jnp.zeros_like(send)

    def one(t):
        axis = 0 if flipped else 1
        value = times(left[cols[t]], jnp.concatenate(halves(tiles[t]), axis=axis), axis)
        if flipped:
            send[where(t)] = value
        else:
            send[where(t)] = value[: value.shape[0] // 2]
            send[where(t) + 1] = value[value.shape[0] // 2 :]

    size = tiles.shape[0] // len(waits)
    for i, wait in enumerate(waits):
        if wait is not None:
            wait()
        tile_loop(size, lambda t, i=i: one(t + i * size))


def add_rows(received, rows, sums):
    for ref in sums:
        ref[...] = jnp.zeros_like(ref)
    for s in range(rows.shape[0]):
        ref = sums[s % len(sums)]
        row = rows[s]
        ref[row] = ref[row] + received(s)
    return lambda b: functools.reduce(lambda p, q: p + q, [ref[b] for ref in sums])


def block_of(ref, b):
    return ref[:, b * LANES : (b + 1) * LANES]


def rho_of(level_ref, b):
    return 0.4 * (1.0 + block_of(level_ref, b).astype(f32))


def slack_of(w, center, width):
    return jnp.minimum(jnp.maximum(w, center - width), center + width)


def total(value):
    return jnp.sum(value, axis=1, keepdims=True)


def open_kernel(per_run, run_length, share, parts, *refs):
    (hbm_rows, hbm_cols, hbm_x, hbm_tiles, *far), (send, slot, tiles), refs = refs[:10], refs[10:13], refs[13:]
    rows_buf, cols_buf, x, pgx, pgw, hsx, hsw, hgx, hgw, left, count, asked, spot, sem = refs
    memory = hgx.shape[0]
    problems = x.shape[0]
    half = problems // 2
    wide = 2 * per_run + 1
    runs = send.shape[0] // wide
    first = lax.axis_index("con") * share
    mine = pl.ds(pl.multiple_of(first * LANES, LANES), share * LANES)
    far_pgx, far_pgw, far_hsx, far_hsw, far_hgx, far_hgw = far
    size = tiles.shape[0] // parts
    moves = [(hbm_rows, rows_buf), (hbm_cols, cols_buf), (hbm_x, x)]
    moves += [(hbm_tiles.at[pl.ds(i * size, size)], tiles.at[pl.ds(i * size, size)]) for i in range(parts)]
    moves += [(far_pgw, pgw), (far_hsw, hsw), (far_hgw, hgw)]
    moves += [(far_pgx.at[:, mine], pgx), (far_hsx.at[:, :, mine], hsx), (far_hgx.at[:, :, mine], hgx)]
    copies = [pltpu.make_async_copy(a, b, sem.at[i]) for i, (a, b) in enumerate(moves)]
    for copy in copies:
        copy.start()
    rows, cols = rows_buf.at[0], cols_buf.at[0]

    for i in range(runs):
        count[i] = 0
    for i in range(runs * per_run):
        asked[i] = 0
    copies[0].wait()
    copies[1].wait()
    for t in range(tiles.shape[0]):
        row = rows[t]
        owner = row >> (run_length.bit_length() - 1)
        rank = count[owner]
        count[owner] = rank + 1
        place = owner * per_run + rank
        slot[t] = place
        spot[t] = owner * wide + rank * 2
        asked[place] = row & (run_length - 1)

    def where(t):
        return spot[t]

    copies[2].wait()
    places = [(False, b) for b in range(pgw.shape[1] // LANES)] + [(True, b) for b in range(share)]

    def read(ref_x, ref_w, place):
        is_x, b = place
        ref = ref_x if is_x else ref_w
        return ref[..., b * LANES : (b + 1) * LANES]

    acc = {}

    def add(lane, value):
        acc[lane] = acc[lane] + value if lane in acc else value

    def early_sums():
        for copy in copies[2 + parts :]:
            copy.wait()
        for place in places:
            g = [read(hgx.at[m], hgw.at[m], place) for m in range(memory)]
            for m in range(memory):
                for n in range(m, memory):
                    add(pair_lane(m, n), g[m] * g[n])
        for place in places:
            p = read(pgx, pgw, place)
            for m in range(memory):
                add(LANE_P + m, read(hgx.at[m], hgw.at[m], place) * p)
                h = read(hsx.at[m], hsw.at[m], place)
                add(LANE_S + m, h * h)

    send_products(x, cols, where, tiles, send, left, [copy.wait for copy in copies[3 : 2 + parts]] + [early_sums], flipped=False)

    lanes = lane_ids((problems, LANES))
    out = jnp.zeros((problems, LANES), f32)
    for lane, value in acc.items():
        out = jnp.where(lanes == lane, total(value), out)
    index = entry_ids(problems) - lax.axis_index("var") * per_run
    for r in range(runs):
        mark = out
        for i in range(per_run):
            mark = jnp.where(index == i, asked[r * per_run + i].astype(f32), mark)
        turned = pltpu.roll(mark, LANES // 2, 1)
        send[r * wide + 2 * per_run] = jnp.where(lanes[:half] < LANES // 2, mark[:half], turned[half:])


def entry_ids(problems):
    shape = (problems, LANES)
    return (lane_ids(shape) - LANE_ENTRY) * problems + lax.broadcasted_iota(jnp.int32, shape, 0)


def penalty_kernel(first, per_run, *refs):
    if first:
        got, w, center, width, level, send, image, early, rows, marks, marks_int, sem, *sums = refs
    else:
        got, rows, w, center, width, level, send, image, *sums = refs
    slots = send.shape[0]
    runs = slots // per_run
    if first:
        wide = 2 * per_run + 1
        folded = functools.reduce(lambda p, q: p + q, [got[r * wide + 2 * per_run] for r in range(runs)])
        early_sum = jnp.concatenate([folded, pltpu.roll(folded, LANES // 2, 1)], axis=0)
        early[...] = early_sum
        marks_int[...] = early_sum.astype(jnp.int32)
        copy = pltpu.make_async_copy(marks_int, marks, sem)
        copy.start()
        copy.wait()
        problems = w.shape[0]
        for s in range(slots):
            rows[s] = marks[s % problems, LANE_ENTRY + s // problems]

        def received(s):
            unit = s // per_run * wide + s % per_run * 2
            return jnp.concatenate([got[unit], got[unit + 1]], axis=0)

        result = add_rows(received, rows, sums)
    else:
        result = add_rows(lambda s: got[s], rows, sums)
    blocks = w.shape[1] // LANES
    for b in range(blocks):
        start = result(b)
        image[:, b * LANES : (b + 1) * LANES] = start
        here = block_of(w, b)
        slack = slack_of(here, block_of(center, b), block_of(width, b))
        rho = rho_of(level, b)
        sums[0][b] = rho * (slack - start) - rho * (here - slack)
    for s in range(slots):
        send[s] = sums[0][rows[s]]


def transpose_kernel(first, *refs):
    if first:
        back, slot, cols, tiles, early, send, acc = refs
    else:
        back, slot, cols, tiles, send, acc = refs
    acc[...] = jnp.zeros_like(acc)

    def one(t):
        high, low = halves(tiles[t])
        term = times(stacked(back[slot[t]]), jnp.concatenate([high, low], axis=0), 0)
        col = cols[t]
        acc[col] = acc[col] + term

    tile_loop(tiles.shape[0], one)
    columns = acc.shape[0]
    for b in range(columns):
        send[:, b * LANES : (b + 1) * LANES] = acc[b]
    if first:
        send[:, columns * LANES :] = early[...]


def prepare_kernel(tiles, hsx, hgx, hsw, hgw, _, flipped, hx, hw):
    tile_loop(tiles.shape[0], lambda t: flipped.__setitem__(t, tiles[t].T))
    for m in range(hx.shape[0]):
        hx[m] = hsx[m] + hgx[m]
        hw[m] = hsw[m] + hgw[m]


def residual_kernel(first, own, other, x, linear, diag, cols, slot, tiles, send, resid, *refs):
    columns = x.shape[1] // LANES
    if first:
        early, left = refs
    else:
        (left,) = refs
    for b in range(columns):
        lo, hi = b * LANES, (b + 1) * LANES
        value = -linear[:, lo:hi] - diag[:, lo:hi] * x[:, lo:hi]
        resid[:, lo:hi] = value + (own[:, lo:hi] + other[:, lo:hi])
    if first:
        early[...] = own[:, columns * LANES :] + other[:, columns * LANES :]
    send_products(resid, cols, lambda t: slot[t], tiles, send, left)


class Sums:
    def __init__(self, problems):
        self.shape = (problems, LANES)
        self.acc = {}

    def add(self, i, value):
        self.acc[i] = self.acc[i] + value if i in self.acc else value

    def tiles(self, tiles):
        turn = (LANES - 16 * lax.broadcasted_iota(jnp.int32, self.shape, 0)) & (LANES - 1)
        lanes = lane_ids(self.shape)
        tiles = list(tiles)
        for i, value in self.acc.items():
            tiles[i // 16] = jnp.where(lanes == turn + i % 16, total(value), tiles[i // 16])
        return tiles


def blocks_of(w, share):
    first = lax.axis_index("con") * share
    return [(False, b) for b in range(w.shape[1] // LANES)] + [(True, first + b) for b in range(share)]


def scalar_kernel(
    share, got, rows, start, w, center, width, level, pw, pgw, x, px, pgx, resid, diag, hgx, hgw, qgx, qgw, send, image, *scratch
):
    result = add_rows(lambda s: got[s], rows, scratch)
    sums = Sums(w.shape[0])
    for is_x, b in blocks_of(w, share):
        if is_x:
            r, p = at(resid, b), at(pgx, b)
            u, v, s, d = -p, relax * r, at(x, b) - at(px, b), p - at(qgx, b)
            sums.add(R_R, r * r)
            sums.add(C_C, at(diag, b) * r * r)
        else:
            ar, p = result(b), block_of(pgw, b)
            image[:, b * LANES : (b + 1) * LANES] = ar
            here = block_of(w, b)
            slack = slack_of(here, block_of(center, b), block_of(width, b))
            u, v, s, d = relax * (block_of(start, b) - slack) - p, relax * ar, here - block_of(pw, b), p - block_of(qgw, b)
            sums.add(C_C, rho_of(level, b) * ar * ar)
        for m in range(MEMORY):
            h = at(hgx.at[m] if is_x else hgw.at[m], b)
            sums.add(U_H + m, u * h)
            sums.add(V_H + m, v * h)
        for i, value in ((U_U, u * u), (U_V, u * v), (U_P, u * p), (V_P, v * p), (V_V, v * v), (S_S, s * s), (U_D, u * d), (V_D, v * d)):
            sums.add(i, value)
    zero = jnp.zeros(sums.shape, f32)
    rows_out = [jnp.sum(tile, axis=0, keepdims=True) for tile in sums.tiles([zero, zero])]
    send[...] = jnp.concatenate(rows_out, axis=0)


def update_kernel(last, steps_before, *refs):
    (late, known, order, sigma_level, x, px, pgx, resid, hx) = refs[:9]
    (w, pw, pgw, start, image, center, width, hw) = refs[9:17]
    refs = refs[17:]
    if steps_before:
        dx, dw = refs[:2]
        refs = refs[2:]
    if last:
        x_out, w_out = refs
    else:
        cols, slot, tiles, x_out, w_out, gx_out, gw_out, dx_out, dw_out, known_out, send, left = refs
    problems = x.shape[0]
    memory = hx.shape[0]
    shape = (problems, LANES)
    lanes = lane_ids(shape)
    program = lax.broadcasted_iota(jnp.int32, shape, 0)
    chains = [late[i] for i in range(min(8, late.shape[0]))]
    for i in range(len(chains), late.shape[0]):
        chains[i % 8] = chains[i % 8] + late[i]
    rows = functools.reduce(lambda p, q: p + q, chains)

    aligned = [
        pltpu.roll(jnp.broadcast_to(rows[i : i + 1], shape), 0, 1, stride=16, stride_axis=0) for i in range(2)
    ]

    def scalar(i):
        return jnp.broadcast_to(aligned[i // 16][:, i % 16 : i % 16 + 1], shape)

    def given(i):
        return jnp.broadcast_to(known[:, i : i + 1], shape)

    new = [jnp.where(order[steps_before] == m, 1.0, 0.0) for m in range(memory)]
    keep = [1.0 - f for f in new]
    if steps_before:
        old = [jnp.where(order[0] == m, 1.0, 0.0) for m in range(memory)]
    sigma = jnp.zeros(shape, f32)
    for k in range(problems):
        sigma = jnp.where(program == k, 0.2 * (1.0 + sigma_level[k].astype(f32)), sigma)
    norm = scalar(R_R)
    step = norm / (scalar(C_C) + sigma * norm)
    u_h = [scalar(U_H + m) for m in range(memory)]
    v_h = [scalar(V_H + m) for m in range(memory)]
    if steps_before:
        u_d, v_d = scalar(U_D), scalar(V_D)
        u_h = [h * (1.0 - f) + u_d * f for h, f in zip(u_h, old)]
        v_h = [h * (1.0 - f) + v_d * f for h, f in zip(v_h, old)]
    dot = [u + step * v for u, v in zip(u_h, v_h)]
    own = scalar(U_U) + 2.0 * step * scalar(U_V) + step * step * scalar(V_V)
    with_p = scalar(U_P) + step * scalar(V_P)
    gram = [[None] * memory for _ in range(memory)]
    for m in range(memory):
        gram[m][m] = given(pair_lane(m, m)) * keep[m] + own * new[m]
        for n in range(m + 1, memory):
            value = given(pair_lane(m, n)) * (keep[m] * keep[n]) + dot[n] * new[m] + dot[m] * new[n]
            gram[m][n] = gram[n][m] = value
    rhs = []
    for m in range(memory):
        value = given(LANE_P + m) * keep[m] + with_p * new[m]
        for n in range(memory):
            value = value + gram[m][n] * new[n]
        rhs.append(value)
    s_s = scalar(S_S)
    squares = [given(LANE_S + m) * keep[m] + s_s * new[m] for m in range(memory)]
    frob = functools.reduce(lambda p, q: p + q, squares + [gram[m][m] for m in range(memory)])
    damp = ridge * frob
    if not last:
        out = jnp.zeros(shape, f32)
        for m in range(memory):
            for n in range(m, memory):
                out = jnp.where(lanes == pair_lane(m, n), gram[m][n], out)
            out = jnp.where(lanes == LANE_P + m, rhs[m], out)
            out = jnp.where(lanes == LANE_S + m, squares[m], out)
        known_out[...] = out
    low = [[None] * memory for _ in range(memory)]
    inverse = []
    for j in range(memory):
        value = gram[j][j] + damp
        for k in range(j):
            value = value - low[j][k] * low[j][k]
        inverse.append(1.0 / jnp.sqrt(value))
        for i in range(j + 1, memory):
            value = gram[i][j]
            for k in range(j):
                value = value - low[i][k] * low[j][k]
            low[i][j] = value * inverse[j]
    half = []
    for i in range(memory):
        value = rhs[i]
        for k in range(i):
            value = value - low[i][k] * half[k]
        half.append(value * inverse[i])
    coef = [None] * memory
    for i in reversed(range(memory)):
        value = half[i]
        for k in range(i + 1, memory):
            value = value - low[k][i] * coef[k]
        coef[i] = value * inverse[i]

    newest = functools.reduce(lambda p, q: p + q, [c * f for c, f in zip(coef, new)])
    left_over = [c * f for c, f in zip(coef, keep)]
    if steps_before:
        older = functools.reduce(lambda p, q: p + q, [c * f for c, f in zip(left_over, old)])
        left_over = [c * (1.0 - f) for c, f in zip(left_over, old)]

    scaled = relax * step
    older = older if steps_before else None
    for b in range(x.shape[1] // LANES):
        g = scaled * block_of(resid, b)
        advance(b, newest, left_over, older, x, px, g, pgx, hx, dx if steps_before else None, x_out, None if last else gx_out, None if last else dx_out)
    for b in range(w.shape[1] // LANES):
        slack = slack_of(block_of(w, b), block_of(center, b), block_of(width, b))
        g = relax * (block_of(start, b) + step * block_of(image, b) - slack)
        advance(b, newest, left_over, older, w, pw, g, pgw, hw, dw if steps_before else None, w_out, None if last else gw_out, None if last else dw_out)
    if not last:
        send_products(x_out, cols, lambda t: slot[t], tiles, send, left)


def advance(b, newest, left_over, older, state, previous, g, previous_g, hist, kept, out, g_out, d_out):
    lo, hi = b * LANES, (b + 1) * LANES
    here = state[:, lo:hi]
    fresh = (here - previous[:, lo:hi]) + (g - previous_g[:, lo:hi])
    value = here + g - newest * fresh
    for m in range(len(left_over)):
        value = value - left_over[m] * hist[m, :, lo:hi]
    if kept is not None:
        value = value - older * kept[:, lo:hi]
    out[:, lo:hi] = value
    if g_out is not None:
        g_out[:, lo:hi] = g
        d_out[:, lo:hi] = fresh


def call(kernel, name, ins, outs, scratch=()):
    spaces = {"v": pltpu.VMEM, "s": pltpu.SMEM, "h": pltpu.HBM}
    return pl.pallas_call(
        kernel,
        out_shape=[jax.ShapeDtypeStruct(shape, dtype) for shape, dtype, _ in outs],
        in_specs=[pl.BlockSpec(memory_space=spaces[space]) for _, space in ins],
        out_specs=[pl.BlockSpec(memory_space=spaces[space]) for _, _, space in outs],
        scratch_shapes=list(scratch),
        compiler_params=pltpu.CompilerParams(vmem_limit_bytes=24 * 1024 * 1024),
        name=name,
    )(*[array for array, _ in ins])


def per_device(
    tiles,
    row_tile,
    col_tile,
    diag_cost,
    linear_cost,
    bound_center,
    bound_width,
    rho_level,
    sigma_level,
    state_x,
    state_w,
    prev_x,
    prev_w,
    prev_gx,
    prev_gw,
    hist_sx,
    hist_sw,
    hist_gx,
    hist_gw,
    slot_order,
):
    problems, var_cols = state_x.shape
    con_cols = state_w.shape[1]
    tile_size = tiles.shape[-1]
    var_count, con_count = lax.axis_size("var"), lax.axis_size("con")
    col_count = var_cols // tile_size
    run_length = con_cols // tile_size
    blocks = tiles.reshape(-1, tile_size, tile_size)
    count = blocks.shape[0]
    per_run = -(-count // var_count)
    slots = var_count * per_run
    rows_here = row_tile.reshape(-1)
    cols_here = col_tile.reshape(-1)
    diag = diag_cost.reshape(1, -1)
    level = rho_level.reshape(1, -1)

    x_like = ((problems, var_cols), f32, "v")
    w_like = ((problems, con_cols), f32, "v")
    panel = ((slots, problems, tile_size), f32, "v")
    wide_panel = (((2 * per_run + 1) * var_count, problems // 2, tile_size), f32, "v")
    one_tile = ((problems, tile_size), f32, "v")
    left = pltpu.VMEM((col_count, 2 * problems, 2 * tile_size), bf16)
    sums = [pltpu.VMEM((run_length, problems, tile_size), f32)] * 4
    bounds = [(bound_center, "v"), (bound_width, "v")]
    vs = lambda *arrays: [(a, "v") for a in arrays]
    ss = lambda *arrays: [(a, "s") for a in arrays]

    def exchange(x):
        return lax.all_to_all(x, "var", 0, 0, tiled=True)

    def over_con(x):
        def partner(x, k):
            return lax.ppermute(x, "con", [(i, i ^ k) for i in range(con_count)])

        others = [partner(x, k) for k in range(2, con_count, 2)]
        terms = [x] + others
        while len(terms) > 1:
            terms = [a + b for a, b in zip(terms[::2], terms[1::2])]
        return terms[0], partner(terms[0], 1)

    one_core = [list(range(k, con_count * var_count, 2)) for k in range(2)]
    share = col_count // con_count
    parts = max(d for d in range(1, 4) if count % d == 0)
    far = [state_x, blocks, prev_gx, prev_gw, hist_sx, hist_sw, hist_gx, hist_gw]
    x_mine, w_mine = pltpu.VMEM((problems, share * tile_size), f32), pltpu.VMEM((problems, con_cols), f32)
    memory = hist_gx.shape[0]
    hx_mine = pltpu.VMEM((memory, problems, share * tile_size), f32)
    hw_mine = pltpu.VMEM((memory, problems, con_cols), f32)
    sent, slot, blocks = call(
        functools.partial(open_kernel, per_run, run_length, share, parts),
        "open",
        [(pltpu.with_memory_space_constraint(a, pltpu.HBM), "h") for a in [row_tile[0], col_tile[0]] + far],
        [wide_panel, ((count,), jnp.int32, "s"), (blocks.shape, f32, "v")],
        [
            pltpu.SMEM((1, count), jnp.int32),
            pltpu.SMEM((1, count), jnp.int32),
            pltpu.VMEM((problems, var_cols), f32),
            x_mine, w_mine, hx_mine, hw_mine, hx_mine, hw_mine,
            left,
            pltpu.SMEM((var_count,), jnp.int32),
            pltpu.SMEM((slots,), jnp.int32),
            pltpu.SMEM((count,), jnp.int32),
            pltpu.SemaphoreType.DMA((3 + parts + 6,)),
        ],
    )
    got = exchange(sent)
    x, w, px, pw, pgx, pgw = state_x, state_w, prev_x, prev_w, prev_gx, prev_gw
    qgx, qgw = pgx, pgw
    kept = []
    known = None
    for step in range(STEPS):
        first, last = step == 0, step == STEPS - 1
        if first:
            sent, start, early, rows = call(
                functools.partial(penalty_kernel, True, per_run),
                "penalty_first",
                vs(got, w, bound_center, bound_width, level),
                [panel, w_like, one_tile, ((slots,), jnp.int32, "s")],
                [pltpu.SMEM((problems, tile_size), jnp.int32), pltpu.VMEM((problems, tile_size), jnp.int32), pltpu.SemaphoreType.DMA(())]
                + sums,
            )
        else:
            sent, start = call(
                functools.partial(penalty_kernel, False, per_run),
                "penalty",
                vs(got) + ss(rows) + vs(w, bound_center, bound_width, level),
                [panel, w_like],
                sums,
            )
        back = exchange(sent)
        width = var_cols + (tile_size if first else 0)
        (sent,) = call(
            functools.partial(transpose_kernel, first),
            "transpose",
            vs(back) + ss(slot, cols_here) + vs(blocks) + (vs(early) if first else []),
            [((problems, width), f32, "v")],
            [pltpu.VMEM((col_count, problems, tile_size), f32)],
        )
        own, other = over_con(sent)
        if first:
            flipped, hist_x, hist_w = call(
                prepare_kernel,
                "prepare",
                vs(blocks, hist_sx, hist_gx, hist_sw, hist_gw, sent),
                [(blocks.shape, f32, "v"), (hist_sx.shape, f32, "v"), (hist_sw.shape, f32, "v")],
            )
        outs = call(
            functools.partial(residual_kernel, first),
            "residual",
            vs(own, other, x, linear_cost, diag) + ss(cols_here, slot) + vs(flipped),
            [panel, x_like] + ([one_tile] if first else []),
            [left],
        )
        sent, resid = outs[:2]
        if first:
            known = outs[2]
        got = exchange(sent)

        sent, image = call(
            functools.partial(scalar_kernel, share),
            "scalars",
            vs(got)
            + ss(rows)
            + vs(start, w, bound_center, bound_width, level, pw, pgw, x, px, pgx, resid, diag, hist_gx, hist_gw, qgx, qgw),
            [((2, LANES), f32, "v"), w_like],
            sums,
        )
        pair = sent + lax.ppermute(sent, "var", [(i, i ^ 1) for i in range(var_count)])
        copies = jnp.broadcast_to(pair[None], (con_count * var_count // 2, 2, LANES))
        late = lax.all_to_all(copies, ("con", "var"), 0, 0, tiled=True, axis_index_groups=one_core)
        outs = call(
            functools.partial(update_kernel, last, step),
            "update",
            vs(late, known)
            + ss(slot_order, sigma_level)
            + vs(x, px, pgx, resid, hist_x, w, pw, pgw, start, image, bound_center, bound_width, hist_w)
            + vs(*kept)
            + ([] if last else ss(cols_here, slot) + vs(flipped)),
            [x_like, w_like] + ([] if last else [x_like, w_like, x_like, w_like, one_tile, panel]),
            [] if last else [left],
        )
        if last:
            return outs[0], outs[1]
        qgx, qgw = pgx, pgw
        px, pw = x, w
        x, w, pgx, pgw, dx, dw, known, sent = outs
        kept = [dx, dw]
        got = exchange(sent)


def solution(mesh):
    in_specs = (
        P("con", "var", None, None, None),
        P("con", "var", None),
        P("con", "var", None),
        P("var"),
        P(None, "var"),
        P(None, ("con", "var")),
        P(None, ("con", "var")),
        P(("con", "var")),
        P(),
        P(None, "var"),
        P(None, ("con", "var")),
        P(None, "var"),
        P(None, ("con", "var")),
        P(None, "var"),
        P(None, ("con", "var")),
        P(None, None, "var"),
        P(None, None, ("con", "var")),
        P(None, None, "var"),
        P(None, None, ("con", "var")),
        P(),
    )
    out_specs = (P(None, "var"), P(None, ("con", "var")))
    return jax.shard_map(
        per_device, mesh=mesh, in_specs=in_specs, out_specs=out_specs, check_vma=False
    )
```

```python
import functools

import jax
import jax.numpy as jnp
from jax import lax
from jax.experimental import pallas as pl
from jax.experimental.pallas import tpu as pltpu
from jax.sharding import PartitionSpec as P

STEPS = 2
LANES = 128
UNROLL = 72

relax = 1.6
ridge = 0.01

f32 = jnp.float32
bf16 = jnp.bfloat16

U_H, V_H, U_U, U_V, U_P, V_P, V_V, S_S, R_R, C_C, U_D, V_D, SCALARS = 0, 8, 16, 17, 18, 19, 20, 21, 22, 23, 24, 25, 26


MEMORY = 8
LANE_P, LANE_S, LANE_ENTRY = 36, 44, 52


def pair_lane(m, n):
    return m * MEMORY - m * (m - 1) // 2 + n - m


def halves(value):
    high = value.astype(bf16)
    return high, (value - high.astype(f32)).astype(bf16)


def stacked(piece):
    high, low = halves(piece)
    return jnp.concatenate(
        [
            jnp.concatenate([high, high], axis=1),
            jnp.concatenate([low, jnp.zeros_like(low)], axis=1),
        ],
        axis=0,
    )


def times(left, right, contract):
    both = lax.dot_general(left, right, (((1,), (contract,)), ((), ())), preferred_element_type=f32)
    half = both.shape[0] // 2
    return both[:half] + both[half:]


def at(ref, block):
    if isinstance(block, int):
        return block_of(ref, block)
    return ref[:, pl.ds(pl.multiple_of(block * LANES, LANES), LANES)]


def tile_loop(count, body):
    step = max(d for d in range(1, UNROLL + 1) if count % d == 0)

    if step == count:
        for j in range(count):
            body(j)
        return

    def some(i, _):
        for j in range(step):
            body(i * step + j)
        return 0

    lax.fori_loop(0, count // step, some, 0)


def lane_ids(shape):
    return lax.broadcasted_iota(jnp.int32, shape, len(shape) - 1)


def send_products(x_ref, cols, where, tiles, send, left, waits=(None,), flipped=True):
    for block in range(x_ref.shape[1] // LANES):
        left[block] = stacked(x_ref[:, block * LANES : (block + 1) * LANES])
    send[...] = jnp.zeros_like(send)

    def one(t):
        axis = 0 if flipped else 1
        value = times(left[cols[t]], jnp.concatenate(halves(tiles[t]), axis=axis), axis)
        spot = where(t)
        if flipped:
            send[spot] = value
        else:
            send[spot] = value[: value.shape[0] // 2]
            send[spot + 1] = value[value.shape[0] // 2 :]

    size = tiles.shape[0] // len(waits)
    for i, wait in enumerate(waits):
        if wait is not None:
            wait()
        tile_loop(size, lambda t, i=i: one(t + i * size))


def add_rows(received, row_of, slots, sums):
    for s in range(slots):
        ref = sums[s % len(sums)]
        row = row_of(s)
        ref[row] = ref[row] + received(s)
    return lambda b: functools.reduce(lambda p, q: p + q, [ref[b] for ref in sums])


def block_of(ref, b):
    return ref[:, b * LANES : (b + 1) * LANES]


def rho_of(level_ref, b):
    return 0.4 * (1.0 + block_of(level_ref, b).astype(f32))


def slack_of(w, center, width):
    return jnp.minimum(jnp.maximum(w, center - width), center + width)


def total(value):
    return jnp.sum(value, axis=1, keepdims=True)


def open_kernel(per_run, run_length, share, parts, *refs):
    (hbm_rows, hbm_cols, hbm_x, hbm_tiles, *far), (send, slot, tiles), refs = refs[:10], refs[10:13], refs[13:]
    rows_buf, cols_buf, x, pgx, pgw, hsx, hsw, hgx, hgw, left, count, asked, sem = refs
    memory = hgx.shape[0]
    problems = x.shape[0]
    half = problems // 2
    wide = 2 * per_run + 1
    runs = send.shape[0] // wide
    first = lax.axis_index("con") * share
    mine = pl.ds(pl.multiple_of(first * LANES, LANES), share * LANES)
    far_pgx, far_pgw, far_hsx, far_hsw, far_hgx, far_hgw = far
    size = tiles.shape[0] // parts
    moves = [(hbm_rows, rows_buf), (hbm_cols, cols_buf), (hbm_x, x)]
    moves += [(hbm_tiles.at[pl.ds(i * size, size)], tiles.at[pl.ds(i * size, size)]) for i in range(parts)]
    moves += [(far_pgw, pgw), (far_hsw, hsw), (far_hgw, hgw)]
    moves += [(far_pgx.at[:, mine], pgx), (far_hsx.at[:, :, mine], hsx), (far_hgx.at[:, :, mine], hgx)]
    copies = [pltpu.make_async_copy(a, b, sem.at[i]) for i, (a, b) in enumerate(moves)]
    for copy in copies:
        copy.start()
    rows, cols = rows_buf.at[0], cols_buf.at[0]

    for i in range(runs):
        count[i] = 0
    for i in range(runs * per_run):
        asked[i] = 0
    def where(t):
        row = rows[t]
        owner = row >> (run_length.bit_length() - 1)
        rank = count[owner]
        count[owner] = rank + 1
        place = owner * per_run + rank
        slot[t] = place
        asked[place] = row & (run_length - 1)
        return owner * wide + rank * 2

    for copy in copies[:3]:
        copy.wait()
    places = [(False, b) for b in range(pgw.shape[1] // LANES)] + [(True, b) for b in range(share)]

    def read(ref_x, ref_w, place):
        is_x, b = place
        ref = ref_x if is_x else ref_w
        return ref[..., b * LANES : (b + 1) * LANES]

    acc = {}

    def add(lane, value):
        acc[lane] = acc[lane] + value if lane in acc else value

    def early_sums():
        for copy in copies[2 + parts :]:
            copy.wait()
        for place in places:
            g = [read(hgx.at[m], hgw.at[m], place) for m in range(memory)]
            for m in range(memory):
                for n in range(m, memory):
                    add(pair_lane(m, n), g[m] * g[n])
        for place in places:
            p = read(pgx, pgw, place)
            for m in range(memory):
                add(LANE_P + m, read(hgx.at[m], hgw.at[m], place) * p)
                h = read(hsx.at[m], hsw.at[m], place)
                add(LANE_S + m, h * h)

    send_products(x, cols, where, tiles, send, left, [copy.wait for copy in copies[3 : 2 + parts]] + [early_sums], flipped=False)

    lanes = lane_ids((problems, LANES))
    out = jnp.zeros((problems, LANES), f32)
    for lane, value in acc.items():
        out = jnp.where(lanes == lane, total(value), out)
    index = entry_ids(problems) - lax.axis_index("var") * per_run
    for r in range(runs):
        mark = out
        for i in range(per_run):
            mark = jnp.where(index == i, asked[r * per_run + i].astype(f32), mark)
        turned = pltpu.roll(mark, LANES // 2, 1)
        send[r * wide + 2 * per_run] = jnp.where(lanes[:half] < LANES // 2, mark[:half], turned[half:])


def entry_ids(problems):
    shape = (problems, LANES)
    return (lane_ids(shape) - LANE_ENTRY) * problems + lax.broadcasted_iota(jnp.int32, shape, 0)


def penalty_kernel(first, per_run, *refs):
    if first:
        got, w, center, width, level, send, image, early, rows, marks, marks_int, sem, *sums = refs
    else:
        got, rows, w, center, width, level, send, image, *sums = refs
    slots = send.shape[0]
    runs = slots // per_run
    if first:
        wide = 2 * per_run + 1
        folded = functools.reduce(lambda p, q: p + q, [got[r * wide + 2 * per_run] for r in range(runs)])
        early_sum = jnp.concatenate([folded, pltpu.roll(folded, LANES // 2, 1)], axis=0)
        early[...] = early_sum
        marks_int[...] = early_sum.astype(jnp.int32)
        copy = pltpu.make_async_copy(marks_int, marks, sem)
        copy.start()
        for ref in sums:
            ref[...] = jnp.zeros_like(ref)
        problems = w.shape[0]
        copy.wait()

        def row_of(s):
            row = marks[s % problems, LANE_ENTRY + s // problems]
            rows[s] = row
            return row

        def received(s):
            unit = s // per_run * wide + s % per_run * 2
            return jnp.concatenate([got[unit], got[unit + 1]], axis=0)

        result = add_rows(received, row_of, slots, sums)
    else:
        for ref in sums:
            ref[...] = jnp.zeros_like(ref)
        result = add_rows(lambda s: got[s], lambda s: rows[s], slots, sums)
    blocks = w.shape[1] // LANES
    for b in range(blocks):
        start = result(b)
        image[:, b * LANES : (b + 1) * LANES] = start
        here = block_of(w, b)
        slack = slack_of(here, block_of(center, b), block_of(width, b))
        rho = rho_of(level, b)
        sums[0][b] = rho * (slack - start) - rho * (here - slack)
    for s in range(slots):
        send[s] = sums[0][rows[s]]


def transpose_kernel(first, *refs):
    if first:
        back, slot, cols, tiles, early, send, acc = refs
    else:
        back, slot, cols, tiles, send, acc = refs
    acc[...] = jnp.zeros_like(acc)

    def one(t):
        high, low = halves(tiles[t])
        term = times(stacked(back[slot[t]]), jnp.concatenate([high, low], axis=0), 0)
        col = cols[t]
        acc[col] = acc[col] + term

    tile_loop(tiles.shape[0], one)
    columns = acc.shape[0]
    for b in range(columns):
        send[:, b * LANES : (b + 1) * LANES] = acc[b]
    if first:
        send[:, columns * LANES :] = early[...]


def prepare_kernel(tiles, hsx, hgx, hsw, hgw, _, flipped, hx, hw):
    tile_loop(tiles.shape[0], lambda t: flipped.__setitem__(t, tiles[t].T))
    for m in range(hx.shape[0]):
        hx[m] = hsx[m] + hgx[m]
        hw[m] = hsw[m] + hgw[m]


def residual_kernel(first, own, other, x, linear, diag, cols, slot, tiles, send, resid, *refs):
    columns = x.shape[1] // LANES
    if first:
        early, left = refs
    else:
        (left,) = refs
    for b in range(columns):
        lo, hi = b * LANES, (b + 1) * LANES
        value = -linear[:, lo:hi] - diag[:, lo:hi] * x[:, lo:hi]
        resid[:, lo:hi] = value + (own[:, lo:hi] + other[:, lo:hi])
    if first:
        early[...] = own[:, columns * LANES :] + other[:, columns * LANES :]
    send_products(resid, cols, lambda t: slot[t], tiles, send, left)


class Sums:
    def __init__(self, problems):
        self.shape = (problems, LANES)
        self.acc = {}

    def add(self, i, value):
        self.acc[i] = self.acc[i] + value if i in self.acc else value

    def tiles(self, tiles):
        turn = (LANES - 16 * lax.broadcasted_iota(jnp.int32, self.shape, 0)) & (LANES - 1)
        lanes = lane_ids(self.shape)
        tiles = list(tiles)
        for i, value in self.acc.items():
            tiles[i // 16] = jnp.where(lanes == turn + i % 16, total(value), tiles[i // 16])
        return tiles


def blocks_of(w, share):
    first = lax.axis_index("con") * share
    return [(False, b) for b in range(w.shape[1] // LANES)] + [(True, first + b) for b in range(share)]


def scalar_kernel(
    share, got, rows, start, w, center, width, level, pw, pgw, x, px, pgx, resid, diag, hgx, hgw, qgx, qgw, send, image, *scratch
):
    for ref in scratch:
        ref[...] = jnp.zeros_like(ref)
    result = add_rows(lambda s: got[s], lambda s: rows[s], rows.shape[0], scratch)
    sums = Sums(w.shape[0])
    for is_x, b in blocks_of(w, share):
        if is_x:
            r, p = at(resid, b), at(pgx, b)
            u, v, s, d = -p, relax * r, at(x, b) - at(px, b), p - at(qgx, b)
            sums.add(R_R, r * r)
            sums.add(C_C, at(diag, b) * r * r)
        else:
            ar, p = result(b), block_of(pgw, b)
            image[:, b * LANES : (b + 1) * LANES] = ar
            here = block_of(w, b)
            slack = slack_of(here, block_of(center, b), block_of(width, b))
            u, v, s, d = relax * (block_of(start, b) - slack) - p, relax * ar, here - block_of(pw, b), p - block_of(qgw, b)
            sums.add(C_C, rho_of(level, b) * ar * ar)
        for m in range(MEMORY):
            h = at(hgx.at[m] if is_x else hgw.at[m], b)
            sums.add(U_H + m, u * h)
            sums.add(V_H + m, v * h)
        for i, value in ((U_U, u * u), (U_V, u * v), (U_P, u * p), (V_P, v * p), (V_V, v * v), (S_S, s * s), (U_D, u * d), (V_D, v * d)):
            sums.add(i, value)
    zero = jnp.zeros(sums.shape, f32)
    rows_out = [jnp.sum(tile, axis=0, keepdims=True) for tile in sums.tiles([zero, zero])]
    send[...] = jnp.concatenate(rows_out, axis=0)


def update_kernel(last, steps_before, *refs):
    (late, known, order, sigma_level, x, px, pgx, resid, hx) = refs[:9]
    (w, pw, pgw, start, image, center, width, hw) = refs[9:17]
    refs = refs[17:]
    if steps_before:
        dx, dw = refs[:2]
        refs = refs[2:]
    if last:
        x_out, w_out = refs
    else:
        cols, slot, tiles, x_out, w_out, gx_out, gw_out, dx_out, dw_out, known_out, send, left = refs
    problems = x.shape[0]
    memory = hx.shape[0]
    shape = (problems, LANES)
    lanes = lane_ids(shape)
    program = lax.broadcasted_iota(jnp.int32, shape, 0)
    chains = [late[i] for i in range(min(8, late.shape[0]))]
    for i in range(len(chains), late.shape[0]):
        chains[i % 8] = chains[i % 8] + late[i]
    rows = functools.reduce(lambda p, q: p + q, chains)

    aligned = [
        pltpu.roll(jnp.broadcast_to(rows[i : i + 1], shape), 0, 1, stride=16, stride_axis=0) for i in range(2)
    ]

    def scalar(i):
        return jnp.broadcast_to(aligned[i // 16][:, i % 16 : i % 16 + 1], shape)

    def given(i):
        return jnp.broadcast_to(known[:, i : i + 1], shape)

    new = [jnp.where(order[steps_before] == m, 1.0, 0.0) for m in range(memory)]
    keep = [1.0 - f for f in new]
    if steps_before:
        old = [jnp.where(order[0] == m, 1.0, 0.0) for m in range(memory)]
    sigma = jnp.zeros(shape, f32)
    for k in range(problems):
        sigma = jnp.where(program == k, 0.2 * (1.0 + sigma_level[k].astype(f32)), sigma)
    norm = scalar(R_R)
    step = norm / (scalar(C_C) + sigma * norm)
    u_h = [scalar(U_H + m) for m in range(memory)]
    v_h = [scalar(V_H + m) for m in range(memory)]
    if steps_before:
        u_d, v_d = scalar(U_D), scalar(V_D)
        u_h = [h * (1.0 - f) + u_d * f for h, f in zip(u_h, old)]
        v_h = [h * (1.0 - f) + v_d * f for h, f in zip(v_h, old)]
    dot = [u + step * v for u, v in zip(u_h, v_h)]
    own = scalar(U_U) + 2.0 * step * scalar(U_V) + step * step * scalar(V_V)
    with_p = scalar(U_P) + step * scalar(V_P)
    gram = [[None] * memory for _ in range(memory)]
    for m in range(memory):
        gram[m][m] = given(pair_lane(m, m)) * keep[m] + own * new[m]
        for n in range(m + 1, memory):
            value = given(pair_lane(m, n)) * (keep[m] * keep[n]) + dot[n] * new[m] + dot[m] * new[n]
            gram[m][n] = gram[n][m] = value
    rhs = []
    for m in range(memory):
        value = given(LANE_P + m) * keep[m] + with_p * new[m]
        for n in range(memory):
            value = value + gram[m][n] * new[n]
        rhs.append(value)
    s_s = scalar(S_S)
    squares = [given(LANE_S + m) * keep[m] + s_s * new[m] for m in range(memory)]
    frob = functools.reduce(lambda p, q: p + q, squares + [gram[m][m] for m in range(memory)])
    damp = ridge * frob
    if not last:
        out = jnp.zeros(shape, f32)
        for m in range(memory):
            for n in range(m, memory):
                out = jnp.where(lanes == pair_lane(m, n), gram[m][n], out)
            out = jnp.where(lanes == LANE_P + m, rhs[m], out)
            out = jnp.where(lanes == LANE_S + m, squares[m], out)
        known_out[...] = out
    low = [[None] * memory for _ in range(memory)]
    inverse = []
    for j in range(memory):
        value = gram[j][j] + damp
        for k in range(j):
            value = value - low[j][k] * low[j][k]
        inverse.append(1.0 / jnp.sqrt(value))
        for i in range(j + 1, memory):
            value = gram[i][j]
            for k in range(j):
                value = value - low[i][k] * low[j][k]
            low[i][j] = value * inverse[j]
    half = []
    for i in range(memory):
        value = rhs[i]
        for k in range(i):
            value = value - low[i][k] * half[k]
        half.append(value * inverse[i])
    coef = [None] * memory
    for i in reversed(range(memory)):
        value = half[i]
        for k in range(i + 1, memory):
            value = value - low[k][i] * coef[k]
        coef[i] = value * inverse[i]

    newest = functools.reduce(lambda p, q: p + q, [c * f for c, f in zip(coef, new)])
    left_over = [c * f for c, f in zip(coef, keep)]
    if steps_before:
        older = functools.reduce(lambda p, q: p + q, [c * f for c, f in zip(left_over, old)])
        left_over = [c * (1.0 - f) for c, f in zip(left_over, old)]

    scaled = relax * step
    older = older if steps_before else None
    for b in range(x.shape[1] // LANES):
        g = scaled * block_of(resid, b)
        advance(b, newest, left_over, older, x, px, g, pgx, hx, dx if steps_before else None, x_out, None if last else gx_out, None if last else dx_out)
    for b in range(w.shape[1] // LANES):
        slack = slack_of(block_of(w, b), block_of(center, b), block_of(width, b))
        g = relax * (block_of(start, b) + step * block_of(image, b) - slack)
        advance(b, newest, left_over, older, w, pw, g, pgw, hw, dw if steps_before else None, w_out, None if last else gw_out, None if last else dw_out)
    if not last:
        send_products(x_out, cols, lambda t: slot[t], tiles, send, left)


def advance(b, newest, left_over, older, state, previous, g, previous_g, hist, kept, out, g_out, d_out):
    lo, hi = b * LANES, (b + 1) * LANES
    here = state[:, lo:hi]
    fresh = (here - previous[:, lo:hi]) + (g - previous_g[:, lo:hi])
    value = here + g - newest * fresh
    for m in range(len(left_over)):
        value = value - left_over[m] * hist[m, :, lo:hi]
    if kept is not None:
        value = value - older * kept[:, lo:hi]
    out[:, lo:hi] = value
    if g_out is not None:
        g_out[:, lo:hi] = g
        d_out[:, lo:hi] = fresh


def call(kernel, name, ins, outs, scratch=()):
    spaces = {"v": pltpu.VMEM, "s": pltpu.SMEM, "h": pltpu.HBM}
    return pl.pallas_call(
        kernel,
        out_shape=[jax.ShapeDtypeStruct(shape, dtype) for shape, dtype, _ in outs],
        in_specs=[pl.BlockSpec(memory_space=spaces[space]) for _, space in ins],
        out_specs=[pl.BlockSpec(memory_space=spaces[space]) for _, _, space in outs],
        scratch_shapes=list(scratch),
        compiler_params=pltpu.CompilerParams(vmem_limit_bytes=24 * 1024 * 1024),
        name=name,
    )(*[array for array, _ in ins])


def per_device(
    tiles,
    row_tile,
    col_tile,
    diag_cost,
    linear_cost,
    bound_center,
    bound_width,
    rho_level,
    sigma_level,
    state_x,
    state_w,
    prev_x,
    prev_w,
    prev_gx,
    prev_gw,
    hist_sx,
    hist_sw,
    hist_gx,
    hist_gw,
    slot_order,
):
    problems, var_cols = state_x.shape
    con_cols = state_w.shape[1]
    tile_size = tiles.shape[-1]
    var_count, con_count = lax.axis_size("var"), lax.axis_size("con")
    col_count = var_cols // tile_size
    run_length = con_cols // tile_size
    blocks = tiles.reshape(-1, tile_size, tile_size)
    count = blocks.shape[0]
    per_run = -(-count // var_count)
    slots = var_count * per_run
    rows_here = row_tile.reshape(-1)
    cols_here = col_tile.reshape(-1)
    diag = diag_cost.reshape(1, -1)
    level = rho_level.reshape(1, -1)

    x_like = ((problems, var_cols), f32, "v")
    w_like = ((problems, con_cols), f32, "v")
    panel = ((slots, problems, tile_size), f32, "v")
    wide_panel = (((2 * per_run + 1) * var_count, problems // 2, tile_size), f32, "v")
    one_tile = ((problems, tile_size), f32, "v")
    left = pltpu.VMEM((col_count, 2 * problems, 2 * tile_size), bf16)
    sums = [pltpu.VMEM((run_length, problems, tile_size), f32)] * 4
    bounds = [(bound_center, "v"), (bound_width, "v")]
    vs = lambda *arrays: [(a, "v") for a in arrays]
    ss = lambda *arrays: [(a, "s") for a in arrays]

    def exchange(x):
        return lax.all_to_all(x, "var", 0, 0, tiled=True)

    def over_con(x):
        def partner(x, k):
            return lax.ppermute(x, "con", [(i, i ^ k) for i in range(con_count)])

        others = [partner(x, k) for k in range(2, con_count, 2)]
        terms = [x] + others
        while len(terms) > 1:
            terms = [a + b for a, b in zip(terms[::2], terms[1::2])]
        return terms[0], partner(terms[0], 1)

    one_core = [list(range(k, con_count * var_count, 2)) for k in range(2)]
    share = col_count // con_count
    parts = max(d for d in range(1, 4) if count % d == 0)
    far = [state_x, blocks, prev_gx, prev_gw, hist_sx, hist_sw, hist_gx, hist_gw]
    x_mine, w_mine = pltpu.VMEM((problems, share * tile_size), f32), pltpu.VMEM((problems, con_cols), f32)
    memory = hist_gx.shape[0]
    hx_mine = pltpu.VMEM((memory, problems, share * tile_size), f32)
    hw_mine = pltpu.VMEM((memory, problems, con_cols), f32)
    sent, slot, blocks = call(
        functools.partial(open_kernel, per_run, run_length, share, parts),
        "open",
        [(pltpu.with_memory_space_constraint(a, pltpu.HBM), "h") for a in [row_tile[0], col_tile[0]] + far],
        [wide_panel, ((count,), jnp.int32, "s"), (blocks.shape, f32, "v")],
        [
            pltpu.SMEM((1, count), jnp.int32),
            pltpu.SMEM((1, count), jnp.int32),
            pltpu.VMEM((problems, var_cols), f32),
            x_mine, w_mine, hx_mine, hw_mine, hx_mine, hw_mine,
            left,
            pltpu.SMEM((var_count,), jnp.int32),
            pltpu.SMEM((slots,), jnp.int32),
            pltpu.SemaphoreType.DMA((3 + parts + 6,)),
        ],
    )
    got = exchange(sent)
    x, w, px, pw, pgx, pgw = state_x, state_w, prev_x, prev_w, prev_gx, prev_gw
    qgx, qgw = pgx, pgw
    kept = []
    known = None
    for step in range(STEPS):
        first, last = step == 0, step == STEPS - 1
        if first:
            sent, start, early, rows = call(
                functools.partial(penalty_kernel, True, per_run),
                "penalty_first",
                vs(got, w, bound_center, bound_width, level),
                [panel, w_like, one_tile, ((slots,), jnp.int32, "s")],
                [pltpu.SMEM((problems, tile_size), jnp.int32), pltpu.VMEM((problems, tile_size), jnp.int32), pltpu.SemaphoreType.DMA(())]
                + sums,
            )
        else:
            sent, start = call(
                functools.partial(penalty_kernel, False, per_run),
                "penalty",
                vs(got) + ss(rows) + vs(w, bound_center, bound_width, level),
                [panel, w_like],
                sums,
            )
        back = exchange(sent)
        width = var_cols + (tile_size if first else 0)
        (sent,) = call(
            functools.partial(transpose_kernel, first),
            "transpose",
            vs(back) + ss(slot, cols_here) + vs(blocks) + (vs(early) if first else []),
            [((problems, width), f32, "v")],
            [pltpu.VMEM((col_count, problems, tile_size), f32)],
        )
        own, other = over_con(sent)
        if first:
            flipped, hist_x, hist_w = call(
                prepare_kernel,
                "prepare",
                vs(blocks, hist_sx, hist_gx, hist_sw, hist_gw, sent),
                [(blocks.shape, f32, "v"), (hist_sx.shape, f32, "v"), (hist_sw.shape, f32, "v")],
            )
        outs = call(
            functools.partial(residual_kernel, first),
            "residual",
            vs(own, other, x, linear_cost, diag) + ss(cols_here, slot) + vs(flipped),
            [panel, x_like] + ([one_tile] if first else []),
            [left],
        )
        sent, resid = outs[:2]
        if first:
            known = outs[2]
        got = exchange(sent)

        sent, image = call(
            functools.partial(scalar_kernel, share),
            "scalars",
            vs(got)
            + ss(rows)
            + vs(start, w, bound_center, bound_width, level, pw, pgw, x, px, pgx, resid, diag, hist_gx, hist_gw, qgx, qgw),
            [((2, LANES), f32, "v"), w_like],
            sums,
        )
        pair = sent + lax.ppermute(sent, "var", [(i, i ^ 1) for i in range(var_count)])
        copies = jnp.broadcast_to(pair[None], (con_count * var_count // 2, 2, LANES))
        late = lax.all_to_all(copies, ("con", "var"), 0, 0, tiled=True, axis_index_groups=one_core)
        outs = call(
            functools.partial(update_kernel, last, step),
            "update",
            vs(late, known)
            + ss(slot_order, sigma_level)
            + vs(x, px, pgx, resid, hist_x, w, pw, pgw, start, image, bound_center, bound_width, hist_w)
            + vs(*kept)
            + ([] if last else ss(cols_here, slot) + vs(flipped)),
            [x_like, w_like] + ([] if last else [x_like, w_like, x_like, w_like, one_tile, panel]),
            [] if last else [left],
        )
        if last:
            return outs[0], outs[1]
        qgx, qgw = pgx, pgw
        px, pw = x, w
        x, w, pgx, pgw, dx, dw, known, sent = outs
        kept = [dx, dw]
        got = exchange(sent)


def solution(mesh):
    in_specs = (
        P("con", "var", None, None, None),
        P("con", "var", None),
        P("con", "var", None),
        P("var"),
        P(None, "var"),
        P(None, ("con", "var")),
        P(None, ("con", "var")),
        P(("con", "var")),
        P(),
        P(None, "var"),
        P(None, ("con", "var")),
        P(None, "var"),
        P(None, ("con", "var")),
        P(None, "var"),
        P(None, ("con", "var")),
        P(None, None, "var"),
        P(None, None, ("con", "var")),
        P(None, None, "var"),
        P(None, None, ("con", "var")),
        P(),
    )
    out_specs = (P(None, "var"), P(None, ("con", "var")))
    return jax.shard_map(
        per_device, mesh=mesh, in_specs=in_specs, out_specs=out_specs, check_vma=False
    )
```

```python
import functools

import jax
import jax.numpy as jnp
from jax import lax
from jax.experimental import pallas as pl
from jax.experimental.pallas import tpu as pltpu
from jax.sharding import PartitionSpec as P

STEPS = 2
LANES = 128
UNROLL = 72

relax = 1.6
ridge = 0.01

f32 = jnp.float32
bf16 = jnp.bfloat16

U_H, V_H, U_U, U_V, U_P, V_P, V_V, S_S, R_R, C_C, U_D, V_D, SCALARS = 0, 8, 16, 17, 18, 19, 20, 21, 22, 23, 24, 25, 26


MEMORY = 8
LANE_P, LANE_S, LANE_ENTRY = 36, 44, 52


def pair_lane(m, n):
    return m * MEMORY - m * (m - 1) // 2 + n - m


def halves(value):
    high = value.astype(bf16)
    return high, (value - high.astype(f32)).astype(bf16)


def stacked(piece):
    high, low = halves(piece)
    return jnp.concatenate(
        [
            jnp.concatenate([high, high], axis=1),
            jnp.concatenate([low, jnp.zeros_like(low)], axis=1),
        ],
        axis=0,
    )


def times(left, right, contract):
    both = lax.dot_general(left, right, (((1,), (contract,)), ((), ())), preferred_element_type=f32)
    half = both.shape[0] // 2
    return both[:half] + both[half:]


def at(ref, block):
    if isinstance(block, int):
        return block_of(ref, block)
    return ref[:, pl.ds(pl.multiple_of(block * LANES, LANES), LANES)]


def tile_loop(count, body):
    step = max(d for d in range(1, UNROLL + 1) if count % d == 0)

    if step == count:
        for j in range(count):
            body(j)
        return

    def some(i, _):
        for j in range(step):
            body(i * step + j)
        return 0

    lax.fori_loop(0, count // step, some, 0)


def lane_ids(shape):
    return lax.broadcasted_iota(jnp.int32, shape, len(shape) - 1)


def send_products(x_ref, cols, where, tiles, send, left, waits=(None,), flipped=True):
    for block in range(x_ref.shape[1] // LANES):
        left[block] = stacked(x_ref[:, block * LANES : (block + 1) * LANES])
    send[...] = jnp.zeros_like(send)

    def one(t):
        axis = 0 if flipped else 1
        value = times(left[cols[t]], jnp.concatenate(halves(tiles[t]), axis=axis), axis)
        if flipped:
            send[where(t)] = value
        else:
            send[where(t)] = value[: value.shape[0] // 2]
            send[where(t) + 1] = value[value.shape[0] // 2 :]

    size = tiles.shape[0] // len(waits)
    for i, wait in enumerate(waits):
        if wait is not None:
            wait()
        tile_loop(size, lambda t, i=i: one(t + i * size))


def add_rows(received, rows, sums):
    for ref in sums:
        ref[...] = jnp.zeros_like(ref)
    for s in range(rows.shape[0]):
        ref = sums[s % len(sums)]
        row = rows[s]
        ref[row] = ref[row] + received(s)
    return lambda b: functools.reduce(lambda p, q: p + q, [ref[b] for ref in sums])


def block_of(ref, b):
    return ref[:, b * LANES : (b + 1) * LANES]


def rho_of(level_ref, b):
    return 0.4 * (1.0 + block_of(level_ref, b).astype(f32))


def slack_of(w, center, width):
    return jnp.minimum(jnp.maximum(w, center - width), center + width)


def total(value):
    return jnp.sum(value, axis=1, keepdims=True)


def open_kernel(per_run, run_length, share, parts, *refs):
    (hbm_rows, hbm_cols, hbm_x, hbm_tiles, *far), (send, slot, tiles), refs = refs[:10], refs[10:13], refs[13:]
    rows_buf, cols_buf, x, pgx, pgw, hsx, hsw, hgx, hgw, left, count, asked, spot, sem = refs
    memory = hgx.shape[0]
    problems = x.shape[0]
    half = problems // 2
    wide = 2 * per_run + 1
    runs = send.shape[0] // wide
    first = lax.axis_index("con") * share
    mine = pl.ds(pl.multiple_of(first * LANES, LANES), share * LANES)
    far_pgx, far_pgw, far_hsx, far_hsw, far_hgx, far_hgw = far
    size = tiles.shape[0] // parts
    moves = [(hbm_rows, rows_buf), (hbm_cols, cols_buf), (hbm_x, x)]
    moves += [(far_pgw, pgw), (far_hsw, hsw), (far_hgw, hgw)]
    moves += [(far_pgx.at[:, mine], pgx), (far_hsx.at[:, :, mine], hsx), (far_hgx.at[:, :, mine], hgx)]
    moves += [(hbm_tiles.at[pl.ds(i * size, size)], tiles.at[pl.ds(i * size, size)]) for i in range(parts)]
    copies = [pltpu.make_async_copy(a, b, sem.at[i]) for i, (a, b) in enumerate(moves)]
    for copy in copies:
        copy.start()
    rows, cols = rows_buf.at[0], cols_buf.at[0]

    for i in range(runs):
        count[i] = 0
    for i in range(runs * per_run):
        asked[i] = 0
    copies[0].wait()
    copies[1].wait()
    for t in range(tiles.shape[0]):
        row = rows[t]
        owner = row >> (run_length.bit_length() - 1)
        rank = count[owner]
        count[owner] = rank + 1
        place = owner * per_run + rank
        slot[t] = place
        spot[t] = owner * wide + rank * 2
        asked[place] = row & (run_length - 1)

    def where(t):
        return spot[t]

    copies[2].wait()
    places = [(False, b) for b in range(pgw.shape[1] // LANES)] + [(True, b) for b in range(share)]

    def read(ref_x, ref_w, place):
        is_x, b = place
        ref = ref_x if is_x else ref_w
        return ref[..., b * LANES : (b + 1) * LANES]

    acc = {}

    def add(lane, value):
        acc[lane] = acc[lane] + value if lane in acc else value

    def while_tiles_come():
        for copy in copies[3:9]:
            copy.wait()
        for place in places:
            g = [read(hgx.at[m], hgw.at[m], place) for m in range(memory)]
            for m in range(memory):
                for n in range(m, memory):
                    add(pair_lane(m, n), g[m] * g[n])
        for place in places:
            p = read(pgx, pgw, place)
            for m in range(memory):
                add(LANE_P + m, read(hgx.at[m], hgw.at[m], place) * p)
                h = read(hsx.at[m], hsw.at[m], place)
                add(LANE_S + m, h * h)
        lanes = lane_ids((problems, LANES))
        out = jnp.zeros((problems, LANES), f32)
        for lane, value in acc.items():
            out = jnp.where(lanes == lane, total(value), out)
        index = entry_ids(problems) - lax.axis_index("var") * per_run
        for r in range(runs):
            mark = out
            for i in range(per_run):
                mark = jnp.where(index == i, asked[r * per_run + i].astype(f32), mark)
            turned = pltpu.roll(mark, LANES // 2, 1)
            send[r * wide + 2 * per_run] = jnp.where(lanes[:half] < LANES // 2, mark[:half], turned[half:])
        copies[9].wait()

    waits = [while_tiles_come] + [copy.wait for copy in copies[10:]]
    send_products(x, cols, where, tiles, send, left, waits, flipped=False)


def entry_ids(problems):
    shape = (problems, LANES)
    return (lane_ids(shape) - LANE_ENTRY) * problems + lax.broadcasted_iota(jnp.int32, shape, 0)


def penalty_kernel(first, per_run, *refs):
    if first:
        got, w, center, width, level, send, image, early, rows, marks, marks_int, sem, *sums = refs
    else:
        got, rows, w, center, width, level, send, image, *sums = refs
    slots = send.shape[0]
    runs = slots // per_run
    if first:
        wide = 2 * per_run + 1
        folded = functools.reduce(lambda p, q: p + q, [got[r * wide + 2 * per_run] for r in range(runs)])
        early_sum = jnp.concatenate([folded, pltpu.roll(folded, LANES // 2, 1)], axis=0)
        early[...] = early_sum
        marks_int[...] = early_sum.astype(jnp.int32)
        copy = pltpu.make_async_copy(marks_int, marks, sem)
        copy.start()
        copy.wait()
        problems = w.shape[0]
        for s in range(slots):
            rows[s] = marks[s % problems, LANE_ENTRY + s // problems]

        def received(s):
            unit = s // per_run * wide + s % per_run * 2
            return jnp.concatenate([got[unit], got[unit + 1]], axis=0)

        result = add_rows(received, rows, sums)
    else:
        result = add_rows(lambda s: got[s], rows, sums)
    blocks = w.shape[1] // LANES
    for b in range(blocks):
        start = result(b)
        image[:, b * LANES : (b + 1) * LANES] = start
        here = block_of(w, b)
        slack = slack_of(here, block_of(center, b), block_of(width, b))
        rho = rho_of(level, b)
        sums[0][b] = rho * (slack - start) - rho * (here - slack)
    for s in range(slots):
        send[s] = sums[0][rows[s]]


def transpose_kernel(first, *refs):
    if first:
        back, slot, cols, tiles, early, send, acc = refs
    else:
        back, slot, cols, tiles, send, acc = refs
    acc[...] = jnp.zeros_like(acc)

    def one(t):
        high, low = halves(tiles[t])
        term = times(stacked(back[slot[t]]), jnp.concatenate([high, low], axis=0), 0)
        col = cols[t]
        acc[col] = acc[col] + term

    tile_loop(tiles.shape[0], one)
    columns = acc.shape[0]
    for b in range(columns):
        send[:, b * LANES : (b + 1) * LANES] = acc[b]
    if first:
        send[:, columns * LANES :] = early[...]


def prepare_kernel(tiles, hsx, hgx, hsw, hgw, _, flipped, hx, hw):
    tile_loop(tiles.shape[0], lambda t: flipped.__setitem__(t, tiles[t].T))
    for m in range(hx.shape[0]):
        hx[m] = hsx[m] + hgx[m]
        hw[m] = hsw[m] + hgw[m]


def residual_kernel(first, own, other, x, linear, diag, cols, slot, tiles, send, resid, *refs):
    columns = x.shape[1] // LANES
    if first:
        early, left = refs
    else:
        (left,) = refs
    for b in range(columns):
        lo, hi = b * LANES, (b + 1) * LANES
        value = -linear[:, lo:hi] - diag[:, lo:hi] * x[:, lo:hi]
        resid[:, lo:hi] = value + (own[:, lo:hi] + other[:, lo:hi])
    if first:
        early[...] = own[:, columns * LANES :] + other[:, columns * LANES :]
    send_products(resid, cols, lambda t: slot[t], tiles, send, left)


class Sums:
    def __init__(self, problems):
        self.shape = (problems, LANES)
        self.acc = {}

    def add(self, i, value):
        self.acc[i] = self.acc[i] + value if i in self.acc else value

    def tiles(self, tiles):
        turn = (LANES - 16 * lax.broadcasted_iota(jnp.int32, self.shape, 0)) & (LANES - 1)
        lanes = lane_ids(self.shape)
        tiles = list(tiles)
        for i, value in self.acc.items():
            tiles[i // 16] = jnp.where(lanes == turn + i % 16, total(value), tiles[i // 16])
        return tiles


def blocks_of(w, share):
    first = lax.axis_index("con") * share
    return [(False, b) for b in range(w.shape[1] // LANES)] + [(True, first + b) for b in range(share)]


def scalar_kernel(
    share, got, rows, start, w, center, width, level, pw, pgw, x, px, pgx, resid, diag, hgx, hgw, qgx, qgw, send, image, *scratch
):
    result = add_rows(lambda s: got[s], rows, scratch)
    sums = Sums(w.shape[0])
    for is_x, b in blocks_of(w, share):
        if is_x:
            r, p = at(resid, b), at(pgx, b)
            u, v, s, d = -p, relax * r, at(x, b) - at(px, b), p - at(qgx, b)
            sums.add(R_R, r * r)
            sums.add(C_C, at(diag, b) * r * r)
        else:
            ar, p = result(b), block_of(pgw, b)
            image[:, b * LANES : (b + 1) * LANES] = ar
            here = block_of(w, b)
            slack = slack_of(here, block_of(center, b), block_of(width, b))
            u, v, s, d = relax * (block_of(start, b) - slack) - p, relax * ar, here - block_of(pw, b), p - block_of(qgw, b)
            sums.add(C_C, rho_of(level, b) * ar * ar)
        for m in range(MEMORY):
            h = at(hgx.at[m] if is_x else hgw.at[m], b)
            sums.add(U_H + m, u * h)
            sums.add(V_H + m, v * h)
        for i, value in ((U_U, u * u), (U_V, u * v), (U_P, u * p), (V_P, v * p), (V_V, v * v), (S_S, s * s), (U_D, u * d), (V_D, v * d)):
            sums.add(i, value)
    zero = jnp.zeros(sums.shape, f32)
    rows_out = [jnp.sum(tile, axis=0, keepdims=True) for tile in sums.tiles([zero, zero])]
    send[...] = jnp.concatenate(rows_out, axis=0)


def update_kernel(last, steps_before, *refs):
    (late, known, order, sigma_level, x, px, pgx, resid, hx) = refs[:9]
    (w, pw, pgw, start, image, center, width, hw) = refs[9:17]
    refs = refs[17:]
    if steps_before:
        dx, dw = refs[:2]
        refs = refs[2:]
    if last:
        x_out, w_out = refs
    else:
        cols, slot, tiles, x_out, w_out, gx_out, gw_out, dx_out, dw_out, known_out, send, left = refs
    problems = x.shape[0]
    memory = hx.shape[0]
    shape = (problems, LANES)
    lanes = lane_ids(shape)
    program = lax.broadcasted_iota(jnp.int32, shape, 0)
    chains = [late[i] for i in range(min(8, late.shape[0]))]
    for i in range(len(chains), late.shape[0]):
        chains[i % 8] = chains[i % 8] + late[i]
    rows = functools.reduce(lambda p, q: p + q, chains)

    aligned = [
        pltpu.roll(jnp.broadcast_to(rows[i : i + 1], shape), 0, 1, stride=16, stride_axis=0) for i in range(2)
    ]

    def scalar(i):
        return jnp.broadcast_to(aligned[i // 16][:, i % 16 : i % 16 + 1], shape)

    def given(i):
        return jnp.broadcast_to(known[:, i : i + 1], shape)

    new = [jnp.where(order[steps_before] == m, 1.0, 0.0) for m in range(memory)]
    keep = [1.0 - f for f in new]
    if steps_before:
        old = [jnp.where(order[0] == m, 1.0, 0.0) for m in range(memory)]
    sigma = jnp.zeros(shape, f32)
    for k in range(problems):
        sigma = jnp.where(program == k, 0.2 * (1.0 + sigma_level[k].astype(f32)), sigma)
    norm = scalar(R_R)
    step = norm / (scalar(C_C) + sigma * norm)
    u_h = [scalar(U_H + m) for m in range(memory)]
    v_h = [scalar(V_H + m) for m in range(memory)]
    if steps_before:
        u_d, v_d = scalar(U_D), scalar(V_D)
        u_h = [h * (1.0 - f) + u_d * f for h, f in zip(u_h, old)]
        v_h = [h * (1.0 - f) + v_d * f for h, f in zip(v_h, old)]
    dot = [u + step * v for u, v in zip(u_h, v_h)]
    own = scalar(U_U) + 2.0 * step * scalar(U_V) + step * step * scalar(V_V)
    with_p = scalar(U_P) + step * scalar(V_P)
    gram = [[None] * memory for _ in range(memory)]
    for m in range(memory):
        gram[m][m] = given(pair_lane(m, m)) * keep[m] + own * new[m]
        for n in range(m + 1, memory):
            value = given(pair_lane(m, n)) * (keep[m] * keep[n]) + dot[n] * new[m] + dot[m] * new[n]
            gram[m][n] = gram[n][m] = value
    rhs = []
    for m in range(memory):
        value = given(LANE_P + m) * keep[m] + with_p * new[m]
        for n in range(memory):
            value = value + gram[m][n] * new[n]
        rhs.append(value)
    s_s = scalar(S_S)
    squares = [given(LANE_S + m) * keep[m] + s_s * new[m] for m in range(memory)]
    frob = functools.reduce(lambda p, q: p + q, squares + [gram[m][m] for m in range(memory)])
    damp = ridge * frob
    if not last:
        out = jnp.zeros(shape, f32)
        for m in range(memory):
            for n in range(m, memory):
                out = jnp.where(lanes == pair_lane(m, n), gram[m][n], out)
            out = jnp.where(lanes == LANE_P + m, rhs[m], out)
            out = jnp.where(lanes == LANE_S + m, squares[m], out)
        known_out[...] = out
    low = [[None] * memory for _ in range(memory)]
    inverse = []
    for j in range(memory):
        value = gram[j][j] + damp
        for k in range(j):
            value = value - low[j][k] * low[j][k]
        inverse.append(1.0 / jnp.sqrt(value))
        for i in range(j + 1, memory):
            value = gram[i][j]
            for k in range(j):
                value = value - low[i][k] * low[j][k]
            low[i][j] = value * inverse[j]
    half = []
    for i in range(memory):
        value = rhs[i]
        for k in range(i):
            value = value - low[i][k] * half[k]
        half.append(value * inverse[i])
    coef = [None] * memory
    for i in reversed(range(memory)):
        value = half[i]
        for k in range(i + 1, memory):
            value = value - low[k][i] * coef[k]
        coef[i] = value * inverse[i]

    newest = functools.reduce(lambda p, q: p + q, [c * f for c, f in zip(coef, new)])
    left_over = [c * f for c, f in zip(coef, keep)]
    if steps_before:
        older = functools.reduce(lambda p, q: p + q, [c * f for c, f in zip(left_over, old)])
        left_over = [c * (1.0 - f) for c, f in zip(left_over, old)]

    scaled = relax * step
    older = older if steps_before else None
    for b in range(x.shape[1] // LANES):
        g = scaled * block_of(resid, b)
        advance(b, newest, left_over, older, x, px, g, pgx, hx, dx if steps_before else None, x_out, None if last else gx_out, None if last else dx_out)
    for b in range(w.shape[1] // LANES):
        slack = slack_of(block_of(w, b), block_of(center, b), block_of(width, b))
        g = relax * (block_of(start, b) + step * block_of(image, b) - slack)
        advance(b, newest, left_over, older, w, pw, g, pgw, hw, dw if steps_before else None, w_out, None if last else gw_out, None if last else dw_out)
    if not last:
        send_products(x_out, cols, lambda t: slot[t], tiles, send, left)


def advance(b, newest, left_over, older, state, previous, g, previous_g, hist, kept, out, g_out, d_out):
    lo, hi = b * LANES, (b + 1) * LANES
    here = state[:, lo:hi]
    fresh = (here - previous[:, lo:hi]) + (g - previous_g[:, lo:hi])
    value = here + g - newest * fresh
    for m in range(len(left_over)):
        value = value - left_over[m] * hist[m, :, lo:hi]
    if kept is not None:
        value = value - older * kept[:, lo:hi]
    out[:, lo:hi] = value
    if g_out is not None:
        g_out[:, lo:hi] = g
        d_out[:, lo:hi] = fresh


def call(kernel, name, ins, outs, scratch=()):
    spaces = {"v": pltpu.VMEM, "s": pltpu.SMEM, "h": pltpu.HBM}
    return pl.pallas_call(
        kernel,
        out_shape=[jax.ShapeDtypeStruct(shape, dtype) for shape, dtype, _ in outs],
        in_specs=[pl.BlockSpec(memory_space=spaces[space]) for _, space in ins],
        out_specs=[pl.BlockSpec(memory_space=spaces[space]) for _, _, space in outs],
        scratch_shapes=list(scratch),
        compiler_params=pltpu.CompilerParams(vmem_limit_bytes=24 * 1024 * 1024),
        name=name,
    )(*[array for array, _ in ins])


def per_device(
    tiles,
    row_tile,
    col_tile,
    diag_cost,
    linear_cost,
    bound_center,
    bound_width,
    rho_level,
    sigma_level,
    state_x,
    state_w,
    prev_x,
    prev_w,
    prev_gx,
    prev_gw,
    hist_sx,
    hist_sw,
    hist_gx,
    hist_gw,
    slot_order,
):
    problems, var_cols = state_x.shape
    con_cols = state_w.shape[1]
    tile_size = tiles.shape[-1]
    var_count, con_count = lax.axis_size("var"), lax.axis_size("con")
    col_count = var_cols // tile_size
    run_length = con_cols // tile_size
    blocks = tiles.reshape(-1, tile_size, tile_size)
    count = blocks.shape[0]
    per_run = -(-count // var_count)
    slots = var_count * per_run
    rows_here = row_tile.reshape(-1)
    cols_here = col_tile.reshape(-1)
    diag = diag_cost.reshape(1, -1)
    level = rho_level.reshape(1, -1)

    x_like = ((problems, var_cols), f32, "v")
    w_like = ((problems, con_cols), f32, "v")
    panel = ((slots, problems, tile_size), f32, "v")
    wide_panel = (((2 * per_run + 1) * var_count, problems // 2, tile_size), f32, "v")
    one_tile = ((problems, tile_size), f32, "v")
    left = pltpu.VMEM((col_count, 2 * problems, 2 * tile_size), bf16)
    sums = [pltpu.VMEM((run_length, problems, tile_size), f32)] * 4
    bounds = [(bound_center, "v"), (bound_width, "v")]
    vs = lambda *arrays: [(a, "v") for a in arrays]
    ss = lambda *arrays: [(a, "s") for a in arrays]

    def exchange(x):
        return lax.all_to_all(x, "var", 0, 0, tiled=True)

    def over_con(x):
        def partner(x, k):
            return lax.ppermute(x, "con", [(i, i ^ k) for i in range(con_count)])

        others = [partner(x, k) for k in range(2, con_count, 2)]
        terms = [x] + others
        while len(terms) > 1:
            terms = [a + b for a, b in zip(terms[::2], terms[1::2])]
        return terms[0], partner(terms[0], 1)

    one_core = [list(range(k, con_count * var_count, 2)) for k in range(2)]
    share = col_count // con_count
    parts = max(d for d in range(1, 7) if count % d == 0)
    far = [state_x, blocks, prev_gx, prev_gw, hist_sx, hist_sw, hist_gx, hist_gw]
    x_mine, w_mine = pltpu.VMEM((problems, share * tile_size), f32), pltpu.VMEM((problems, con_cols), f32)
    memory = hist_gx.shape[0]
    hx_mine = pltpu.VMEM((memory, problems, share * tile_size), f32)
    hw_mine = pltpu.VMEM((memory, problems, con_cols), f32)
    sent, slot, blocks = call(
        functools.partial(open_kernel, per_run, run_length, share, parts),
        "open",
        [(pltpu.with_memory_space_constraint(a, pltpu.HBM), "h") for a in [row_tile[0], col_tile[0]] + far],
        [wide_panel, ((count,), jnp.int32, "s"), (blocks.shape, f32, "v")],
        [
            pltpu.SMEM((1, count), jnp.int32),
            pltpu.SMEM((1, count), jnp.int32),
            pltpu.VMEM((problems, var_cols), f32),
            x_mine, w_mine, hx_mine, hw_mine, hx_mine, hw_mine,
            left,
            pltpu.SMEM((var_count,), jnp.int32),
            pltpu.SMEM((slots,), jnp.int32),
            pltpu.SMEM((count,), jnp.int32),
            pltpu.SemaphoreType.DMA((3 + parts + 6,)),
        ],
    )
    got = exchange(sent)
    x, w, px, pw, pgx, pgw = state_x, state_w, prev_x, prev_w, prev_gx, prev_gw
    qgx, qgw = pgx, pgw
    kept = []
    known = None
    for step in range(STEPS):
        first, last = step == 0, step == STEPS - 1
        if first:
            sent, start, early, rows = call(
                functools.partial(penalty_kernel, True, per_run),
                "penalty_first",
                vs(got, w, bound_center, bound_width, level),
                [panel, w_like, one_tile, ((slots,), jnp.int32, "s")],
                [pltpu.SMEM((problems, tile_size), jnp.int32), pltpu.VMEM((problems, tile_size), jnp.int32), pltpu.SemaphoreType.DMA(())]
                + sums,
            )
        else:
            sent, start = call(
                functools.partial(penalty_kernel, False, per_run),
                "penalty",
                vs(got) + ss(rows) + vs(w, bound_center, bound_width, level),
                [panel, w_like],
                sums,
            )
        back = exchange(sent)
        width = var_cols + (tile_size if first else 0)
        (sent,) = call(
            functools.partial(transpose_kernel, first),
            "transpose",
            vs(back) + ss(slot, cols_here) + vs(blocks) + (vs(early) if first else []),
            [((problems, width), f32, "v")],
            [pltpu.VMEM((col_count, problems, tile_size), f32)],
        )
        own, other = over_con(sent)
        if first:
            flipped, hist_x, hist_w = call(
                prepare_kernel,
                "prepare",
                vs(blocks, hist_sx, hist_gx, hist_sw, hist_gw, sent),
                [(blocks.shape, f32, "v"), (hist_sx.shape, f32, "v"), (hist_sw.shape, f32, "v")],
            )
        outs = call(
            functools.partial(residual_kernel, first),
            "residual",
            vs(own, other, x, linear_cost, diag) + ss(cols_here, slot) + vs(flipped),
            [panel, x_like] + ([one_tile] if first else []),
            [left],
        )
        sent, resid = outs[:2]
        if first:
            known = outs[2]
        got = exchange(sent)

        sent, image = call(
            functools.partial(scalar_kernel, share),
            "scalars",
            vs(got)
            + ss(rows)
            + vs(start, w, bound_center, bound_width, level, pw, pgw, x, px, pgx, resid, diag, hist_gx, hist_gw, qgx, qgw),
            [((2, LANES), f32, "v"), w_like],
            sums,
        )
        pair = sent + lax.ppermute(sent, "var", [(i, i ^ 1) for i in range(var_count)])
        copies = jnp.broadcast_to(pair[None], (con_count * var_count // 2, 2, LANES))
        late = lax.all_to_all(copies, ("con", "var"), 0, 0, tiled=True, axis_index_groups=one_core)
        outs = call(
            functools.partial(update_kernel, last, step),
            "update",
            vs(late, known)
            + ss(slot_order, sigma_level)
            + vs(x, px, pgx, resid, hist_x, w, pw, pgw, start, image, bound_center, bound_width, hist_w)
            + vs(*kept)
            + ([] if last else ss(cols_here, slot) + vs(flipped)),
            [x_like, w_like] + ([] if last else [x_like, w_like, x_like, w_like, one_tile, panel]),
            [] if last else [left],
        )
        if last:
            return outs[0], outs[1]
        qgx, qgw = pgx, pgw
        px, pw = x, w
        x, w, pgx, pgw, dx, dw, known, sent = outs
        kept = [dx, dw]
        got = exchange(sent)


def solution(mesh):
    in_specs = (
        P("con", "var", None, None, None),
        P("con", "var", None),
        P("con", "var", None),
        P("var"),
        P(None, "var"),
        P(None, ("con", "var")),
        P(None, ("con", "var")),
        P(("con", "var")),
        P(),
        P(None, "var"),
        P(None, ("con", "var")),
        P(None, "var"),
        P(None, ("con", "var")),
        P(None, "var"),
        P(None, ("con", "var")),
        P(None, None, "var"),
        P(None, None, ("con", "var")),
        P(None, None, "var"),
        P(None, None, ("con", "var")),
        P(),
    )
    out_specs = (P(None, "var"), P(None, ("con", "var")))
    return jax.shard_map(
        per_device, mesh=mesh, in_specs=in_specs, out_specs=out_specs, check_vma=False
    )
```

```python
import functools

import jax
import jax.numpy as jnp
from jax import lax
from jax.experimental import pallas as pl
from jax.experimental.pallas import tpu as pltpu
from jax.sharding import PartitionSpec as P

STEPS = 2
LANES = 128
UNROLL = 72

relax = 1.6
ridge = 0.01

f32 = jnp.float32
bf16 = jnp.bfloat16

U_H, V_H, U_U, U_V, U_P, V_P, V_V, S_S, R_R, C_C, U_D, V_D, SCALARS = 0, 8, 16, 17, 18, 19, 20, 21, 22, 23, 24, 25, 26


MEMORY = 8
LANE_P, LANE_S, LANE_ENTRY = 36, 44, 52


def pair_lane(m, n):
    return m * MEMORY - m * (m - 1) // 2 + n - m


def halves(value):
    high = value.astype(bf16)
    return high, (value - high.astype(f32)).astype(bf16)


def stacked(piece):
    high, low = halves(piece)
    return jnp.concatenate(
        [
            jnp.concatenate([high, high], axis=1),
            jnp.concatenate([low, jnp.zeros_like(low)], axis=1),
        ],
        axis=0,
    )


def times(left, right, contract):
    both = lax.dot_general(left, right, (((1,), (contract,)), ((), ())), preferred_element_type=f32)
    half = both.shape[0] // 2
    return both[:half] + both[half:]


def at(ref, block):
    if isinstance(block, int):
        return block_of(ref, block)
    return ref[:, pl.ds(pl.multiple_of(block * LANES, LANES), LANES)]


def tile_loop(count, body):
    step = max(d for d in range(1, UNROLL + 1) if count % d == 0)

    if step == count:
        for j in range(count):
            body(j)
        return

    def some(i, _):
        for j in range(step):
            body(i * step + j)
        return 0

    lax.fori_loop(0, count // step, some, 0)


def lane_ids(shape):
    return lax.broadcasted_iota(jnp.int32, shape, len(shape) - 1)


def send_products(x_ref, cols, where, tiles, send, left, waits=(None,), flipped=True):
    for block in range(x_ref.shape[1] // LANES):
        left[block] = stacked(x_ref[:, block * LANES : (block + 1) * LANES])
    send[...] = jnp.zeros_like(send)

    def one(t):
        axis = 0 if flipped else 1
        value = times(left[cols[t]], jnp.concatenate(halves(tiles[t]), axis=axis), axis)
        if flipped:
            send[where(t)] = value
        else:
            send[where(t)] = value[: value.shape[0] // 2]
            send[where(t) + 1] = value[value.shape[0] // 2 :]

    size = tiles.shape[0] // len(waits)
    for i, wait in enumerate(waits):
        if wait is not None:
            wait()
        tile_loop(size, lambda t, i=i: one(t + i * size))


def add_rows(received, rows, sums):
    for ref in sums:
        ref[...] = jnp.zeros_like(ref)
    for s in range(rows.shape[0]):
        ref = sums[s % len(sums)]
        row = rows[s]
        ref[row] = ref[row] + received(s)
    return lambda b: functools.reduce(lambda p, q: p + q, [ref[b] for ref in sums])


def block_of(ref, b):
    return ref[:, b * LANES : (b + 1) * LANES]


def rho_of(level_ref, b):
    return 0.4 * (1.0 + block_of(level_ref, b).astype(f32))


def slack_of(w, center, width):
    return jnp.minimum(jnp.maximum(w, center - width), center + width)


def total(value):
    return jnp.sum(value, axis=1, keepdims=True)


def open_kernel(per_run, run_length, share, parts, *refs):
    (hbm_rows, hbm_cols, hbm_x, hbm_tiles, *far), (send, slot, tiles), refs = refs[:10], refs[10:13], refs[13:]
    rows_buf, cols_buf, x, pgx, pgw, hsx, hsw, hgx, hgw, left, count, asked, spot, sem = refs
    memory = hgx.shape[0]
    problems = x.shape[0]
    half = problems // 2
    wide = 2 * per_run + 1
    runs = send.shape[0] // wide
    first = lax.axis_index("con") * share
    mine = pl.ds(pl.multiple_of(first * LANES, LANES), share * LANES)
    far_pgx, far_pgw, far_hsx, far_hsw, far_hgx, far_hgw = far
    size = tiles.shape[0] // parts
    moves = [(hbm_rows, rows_buf), (hbm_cols, cols_buf), (hbm_x, x)]
    moves += [(hbm_tiles.at[pl.ds(i * size, size)], tiles.at[pl.ds(i * size, size)]) for i in range(parts)]
    moves += [(far_pgw, pgw), (far_hsw, hsw), (far_hgw, hgw)]
    moves += [(far_pgx.at[:, mine], pgx), (far_hsx.at[:, :, mine], hsx), (far_hgx.at[:, :, mine], hgx)]
    copies = [pltpu.make_async_copy(a, b, sem.at[i]) for i, (a, b) in enumerate(moves)]
    for copy in copies:
        copy.start()
    rows, cols = rows_buf.at[0], cols_buf.at[0]

    for i in range(runs):
        count[i] = 0
    for i in range(runs * per_run):
        asked[i] = 0
    copies[0].wait()
    copies[1].wait()
    for t in range(tiles.shape[0]):
        row = rows[t]
        owner = row >> (run_length.bit_length() - 1)
        rank = count[owner]
        count[owner] = rank + 1
        place = owner * per_run + rank
        slot[t] = place
        spot[t] = owner * wide + rank * 2
        asked[place] = row & (run_length - 1)

    def where(t):
        return spot[t]

    copies[2].wait()
    places = [(False, b) for b in range(pgw.shape[1] // LANES)] + [(True, b) for b in range(share)]

    def read(ref_x, ref_w, place):
        is_x, b = place
        ref = ref_x if is_x else ref_w
        return ref[..., b * LANES : (b + 1) * LANES]

    acc = {}

    def add(lane, value):
        acc[lane] = acc[lane] + value if lane in acc else value

    def early_sums():
        for copy in copies[2 + parts :]:
            copy.wait()
        for place in places:
            g = [read(hgx.at[m], hgw.at[m], place) for m in range(memory)]
            for m in range(memory):
                for n in range(m, memory):
                    add(pair_lane(m, n), g[m] * g[n])
        for place in places:
            p = read(pgx, pgw, place)
            for m in range(memory):
                add(LANE_P + m, read(hgx.at[m], hgw.at[m], place) * p)
                h = read(hsx.at[m], hsw.at[m], place)
                add(LANE_S + m, h * h)

    send_products(x, cols, where, tiles, send, left, [copy.wait for copy in copies[3 : 2 + parts]] + [early_sums], flipped=False)

    lanes = lane_ids((problems, LANES))
    out = jnp.zeros((problems, LANES), f32)
    for lane, value in acc.items():
        out = jnp.where(lanes == lane, total(value), out)
    index = entry_ids(problems) - lax.axis_index("var") * per_run
    for r in range(runs):
        mark = out
        for i in range(per_run):
            mark = jnp.where(index == i, asked[r * per_run + i].astype(f32), mark)
        turned = pltpu.roll(mark, LANES // 2, 1)
        send[r * wide + 2 * per_run] = jnp.where(lanes[:half] < LANES // 2, mark[:half], turned[half:])


def entry_ids(problems):
    shape = (problems, LANES)
    return (lane_ids(shape) - LANE_ENTRY) * problems + lax.broadcasted_iota(jnp.int32, shape, 0)


def penalty_kernel(first, per_run, *refs):
    if first:
        got, w, center, width, level, send, image, early, rows, marks, marks_int, sem, *sums = refs
    else:
        got, rows, w, center, width, level, send, image, *sums = refs
    slots = send.shape[0]
    runs = slots // per_run
    if first:
        wide = 2 * per_run + 1
        folded = functools.reduce(lambda p, q: p + q, [got[r * wide + 2 * per_run] for r in range(runs)])
        early_sum = jnp.concatenate([folded, pltpu.roll(folded, LANES // 2, 1)], axis=0)
        early[...] = early_sum
        marks_int[...] = early_sum.astype(jnp.int32)
        copy = pltpu.make_async_copy(marks_int, marks, sem)
        copy.start()
        copy.wait()
        problems = w.shape[0]
        for s in range(slots):
            rows[s] = marks[s % problems, LANE_ENTRY + s // problems]

        def received(s):
            unit = s // per_run * wide + s % per_run * 2
            return jnp.concatenate([got[unit], got[unit + 1]], axis=0)

        result = add_rows(received, rows, sums)
    else:
        result = add_rows(lambda s: got[s], rows, sums)
    blocks = w.shape[1] // LANES
    for b in range(blocks):
        start = result(b)
        image[:, b * LANES : (b + 1) * LANES] = start
        here = block_of(w, b)
        slack = slack_of(here, block_of(center, b), block_of(width, b))
        rho = rho_of(level, b)
        sums[0][b] = rho * (slack - start) - rho * (here - slack)
    for s in range(slots):
        send[s] = sums[0][rows[s]]


def transpose_kernel(first, *refs):
    if first:
        back, slot, cols, tiles, early, send, acc = refs
    else:
        back, slot, cols, tiles, send, acc = refs
    acc[...] = jnp.zeros_like(acc)

    def one(t):
        high, low = halves(tiles[t])
        term = times(stacked(back[slot[t]]), jnp.concatenate([high, low], axis=0), 0)
        col = cols[t]
        acc[col] = acc[col] + term

    tile_loop(tiles.shape[0], one)
    columns = acc.shape[0]
    for b in range(columns):
        send[:, b * LANES : (b + 1) * LANES] = acc[b]
    if first:
        send[:, columns * LANES :] = early[...]


def prepare_kernel(tiles, hsx, hgx, hsw, hgw, _, flipped, hx, hw):
    tile_loop(tiles.shape[0], lambda t: flipped.__setitem__(t, tiles[t].T))
    for m in range(hx.shape[0]):
        hx[m] = hsx[m] + hgx[m]
        hw[m] = hsw[m] + hgw[m]


def residual_kernel(first, own, other, x, linear, diag, cols, slot, tiles, send, resid, *refs):
    columns = x.shape[1] // LANES
    if first:
        early, left = refs
    else:
        (left,) = refs
    for b in range(columns):
        lo, hi = b * LANES, (b + 1) * LANES
        value = -linear[:, lo:hi] - diag[:, lo:hi] * x[:, lo:hi]
        resid[:, lo:hi] = value + (own[:, lo:hi] + other[:, lo:hi])
    if first:
        early[...] = own[:, columns * LANES :] + other[:, columns * LANES :]
    send_products(resid, cols, lambda t: slot[t], tiles, send, left)


class Sums:
    def __init__(self, problems):
        self.shape = (problems, LANES)
        self.acc = {}

    def add(self, i, value):
        self.acc[i] = self.acc[i] + value if i in self.acc else value

    def tiles(self, tiles):
        turn = (LANES - 16 * lax.broadcasted_iota(jnp.int32, self.shape, 0)) & (LANES - 1)
        lanes = lane_ids(self.shape)
        tiles = list(tiles)
        for i, value in self.acc.items():
            tiles[i // 16] = jnp.where(lanes == turn + i % 16, total(value), tiles[i // 16])
        return tiles


def blocks_of(w, share):
    first = lax.axis_index("con") * share
    return [(False, b) for b in range(w.shape[1] // LANES)] + [(True, first + b) for b in range(share)]


def scalar_kernel(
    share, got, rows, start, w, center, width, level, pw, pgw, x, px, pgx, resid, diag, hgx, hgw, qgx, qgw, send, image, *scratch
):
    result = add_rows(lambda s: got[s], rows, scratch)
    sums = Sums(w.shape[0])
    for is_x, b in blocks_of(w, share):
        if is_x:
            r, p = at(resid, b), at(pgx, b)
            u, v, s, d = -p, relax * r, at(x, b) - at(px, b), p - at(qgx, b)
            sums.add(R_R, r * r)
            sums.add(C_C, at(diag, b) * r * r)
        else:
            ar, p = result(b), block_of(pgw, b)
            image[:, b * LANES : (b + 1) * LANES] = ar
            here = block_of(w, b)
            slack = slack_of(here, block_of(center, b), block_of(width, b))
            u, v, s, d = relax * (block_of(start, b) - slack) - p, relax * ar, here - block_of(pw, b), p - block_of(qgw, b)
            sums.add(C_C, rho_of(level, b) * ar * ar)
        for m in range(MEMORY):
            h = at(hgx.at[m] if is_x else hgw.at[m], b)
            sums.add(U_H + m, u * h)
            sums.add(V_H + m, v * h)
        for i, value in ((U_U, u * u), (U_V, u * v), (U_P, u * p), (V_P, v * p), (V_V, v * v), (S_S, s * s), (U_D, u * d), (V_D, v * d)):
            sums.add(i, value)
    zero = jnp.zeros(sums.shape, f32)
    rows_out = [jnp.sum(tile, axis=0, keepdims=True) for tile in sums.tiles([zero, zero])]
    send[...] = jnp.concatenate(rows_out, axis=0)


def update_kernel(last, steps_before, *refs):
    (late, known, order, sigma_level, x, px, pgx, resid, hx) = refs[:9]
    (w, pw, pgw, start, image, center, width, hw) = refs[9:17]
    refs = refs[17:]
    if steps_before:
        dx, dw = refs[:2]
        refs = refs[2:]
    if last:
        x_out, w_out = refs
    else:
        cols, slot, tiles, x_out, w_out, gx_out, gw_out, dx_out, dw_out, known_out, send, left = refs
    problems = x.shape[0]
    memory = hx.shape[0]
    shape = (problems, LANES)
    lanes = lane_ids(shape)
    program = lax.broadcasted_iota(jnp.int32, shape, 0)
    chains = [late[i] for i in range(min(8, late.shape[0]))]
    for i in range(len(chains), late.shape[0]):
        chains[i % 8] = chains[i % 8] + late[i]
    rows = functools.reduce(lambda p, q: p + q, chains)

    aligned = [
        pltpu.roll(jnp.broadcast_to(rows[i : i + 1], shape), 0, 1, stride=16, stride_axis=0) for i in range(2)
    ]

    def scalar(i):
        return jnp.broadcast_to(aligned[i // 16][:, i % 16 : i % 16 + 1], shape)

    def given(i):
        return jnp.broadcast_to(known[:, i : i + 1], shape)

    new = [jnp.where(order[steps_before] == m, 1.0, 0.0) for m in range(memory)]
    keep = [1.0 - f for f in new]
    if steps_before:
        old = [jnp.where(order[0] == m, 1.0, 0.0) for m in range(memory)]
    sigma = jnp.zeros(shape, f32)
    for k in range(problems):
        sigma = jnp.where(program == k, 0.2 * (1.0 + sigma_level[k].astype(f32)), sigma)
    norm = scalar(R_R)
    step = norm / (scalar(C_C) + sigma * norm)
    u_h = [scalar(U_H + m) for m in range(memory)]
    v_h = [scalar(V_H + m) for m in range(memory)]
    if steps_before:
        u_d, v_d = scalar(U_D), scalar(V_D)
        u_h = [h * (1.0 - f) + u_d * f for h, f in zip(u_h, old)]
        v_h = [h * (1.0 - f) + v_d * f for h, f in zip(v_h, old)]
    dot = [u + step * v for u, v in zip(u_h, v_h)]
    own = scalar(U_U) + 2.0 * step * scalar(U_V) + step * step * scalar(V_V)
    with_p = scalar(U_P) + step * scalar(V_P)
    gram = [[None] * memory for _ in range(memory)]
    for m in range(memory):
        gram[m][m] = given(pair_lane(m, m)) * keep[m] + own * new[m]
        for n in range(m + 1, memory):
            value = given(pair_lane(m, n)) * (keep[m] * keep[n]) + dot[n] * new[m] + dot[m] * new[n]
            gram[m][n] = gram[n][m] = value
    rhs = []
    for m in range(memory):
        value = given(LANE_P + m) * keep[m] + with_p * new[m]
        for n in range(memory):
            value = value + gram[m][n] * new[n]
        rhs.append(value)
    s_s = scalar(S_S)
    squares = [given(LANE_S + m) * keep[m] + s_s * new[m] for m in range(memory)]
    frob = functools.reduce(lambda p, q: p + q, squares + [gram[m][m] for m in range(memory)])
    damp = ridge * frob
    if not last:
        out = jnp.zeros(shape, f32)
        for m in range(memory):
            for n in range(m, memory):
                out = jnp.where(lanes == pair_lane(m, n), gram[m][n], out)
            out = jnp.where(lanes == LANE_P + m, rhs[m], out)
            out = jnp.where(lanes == LANE_S + m, squares[m], out)
        known_out[...] = out
    low = [[None] * memory for _ in range(memory)]
    inverse = []
    for j in range(memory):
        value = gram[j][j] + damp
        for k in range(j):
            value = value - low[j][k] * low[j][k]
        inverse.append(1.0 / jnp.sqrt(value))
        for i in range(j + 1, memory):
            value = gram[i][j]
            for k in range(j):
                value = value - low[i][k] * low[j][k]
            low[i][j] = value * inverse[j]
    half = []
    for i in range(memory):
        value = rhs[i]
        for k in range(i):
            value = value - low[i][k] * half[k]
        half.append(value * inverse[i])
    coef = [None] * memory
    for i in reversed(range(memory)):
        value = half[i]
        for k in range(i + 1, memory):
            value = value - low[k][i] * coef[k]
        coef[i] = value * inverse[i]

    newest = functools.reduce(lambda p, q: p + q, [c * f for c, f in zip(coef, new)])
    left_over = [c * f for c, f in zip(coef, keep)]
    if steps_before:
        older = functools.reduce(lambda p, q: p + q, [c * f for c, f in zip(left_over, old)])
        left_over = [c * (1.0 - f) for c, f in zip(left_over, old)]

    scaled = relax * step
    older = older if steps_before else None
    for b in range(x.shape[1] // LANES):
        g = scaled * block_of(resid, b)
        advance(b, newest, left_over, older, x, px, g, pgx, hx, dx if steps_before else None, x_out, None if last else gx_out, None if last else dx_out)
    for b in range(w.shape[1] // LANES):
        slack = slack_of(block_of(w, b), block_of(center, b), block_of(width, b))
        g = relax * (block_of(start, b) + step * block_of(image, b) - slack)
        advance(b, newest, left_over, older, w, pw, g, pgw, hw, dw if steps_before else None, w_out, None if last else gw_out, None if last else dw_out)
    if not last:
        send_products(x_out, cols, lambda t: slot[t], tiles, send, left)


def advance(b, newest, left_over, older, state, previous, g, previous_g, hist, kept, out, g_out, d_out):
    lo, hi = b * LANES, (b + 1) * LANES
    here = state[:, lo:hi]
    fresh = (here - previous[:, lo:hi]) + (g - previous_g[:, lo:hi])
    value = here + g - newest * fresh
    for m in range(len(left_over)):
        value = value - left_over[m] * hist[m, :, lo:hi]
    if kept is not None:
        value = value - older * kept[:, lo:hi]
    out[:, lo:hi] = value
    if g_out is not None:
        g_out[:, lo:hi] = g
        d_out[:, lo:hi] = fresh


def call(kernel, name, ins, outs, scratch=()):
    spaces = {"v": pltpu.VMEM, "s": pltpu.SMEM, "h": pltpu.HBM}
    return pl.pallas_call(
        kernel,
        out_shape=[jax.ShapeDtypeStruct(shape, dtype) for shape, dtype, _ in outs],
        in_specs=[pl.BlockSpec(memory_space=spaces[space]) for _, space in ins],
        out_specs=[pl.BlockSpec(memory_space=spaces[space]) for _, _, space in outs],
        scratch_shapes=list(scratch),
        compiler_params=pltpu.CompilerParams(vmem_limit_bytes=24 * 1024 * 1024),
        name=name,
    )(*[array for array, _ in ins])


def per_device(
    tiles,
    row_tile,
    col_tile,
    diag_cost,
    linear_cost,
    bound_center,
    bound_width,
    rho_level,
    sigma_level,
    state_x,
    state_w,
    prev_x,
    prev_w,
    prev_gx,
    prev_gw,
    hist_sx,
    hist_sw,
    hist_gx,
    hist_gw,
    slot_order,
):
    problems, var_cols = state_x.shape
    con_cols = state_w.shape[1]
    tile_size = tiles.shape[-1]
    var_count, con_count = lax.axis_size("var"), lax.axis_size("con")
    col_count = var_cols // tile_size
    run_length = con_cols // tile_size
    blocks = tiles.reshape(-1, tile_size, tile_size)
    count = blocks.shape[0]
    per_run = -(-count // var_count)
    slots = var_count * per_run
    rows_here = row_tile.reshape(-1)
    cols_here = col_tile.reshape(-1)
    diag = diag_cost.reshape(1, -1)
    level = rho_level.reshape(1, -1)

    x_like = ((problems, var_cols), f32, "v")
    w_like = ((problems, con_cols), f32, "v")
    panel = ((slots, problems, tile_size), f32, "v")
    wide_panel = (((2 * per_run + 1) * var_count, problems // 2, tile_size), f32, "v")
    one_tile = ((problems, tile_size), f32, "v")
    left = pltpu.VMEM((col_count, 2 * problems, 2 * tile_size), bf16)
    sums = [pltpu.VMEM((run_length, problems, tile_size), f32)] * 4
    bounds = [(bound_center, "v"), (bound_width, "v")]
    vs = lambda *arrays: [(a, "v") for a in arrays]
    ss = lambda *arrays: [(a, "s") for a in arrays]

    def exchange(x):
        return lax.all_to_all(x, "var", 0, 0, tiled=True)

    def over_con(x):
        def partner(x, k):
            return lax.ppermute(x, "con", [(i, i ^ k) for i in range(con_count)])

        pair = x + partner(x, 1)
        terms = [pair] + [partner(pair, k) for k in range(2, con_count, 2)]
        while len(terms) > 2:
            terms = [a + b for a, b in zip(terms[::2], terms[1::2])]
        return terms

    one_core = [list(range(k, con_count * var_count, 2)) for k in range(2)]
    share = col_count // con_count
    parts = max(d for d in range(1, 4) if count % d == 0)
    far = [state_x, blocks, prev_gx, prev_gw, hist_sx, hist_sw, hist_gx, hist_gw]
    x_mine, w_mine = pltpu.VMEM((problems, share * tile_size), f32), pltpu.VMEM((problems, con_cols), f32)
    memory = hist_gx.shape[0]
    hx_mine = pltpu.VMEM((memory, problems, share * tile_size), f32)
    hw_mine = pltpu.VMEM((memory, problems, con_cols), f32)
    sent, slot, blocks = call(
        functools.partial(open_kernel, per_run, run_length, share, parts),
        "open",
        [(pltpu.with_memory_space_constraint(a, pltpu.HBM), "h") for a in [row_tile[0], col_tile[0]] + far],
        [wide_panel, ((count,), jnp.int32, "s"), (blocks.shape, f32, "v")],
        [
            pltpu.SMEM((1, count), jnp.int32),
            pltpu.SMEM((1, count), jnp.int32),
            pltpu.VMEM((problems, var_cols), f32),
            x_mine, w_mine, hx_mine, hw_mine, hx_mine, hw_mine,
            left,
            pltpu.SMEM((var_count,), jnp.int32),
            pltpu.SMEM((slots,), jnp.int32),
            pltpu.SMEM((count,), jnp.int32),
            pltpu.SemaphoreType.DMA((3 + parts + 6,)),
        ],
    )
    got = exchange(sent)
    x, w, px, pw, pgx, pgw = state_x, state_w, prev_x, prev_w, prev_gx, prev_gw
    qgx, qgw = pgx, pgw
    kept = []
    known = None
    for step in range(STEPS):
        first, last = step == 0, step == STEPS - 1
        if first:
            sent, start, early, rows = call(
                functools.partial(penalty_kernel, True, per_run),
                "penalty_first",
                vs(got, w, bound_center, bound_width, level),
                [panel, w_like, one_tile, ((slots,), jnp.int32, "s")],
                [pltpu.SMEM((problems, tile_size), jnp.int32), pltpu.VMEM((problems, tile_size), jnp.int32), pltpu.SemaphoreType.DMA(())]
                + sums,
            )
        else:
            sent, start = call(
                functools.partial(penalty_kernel, False, per_run),
                "penalty",
                vs(got) + ss(rows) + vs(w, bound_center, bound_width, level),
                [panel, w_like],
                sums,
            )
        back = exchange(sent)
        width = var_cols + (tile_size if first else 0)
        (sent,) = call(
            functools.partial(transpose_kernel, first),
            "transpose",
            vs(back) + ss(slot, cols_here) + vs(blocks) + (vs(early) if first else []),
            [((problems, width), f32, "v")],
            [pltpu.VMEM((col_count, problems, tile_size), f32)],
        )
        own, other = over_con(sent)
        if first:
            flipped, hist_x, hist_w = call(
                prepare_kernel,
                "prepare",
                vs(blocks, hist_sx, hist_gx, hist_sw, hist_gw, sent),
                [(blocks.shape, f32, "v"), (hist_sx.shape, f32, "v"), (hist_sw.shape, f32, "v")],
            )
        outs = call(
            functools.partial(residual_kernel, first),
            "residual",
            vs(own, other, x, linear_cost, diag) + ss(cols_here, slot) + vs(flipped),
            [panel, x_like] + ([one_tile] if first else []),
            [left],
        )
        sent, resid = outs[:2]
        if first:
            known = outs[2]
        got = exchange(sent)

        sent, image = call(
            functools.partial(scalar_kernel, share),
            "scalars",
            vs(got)
            + ss(rows)
            + vs(start, w, bound_center, bound_width, level, pw, pgw, x, px, pgx, resid, diag, hist_gx, hist_gw, qgx, qgw),
            [((2, LANES), f32, "v"), w_like],
            sums,
        )
        pair = sent + lax.ppermute(sent, "var", [(i, i ^ 1) for i in range(var_count)])
        copies = jnp.broadcast_to(pair[None], (con_count * var_count // 2, 2, LANES))
        late = lax.all_to_all(copies, ("con", "var"), 0, 0, tiled=True, axis_index_groups=one_core)
        outs = call(
            functools.partial(update_kernel, last, step),
            "update",
            vs(late, known)
            + ss(slot_order, sigma_level)
            + vs(x, px, pgx, resid, hist_x, w, pw, pgw, start, image, bound_center, bound_width, hist_w)
            + vs(*kept)
            + ([] if last else ss(cols_here, slot) + vs(flipped)),
            [x_like, w_like] + ([] if last else [x_like, w_like, x_like, w_like, one_tile, panel]),
            [] if last else [left],
        )
        if last:
            return outs[0], outs[1]
        qgx, qgw = pgx, pgw
        px, pw = x, w
        x, w, pgx, pgw, dx, dw, known, sent = outs
        kept = [dx, dw]
        got = exchange(sent)


def solution(mesh):
    in_specs = (
        P("con", "var", None, None, None),
        P("con", "var", None),
        P("con", "var", None),
        P("var"),
        P(None, "var"),
        P(None, ("con", "var")),
        P(None, ("con", "var")),
        P(("con", "var")),
        P(),
        P(None, "var"),
        P(None, ("con", "var")),
        P(None, "var"),
        P(None, ("con", "var")),
        P(None, "var"),
        P(None, ("con", "var")),
        P(None, None, "var"),
        P(None, None, ("con", "var")),
        P(None, None, "var"),
        P(None, None, ("con", "var")),
        P(),
    )
    out_specs = (P(None, "var"), P(None, ("con", "var")))
    return jax.shard_map(
        per_device, mesh=mesh, in_specs=in_specs, out_specs=out_specs, check_vma=False
    )
```
